32 devices in a mesh: gx: 8 (over z, y), yz: 4 (over x, core).
Axes of the slice: x: 2, y: 2, z: 4, core: 2. Of those that a mesh axis runs over, the one named last changes fastest.
Arguments:
- right_side: float32 [32, 128, 512], P('gx', 'yz'), may hold values from -5 to 5
- phase: int32 [32, 128, 512], P('gx', 'yz'), may hold values 0 or 1
- pressure_guess: float32 [32, 128, 512], P('gx', 'yz'), may hold values from -6 to 6
Outputs:
- pressure: float32 [32, 128, 512], P('gx', 'yz')
- residual: float32 [32, 128, 512], P('gx', 'yz')
The draws below stay inside these ranges and needn't reach their ends.
All inputs are finite; a program needn't handle non-finite values. No bound on the sum of `phase` on one device may be relied on, other than what follows from the above.
Results may differ from the reference program's by a relative error of at most 0.0003.
Values sent between devices are 32-bit elements; how exact they have to be, the bound alone decides.
No kernel may reach another device: no remote copies, remote signals or barrier semaphores. Data moves between devices by JAX's collectives and lax.ppermute only.
A program may use at most 128 MiB of HBM per device.

```python
import jax
import jax.numpy as jnp
from jax import lax

NZ = 512
SWEEPS = 2
BOTTOM_SWEEPS = 4
NX = 32
NY = 128


def draw_right_side(key, part):
    extent = (NX, NY, NZ)
    return jnp.clip(jax.random.normal(key, extent, jnp.float32), -5.0, 5.0)


def place_ends(entries, own_key, low, high):
    longest = entries.shape.index(max(entries.shape))
    spots = []
    for shift in (0, 1):
        where = [jax.random.randint(jax.random.fold_in(own_key, axis), (), 0, length) for axis, length in enumerate(entries.shape)]
        where[longest] = (where[longest] + shift) % entries.shape[longest]
        spots.append(tuple(where))
    return entries.at[spots[0]].set(low).at[spots[1]].set(high)


def steps_of(stream_key, dims, shards, low, largest):
    def one(position, blocks):
        draws = jax.random.uniform(jax.random.fold_in(jax.random.fold_in(stream_key, 6), position), (blocks,), jnp.float32, low / len(shards), largest / len(shards))
        return jnp.repeat(jnp.exp(draws), dims[position] // blocks).reshape((-1,) + (1,) * (len(dims) - position - 1))

    gain = one(*shards[0])
    for cut in shards[1:]:
        gain = gain * one(*cut)
    return gain


def gaussian(key, dims, deviation, reach, cuts=(), held_as=jnp.bfloat16):
    gain = steps_of(key, dims, cuts, -0.22, 0.18) if cuts else 1.0
    array = jax.random.normal(key, dims, jnp.float32) * deviation * gain
    return jnp.minimum(jnp.maximum(array, -reach), reach).astype(held_as)


def setup_inputs(seed: int = 0) -> dict:
    seeds = jax.random.split(jax.random.key(seed), 4)
    return {
        "right_side": draw_right_side(jax.random.fold_in(seeds[3], 71), 0),
        "phase": place_ends((jax.random.randint(seeds[1], (NX, NY, NZ), 0, 4) < 1).astype(jnp.int32), jax.random.fold_in(seeds[1], 1), 0, 1),
        "pressure_guess": gaussian(seeds[2], (NX, NY, NZ), 1.0, 6.0, ((0, 8), (1, 4)), jnp.float32),
    }


def harmonic(left, right):
    total = left + right
    safe = jnp.where(total > 0, total, 1.0)
    return jnp.where(total > 0, 2.0 * left * right / safe, 0.0)


def coefficients(padded):
    faces_x = harmonic(padded[1:], padded[:-1])
    faces_y = harmonic(padded[:, 1:], padded[:, :-1])
    centre = padded[1:-1, 1:-1]
    faces_z = harmonic(centre[:, :, 1:], centre[:, :, :-1])
    zero_plane = jnp.zeros_like(centre[:, :, :1])
    x_lower = faces_x[:-1, 1:-1]
    x_upper = faces_x[1:, 1:-1]
    y_lower = faces_y[1:-1, :-1]
    y_upper = faces_y[1:-1, 1:]
    z_lower = jnp.concatenate([zero_plane, faces_z], axis=2)
    z_upper = jnp.concatenate([faces_z, 2.0 * centre[:, :, -1:]], axis=2)
    diagonal = x_lower + x_upper + y_lower + y_upper + z_lower + z_upper
    diagonal = jnp.where(diagonal > 0, diagonal, 1.0)
    return (x_lower, x_upper, y_lower, y_upper, z_lower, z_upper, diagonal)


def parity_of(extent, start_x, start_y):
    index_x = lax.broadcasted_iota(jnp.int32, extent, 0) + start_x
    index_y = lax.broadcasted_iota(jnp.int32, extent, 1) + start_y
    index_z = lax.broadcasted_iota(jnp.int32, extent, 2)
    return (index_x + index_y + index_z) % 2


def neighbours(padded, coeffs):
    centre = padded[1:-1, 1:-1]
    zero_plane = jnp.zeros_like(centre[:, :, :1])
    lower_z = jnp.concatenate([zero_plane, centre[:, :, :-1]], axis=2)
    upper_z = jnp.concatenate([centre[:, :, 1:], zero_plane], axis=2)
    beside_all = coeffs[0] * padded[:-2, 1:-1] + coeffs[1] * padded[2:, 1:-1]
    beside_all = beside_all + coeffs[2] * padded[1:-1, :-2] + coeffs[3] * padded[1:-1, 2:]
    beside_all = beside_all + coeffs[4] * lower_z + coeffs[5] * upper_z
    return beside_all, centre


def colour_pass(padded, source, coeffs, parity, colour):
    beside_all, centre = neighbours(padded, coeffs)
    updated = (source + beside_all) / coeffs[6]
    return jnp.where(parity == colour, updated, centre)


def residual_of(padded, source, coeffs):
    beside_all, centre = neighbours(padded, coeffs)
    return source - (coeffs[6] * centre - beside_all)


def restrict_sum(field):
    size_x, size_y, size_z = field.shape
    return 0.5 * field.reshape(size_x // 2, 2, size_y // 2, 2, size_z // 2, 2).sum(axis=(1, 3, 5))


def restrict_mean(field):
    size_x, size_y, size_z = field.shape
    return 0.125 * field.reshape(size_x // 2, 2, size_y // 2, 2, size_z // 2, 2).sum(axis=(1, 3, 5))


def inject(field):
    return jnp.repeat(jnp.repeat(jnp.repeat(field, 2, axis=0), 2, axis=1), 2, axis=2)


def pad_xy(field):
    return jnp.pad(field, ((1, 1), (1, 1), (0, 0)))


def smooth_whole(field, source, coeffs, parity, sweeps):
    for _ in range(sweeps):
        field = colour_pass(pad_xy(field), source, coeffs, parity, 0)
        field = colour_pass(pad_xy(field), source, coeffs, parity, 1)
    return field


def reference(right_side, phase, pressure_guess):
    mobility = 1.0 + 999.0 * phase.astype(jnp.float32)
    coeffs_zero = coefficients(pad_xy(mobility))
    parity_zero = parity_of(mobility.shape, 0, 0)
    pressure = smooth_whole(pressure_guess, right_side, coeffs_zero, parity_zero, SWEEPS)
    fine_res = residual_of(pad_xy(pressure), right_side, coeffs_zero)
    source_one = restrict_sum(fine_res)
    mobility_one = restrict_mean(mobility)
    coeffs_one = coefficients(pad_xy(mobility_one))
    parity_one = parity_of(mobility_one.shape, 0, 0)
    coarse_one = smooth_whole(jnp.zeros_like(source_one), source_one, coeffs_one, parity_one, SWEEPS)
    res_one = residual_of(pad_xy(coarse_one), source_one, coeffs_one)
    source_two = restrict_sum(res_one)
    mobility_two = restrict_mean(mobility_one)
    coeffs_two = coefficients(pad_xy(mobility_two))
    parity_two = parity_of(mobility_two.shape, 0, 0)
    coarse_two = smooth_whole(jnp.zeros_like(source_two), source_two, coeffs_two, parity_two, BOTTOM_SWEEPS)
    coarse_one = smooth_whole(coarse_one + inject(coarse_two), source_one, coeffs_one, parity_one, SWEEPS)
    pressure = smooth_whole(pressure + inject(coarse_one), right_side, coeffs_zero, parity_zero, SWEEPS)
    residual = residual_of(pad_xy(pressure), right_side, coeffs_zero)
    return (pressure, residual)
```

```python
import functools

import jax
import jax.numpy as jnp
from jax import lax
from jax.experimental import pallas as pl
from jax.experimental.pallas import tpu as pltpu
from jax.sharding import PartitionSpec as P

SWEEPS = 2
BOTTOM_SWEEPS = 4


def with_halo(x, sides, width):
    for axis, dim in sides:
        size, length = (lax.axis_size(axis), x.shape[dim])
        up = [(i, (i + 1) % size) for i in range(size - 1)]
        down = [(j, i) for i, j in up]
        last = lax.slice_in_dim(x, length - width, length, axis=dim)
        first = lax.slice_in_dim(x, 0, width, axis=dim)
        before = lax.ppermute(last, axis, up)
        after = lax.ppermute(first, axis, down)
        x = jnp.concatenate([before, x, after], axis=dim)
    return x


def harmonic(left, right):
    total = left + right
    safe = jnp.where(total > 0, total, 1.0)
    return jnp.where(total > 0, 2.0 * left * right / safe, 0.0)


def coefficients(padded):
    faces_x = harmonic(padded[1:], padded[:-1])
    faces_y = harmonic(padded[:, 1:], padded[:, :-1])
    centre = padded[1:-1, 1:-1]
    faces_z = harmonic(centre[:, :, 1:], centre[:, :, :-1])
    zero_plane = jnp.zeros_like(centre[:, :, :1])
    x_lower = faces_x[:-1, 1:-1]
    x_upper = faces_x[1:, 1:-1]
    y_lower = faces_y[1:-1, :-1]
    y_upper = faces_y[1:-1, 1:]
    z_lower = jnp.concatenate([zero_plane, faces_z], axis=2)
    z_upper = jnp.concatenate([faces_z, 2.0 * centre[:, :, -1:]], axis=2)
    diagonal = x_lower + x_upper + y_lower + y_upper + z_lower + z_upper
    diagonal = jnp.where(diagonal > 0, diagonal, 1.0)
    return (x_lower, x_upper, y_lower, y_upper, z_lower, z_upper, diagonal)


def shrink(coeffs):
    return tuple((item[1:-1, 1:-1] for item in coeffs))


def parity_of(extent, start_x, start_y):
    index_x = lax.broadcasted_iota(jnp.int32, extent, 0) + start_x
    index_y = lax.broadcasted_iota(jnp.int32, extent, 1) + start_y
    index_z = lax.broadcasted_iota(jnp.int32, extent, 2)
    return (index_x + index_y + index_z) % 2


def neighbours(padded, coeffs):
    centre = padded[1:-1, 1:-1]
    zero_plane = jnp.zeros_like(centre[:, :, :1])
    lower_z = jnp.concatenate([zero_plane, centre[:, :, :-1]], axis=2)
    upper_z = jnp.concatenate([centre[:, :, 1:], zero_plane], axis=2)
    beside_all = coeffs[0] * padded[:-2, 1:-1] + coeffs[1] * padded[2:, 1:-1]
    beside_all = beside_all + coeffs[2] * padded[1:-1, :-2] + coeffs[3] * padded[1:-1, 2:]
    beside_all = beside_all + coeffs[4] * lower_z + coeffs[5] * upper_z
    return (beside_all, centre)


def colour_pass(padded, source, coeffs, parity, colour):
    beside_all, centre = neighbours(padded, coeffs)
    updated = (source + beside_all) / coeffs[6]
    return jnp.where(parity == colour, updated, centre)


def residual_of(padded, source, coeffs):
    beside_all, centre = neighbours(padded, coeffs)
    return source - (coeffs[6] * centre - beside_all)


def restrict_sum(field):
    size_x, size_y, size_z = field.shape
    return 0.5 * field.reshape(size_x // 2, 2, size_y // 2, 2, size_z // 2, 2).sum(axis=(1, 3, 5))


def restrict_mean(field):
    size_x, size_y, size_z = field.shape
    return 0.125 * field.reshape(size_x // 2, 2, size_y // 2, 2, size_z // 2, 2).sum(axis=(1, 3, 5))


def inject(field):
    return jnp.repeat(jnp.repeat(jnp.repeat(field, 2, axis=0), 2, axis=1), 2, axis=2)


def rim_one(field):
    return with_halo(field, (("gx", 0), ("yz", 1)), 1)


def rim_two(field):
    return with_halo(field, (("gx", 0), ("yz", 1)), 2)


def offsets(field):
    return (lax.axis_index("gx") * field.shape[0], lax.axis_index("yz") * field.shape[1])


def prepare_plain(mobility):
    start_x, start_y = offsets(mobility)
    return (coefficients(rim_one(mobility)), parity_of(mobility.shape, start_x, start_y))


def prepare(mobility):
    start_x, start_y = offsets(mobility)
    size_x, size_y, size_z = mobility.shape
    region = coefficients(rim_two(mobility))
    loop_parity = parity_of((size_x + 2, size_y + 2, size_z), start_x - 1, start_y - 1)
    operator_set = (
        shrink(region),
        parity_of(mobility.shape, start_x, start_y),
        region,
        loop_parity,
    )
    return operator_set


def smooth_plain(field, source, operator_set, sweeps, rim):
    coeffs = operator_set[0]
    parity = operator_set[1]
    for _ in range(sweeps):
        field = colour_pass(rim(field), source, coeffs, parity, 0)
        field = colour_pass(rim(field), source, coeffs, parity, 1)
    return field


def smooth(field, source, operator_set, sweeps):
    interior, parity, region, loop_parity = operator_set
    source_loop = rim_one(source)
    for _ in range(sweeps):
        loop_field = colour_pass(rim_two(field), source_loop, region, loop_parity, 0)
        field = colour_pass(loop_field, source, interior, parity, 1)
    return field


def local(right_side, phase, pressure_guess):
    mobility = 1.0 + 999.0 * phase.astype(jnp.float32)
    level_zero = prepare(mobility)
    pressure = smooth(pressure_guess, right_side, level_zero, SWEEPS)
    fine_res = residual_of(rim_one(pressure), right_side, level_zero[0])
    source_one = restrict_sum(fine_res)
    mobility_one = restrict_mean(mobility)
    level_one = prepare(mobility_one)
    coarse_one = smooth(jnp.zeros_like(source_one), source_one, level_one, SWEEPS)
    res_one = residual_of(rim_one(coarse_one), source_one, level_one[0])
    source_two = restrict_sum(res_one)
    mobility_two = restrict_mean(mobility_one)
    level_two = prepare_plain(mobility_two)
    coarse_two = smooth_plain(
        jnp.zeros_like(source_two), source_two, level_two, BOTTOM_SWEEPS, rim_one
    )
    coarse_one = smooth(coarse_one + inject(coarse_two), source_one, level_one, SWEEPS)
    pressure = smooth(pressure + inject(coarse_one), right_side, level_zero, SWEEPS)
    residual = residual_of(rim_one(pressure), right_side, level_zero[0])
    return (pressure, residual)


ROWS = 8
WIN = 3 * ROWS
REACH = 3
MIX = 2.0 / 1001.0


def place_of(rows, columns):
    slab = []
    for g in range(rows):
        a = (g // 2) * 2 + ((g % 2) ^ ((g // 2) % 2))
        slab += [a * columns + (j if a % 2 == 0 else columns - 1 - j) for j in range(columns)]
    return slab


def slab_index(columns):
    g, j = lax.axis_index("gx"), lax.axis_index("yz")
    a = (g // 2) * 2 + (g + g // 2) % 2
    return a * columns + jnp.where(a % 2 == 0, j, columns - 1 - j)


def device_of(slab, columns):
    a, b = slab // columns, slab % columns
    g = (a // 2) * 2 + (a + a // 2) % 2
    return g * columns + jnp.where(a % 2 == 0, b, columns - 1 - b)


def lanes(shape):
    return lax.broadcasted_iota(jnp.int32, shape, len(shape) - 1)


def swap_lanes(v, step):
    width = v.shape[-1]
    up, down = pltpu.roll(v, step, 1), pltpu.roll(v, width - step, 1)
    return jnp.where((lanes(v.shape) // step) % 2 == 0, down, up)


def swap_blocks(tiles):
    block = lanes(tiles[0].shape) // 32
    low, even = block < 2, block % 2 == 0
    t = [None] * 4
    for a in (0, 1):
        t[a] = jnp.where(low, tiles[a], pltpu.roll(tiles[a + 2], 64, 1))
        t[a + 2] = jnp.where(low, pltpu.roll(tiles[a], 64, 1), tiles[a + 2])
    out = [None] * 4
    for a in (0, 2):
        out[a] = jnp.where(even, t[a], pltpu.roll(t[a + 1], 32, 1))
        out[a + 1] = jnp.where(even, pltpu.roll(t[a], 96, 1), t[a + 1])
    return out


def brick_parity(shape):
    lane = lanes(shape)
    return (lane // 32 + lane) % 2


def pack_kernel(order, source_ref, phase_ref, guess_ref, out_ref, turned):
    for a, ref in enumerate((source_ref, phase_ref, guess_ref)):
        brick = ref[...].reshape(128, ref.shape[2])
        if a == 1:
            brick = 1.0 + 999.0 * brick.astype(jnp.float32)
        turned[a] = brick.T
    even = brick_parity((ROWS, 128)) == 0
    for device, slab in enumerate(order):
        base = 2 * ROWS * slab
        for a, at in ((1, 0), (0, 2 * ROWS), (2, 3 * ROWS)):
            low = turned[a, pl.ds(base, ROWS, stride=2), :]
            high = turned[a, pl.ds(base + 1, ROWS, stride=2), :]
            if a != 2:
                out_ref[device, at : at + ROWS, :] = jnp.where(even, low, high)
            out_ref[device, at + ROWS : at + 2 * ROWS, :] = jnp.where(even, high, low)


def unpack_kernel(order, in_ref, pressure_ref, residual_ref, turned):
    even = brick_parity((ROWS, 128)) == 0
    for device, slab in enumerate(order):
        base = 2 * ROWS * slab
        p0, p1 = in_ref[device, 0:ROWS, :], in_ref[device, ROWS : 2 * ROWS, :]
        r0 = in_ref[device, 2 * ROWS : 3 * ROWS, :]
        turned[0, pl.ds(base, ROWS, stride=2), :] = jnp.where(even, p0, p1)
        turned[0, pl.ds(base + 1, ROWS, stride=2), :] = jnp.where(even, p1, p0)
        turned[1, pl.ds(base, ROWS, stride=2), :] = jnp.where(even, r0, 0.0)
        turned[1, pl.ds(base + 1, ROWS, stride=2), :] = jnp.where(even, 0.0, r0)
    for a, ref in enumerate((pressure_ref, residual_ref)):
        ref[...] = turned[a].T.reshape(ref.shape)


MID = slice(ROWS, ROWS + WIN)
BELOW = slice(ROWS - 1, ROWS + WIN - 1)
ABOVE = slice(ROWS + 1, ROWS + WIN + 1)


def clear_edges(ref):
    planes, _, width = ref.shape
    zero = jnp.zeros((ref.shape[1], width), jnp.float32)
    ref[0] = zero
    ref[planes - 1] = zero

    def one(x, _):
        ref[x, 0:ROWS, :] = zero[:ROWS]
        ref[x, ROWS + WIN :, :] = zero[:ROWS]
        return 0

    lax.fori_loop(1, planes - 1, one, 0)


def around_fine(ref, x, low):
    centre = ref[x + 1, MID, :]
    width = centre.shape[1]
    return (
        ref[x, MID, :],
        ref[x + 2, MID, :],
        pltpu.roll(centre, 1, 1),
        pltpu.roll(centre, width - 1, 1),
        centre,
        jnp.where(low, ref[x + 1, BELOW, :], ref[x + 1, ABOVE, :]),
    )


def around_coarse(ref, i, low):
    centre = ref[i + 1, MID, :]
    width = centre.shape[1]
    return (
        ref[i + 1, BELOW, :],
        ref[i + 1, ABOVE, :],
        pltpu.roll(centre, 2, 1),
        pltpu.roll(centre, width - 2, 1),
        centre,
        jnp.where(low, ref[i, MID, :], ref[i + 2, MID, :]),
    )


def around_coarsest(planes, k, low):
    centre = planes[k + 1]
    rows, width = centre.shape
    return (
        pltpu.roll(centre, 1, 0),
        pltpu.roll(centre, rows - 1, 0),
        pltpu.roll(centre, 4, 1),
        pltpu.roll(centre, width - 4, 1),
        centre,
        jnp.where(low, planes[k], planes[k + 2]),
    )


def walls(sides, first, last):
    return sides[:2] + (jnp.where(first, 0.0, sides[2]), jnp.where(last, 0.0, sides[3])) + sides[4:]


def mean_fine(u, w):
    return jnp.where(u == w, u, u * w * MIX)


def mean_any(u, w):
    total = u + w
    return 2.0 * u * w / jnp.where(total > 0, total, 1.0)


def weights(mean, u, sides, top):
    faces = [mean(u, w) for w in sides]
    diagonal = (faces[0] + faces[1]) + (faces[2] + faces[3]) + (faces[4] + faces[5])
    diagonal = diagonal + jnp.where(top, 2.0 * u, 0.0)
    diagonal = jnp.where(diagonal > 0, diagonal, 1.0)
    inverse = 1.0 / diagonal
    return [face * inverse for face in faces], inverse, diagonal


def relax(scaled, share, sides):
    parts = [share[a] * sides[a] for a in range(6)]
    return scaled + ((parts[0] + parts[1]) + (parts[2] + parts[3]) + (parts[4] + parts[5]))


def fine_low(x_parity, colour, width):
    return (lanes((WIN, width)) + (x_parity + colour)) % 2 == 0


def coarse_low(colour, width):
    row = lax.broadcasted_iota(jnp.int32, (WIN, width), 0)
    return (row + lanes((WIN, width)) // 2 + colour) % 2 == 0


def fine_pass(colour, target, other, share, scaled):
    planes, width = share.shape[1], share.shape[3]

    def two(i, _):
        for parity in (0, 1):
            x = 2 * i + parity
            sides = around_fine(other, x, fine_low(parity, colour, width))
            target[x + 1, MID, :] = relax(scaled[x], share[:, x], sides)
        return 0

    lax.fori_loop(0, planes // 2, two, 0)


def coarse_pass(colour, target, other, share, scaled):
    planes, width = share.shape[1], share.shape[3]

    def one(i, _):
        sides = around_coarse(other, i, coarse_low(colour, width))
        target[i + 1, MID, :] = relax(scaled[i], share[:, i], sides)
        return 0

    lax.fori_loop(0, planes, one, 0)


def down_kernel(
    own, before, after,
    share0, share1, scaled0, scaled1, diagonal0, field1,
    cshare0, cshare1, cscaled0, cscaled1, cfield1, packed, message,
    m0, m1, v0, v1, cm0, cm1, e0, e1, cdiagonal0, rest,
):
    planes, width = share0.shape[1], share0.shape[3]
    for ref in (m0, m1, v0, v1, cm0, cm1, e0, e1):
        clear_edges(ref)

    def unfold(i, _):
        for slab, ref in enumerate((before, own, after)):
            at = slab * ROWS
            for a, to in enumerate((m0, m1, scaled0, scaled1, v1)):
                tiles = [ref[4 * i + j, a * ROWS : (a + 1) * ROWS, :] for j in range(4)]
                shift = 1 if a in (0, 1, 4) else 0
                for j, tile in enumerate(swap_blocks(tiles)):
                    row = at + ROWS * shift
                    to[4 * i + j + shift, row : row + ROWS, :] = tile
        return 0

    lax.fori_loop(0, planes // 4, unfold, 0)

    lane = lanes((WIN, width))

    def fine_weights(i, _):
        for parity in (0, 1):
            x = 2 * i + parity
            for colour, mine, other, share, scaled in ((0, m0, m1, share0, scaled0), (1, m1, m0, share1, scaled1)):
                low = fine_low(parity, colour, width)
                u = mine[x + 1, MID, :]
                sides = walls(around_fine(other, x, low), lane == 0, lane == width - 1)
                top = jnp.logical_and(jnp.logical_not(low), sides[5] == 0)
                shares, inverse, diagonal = weights(mean_fine, u, sides, top)
                for a in range(6):
                    share[a, x] = shares[a]
                scaled[x] = scaled[x] * inverse
                if colour == 0:
                    diagonal0[x] = diagonal
        return 0

    lax.fori_loop(0, planes // 2, fine_weights, 0)

    for _ in range(SWEEPS):
        fine_pass(0, v0, v1, share0, scaled0)
        fine_pass(1, v1, v0, share1, scaled1)

    even = coarse_low(0, width)

    def restrict(i, _):
        fields, mobilities = [], []
        for half in (0, 1):
            total, mass = 0.0, 0.0
            for parity in (0, 1):
                x = 4 * i + 2 * half + parity
                sides = around_fine(v1, x, fine_low(parity, 0, width))
                total = total + diagonal0[x] * (relax(scaled0[x], share0[:, x], sides) - v0[x + 1, MID, :])
                mass = mass + (m0[x + 1, MID, :] + m1[x + 1, MID, :])
            fields.append(0.5 * (total + swap_lanes(total, 1)))
            mobilities.append(0.125 * (mass + swap_lanes(mass, 1)))
        cscaled0[i] = jnp.where(even, fields[0], fields[1])
        cscaled1[i] = jnp.where(even, fields[1], fields[0])
        cm0[i + 1, MID, :] = jnp.where(even, mobilities[0], mobilities[1])
        cm1[i + 1, MID, :] = jnp.where(even, mobilities[1], mobilities[0])
        return 0

    lax.fori_loop(0, planes // 4, restrict, 0)

    def copy_field(x, _):
        field1[x] = v1[x + 1, MID, :]
        return 0

    lax.fori_loop(0, planes, copy_field, 0)

    def coarse_weights(i, _):
        for colour, mine, other, share, scaled in ((0, cm0, cm1, cshare0, cscaled0), (1, cm1, cm0, cshare1, cscaled1)):
            u = mine[i + 1, MID, :]
            sides = walls(around_coarse(other, i, coarse_low(colour, width)), lane < 2, lane >= width - 2)
            shares, inverse, diagonal = weights(mean_any, u, sides, sides[1] == 0)
            for a in range(6):
                share[a, i] = shares[a]
            scaled[i] = scaled[i] * inverse
            if colour == 0:
                cdiagonal0[i] = diagonal
        e0[i + 1, MID, :] = cscaled0[i]
        return 0

    lax.fori_loop(0, planes // 4, coarse_weights, 0)

    for sweep in range(SWEEPS):
        if sweep:
            coarse_pass(0, e0, e1, cshare0, cscaled0)
        coarse_pass(1, e1, e0, cshare1, cscaled1)

    here = slice(ROWS, 2 * ROWS)
    part = lanes((ROWS, width)) % 4
    row = lax.broadcasted_iota(jnp.int32, (ROWS, width), 0)
    pick = jnp.logical_and(row % 2 == 0, part == row // 2)
    first = lanes((ROWS, width)) % 2 == 0
    low = coarse_low(0, width)
    for i in range(planes // 4):
        sides = around_coarse(e1, i, low)
        rest[...] = cdiagonal0[i] * (relax(cscaled0[i], cshare0[:, i], sides) - e0[i + 1, MID, :])
        pair = rest[ROWS : 2 * ROWS, :] + rest[ROWS + 1 : 2 * ROWS + 1, :]
        pair = 0.5 * (pair + swap_lanes(pair, 2))
        packed[0, i : i + 1, :] = jnp.sum(jnp.where(pick, pair, 0.0), axis=0, keepdims=True)
        rest[...] = cm0[i + 1, MID, :] + cm1[i + 1, MID, :]
        pair = rest[ROWS : 2 * ROWS, :] + rest[ROWS + 1 : 2 * ROWS + 1, :]
        pair = 0.125 * (pair + swap_lanes(pair, 2))
        at = planes // 4 + i
        packed[0, at : at + 1, :] = jnp.sum(jnp.where(pick, pair, 0.0), axis=0, keepdims=True)
        cfield1[i] = e1[i + 1, MID, :]
        message[i] = jnp.where(first, cfield1[i, here, :], cscaled0[i, here, :])
    tile = packed[0]
    for device in range(1, packed.shape[0]):
        packed[device] = tile


def up_kernel(
    columns,
    gathered, before, after,
    share0, share1, scaled0, scaled1, diagonal0, field1,
    cshare0, cshare1, cscaled0, cscaled1, cfield1,
    out,
    v0, v1, e0, e1, wide0, bshare, coarsest, spread,
):
    planes, width = share0.shape[1], share0.shape[3]
    count = gathered.shape[0]
    rows = planes // 4
    for ref in (v0, v1, e0, e1):
        clear_edges(ref)

    slab = slab_index(columns)
    lane = lanes((rows, width))
    part = lane % 4
    sources, mobilities = [], []
    for w in range(-REACH, REACH + 1):
        near = slab + w
        inside = jnp.logical_and(near >= 0, near < count)
        device = device_of(jnp.clip(near, 0, count - 1), columns)
        keep = jnp.where(inside, 1.0, 0.0)
        for at, into in ((0, sources), (rows, mobilities)):
            tile = gathered[device, at : at + rows, :] * keep
            for z in range(4):
                v = jnp.where(part == z, tile, 0.0)
                v = v + swap_lanes(v, 1)
                into.append(v + swap_lanes(v, 2))

    parity = (lax.broadcasted_iota(jnp.int32, (rows, width), 0) + lane // 4) % 2
    pairs = len(sources) // 2
    zero = jnp.zeros((rows, width), jnp.float32)
    low = (parity == 0, parity == 1)

    def coloured(planes_of):
        first = [jnp.where(low[0], planes_of[2 * k], planes_of[2 * k + 1]) for k in range(pairs)]
        second = [jnp.where(low[0], planes_of[2 * k + 1], planes_of[2 * k]) for k in range(pairs)]
        return [zero] + first + [zero], [zero] + second + [zero]

    source, mobility = coloured(sources), coloured(mobilities)
    row = lax.broadcasted_iota(jnp.int32, (rows, width), 0)
    scaled = ([], [])
    for k in range(pairs):
        for colour in (0, 1):
            sides = around_coarsest(mobility[1 - colour], k, low[colour])
            sides = (jnp.where(row == 0, 0.0, sides[0]), jnp.where(row == rows - 1, 0.0, sides[1])) + sides[2:]
            sides = walls(sides, lane < 4, lane >= width - 4)
            top = jnp.logical_and(jnp.logical_not(low[colour]), sides[5] == 0)
            shares, inverse, _ = weights(mean_any, mobility[colour][k + 1], sides, top)
            for a in range(6):
                bshare[colour, a, k] = shares[a]
            scaled[colour].append(source[colour][k + 1] * inverse)

    fields = [[zero] + scaled[0] + [zero], None]
    for step in range(1, 2 * BOTTOM_SWEEPS):
        colour = step % 2
        new = []
        for k in range(pairs):
            sides = around_coarsest(fields[1 - colour], k, low[colour])
            new.append(relax(scaled[colour][k], [bshare[colour, a, k] for a in range(6)], sides))
        fields[colour] = [zero] + new + [zero]

    start = 4 * REACH - ROWS // 2
    for k in range(WIN // 4):
        a, b = fields[0][start // 2 + k + 1], fields[1][start // 2 + k + 1]
        coarsest[2 * k * rows : (2 * k + 1) * rows, :] = jnp.where(low[0], a, b)
        coarsest[(2 * k + 1) * rows : (2 * k + 2) * rows, :] = jnp.where(low[0], b, a)

    first = lanes((ROWS, width)) % 2 == 0
    for i in range(rows):
        half = coarsest[pl.ds(i, WIN // 2, stride=rows), :]
        spread[pl.ds(0, WIN // 2, stride=2), :] = half
        spread[pl.ds(1, WIN // 2, stride=2), :] = half
        e1[i + 1, 2 * ROWS : 3 * ROWS, :] = cfield1[i, ROWS : 2 * ROWS, :] + spread[ROWS : 2 * ROWS, :]
        for at, ref in ((0, before), (2 * ROWS, after)):
            mixed = ref[i]
            other = swap_lanes(mixed, 1)
            e1[i + 1, ROWS + at : 2 * ROWS + at, :] = jnp.where(first, mixed, other) + spread[at : at + ROWS, :]
            wide0[i, at : at + ROWS, :] = jnp.where(first, other, mixed)
        wide0[i, ROWS : 2 * ROWS, :] = cscaled0[i, ROWS : 2 * ROWS, :]

    for _ in range(SWEEPS):
        coarse_pass(0, e0, e1, cshare0, wide0)
        coarse_pass(1, e1, e0, cshare1, cscaled1)

    even = coarse_low(0, width)

    def correct(i, _):
        a, b = e0[i + 1, MID, :], e1[i + 1, MID, :]
        for half, add in ((0, jnp.where(even, a, b)), (1, jnp.where(even, b, a))):
            for parity in (0, 1):
                x = 4 * i + 2 * half + parity
                v1[x + 1, MID, :] = field1[x] + add
        return 0

    lax.fori_loop(0, rows, correct, 0)

    for _ in range(SWEEPS):
        fine_pass(0, v0, v1, share0, scaled0)
        fine_pass(1, v1, v0, share1, scaled1)

    here = slice(2 * ROWS, 3 * ROWS)

    def fold(i, _):
        rest = []
        for parity in range(4):
            x = 4 * i + parity
            sides = around_fine(v1, x, fine_low(parity % 2, 0, width))
            full = diagonal0[x] * (relax(scaled0[x], share0[:, x], sides) - v0[x + 1, MID, :])
            rest.append(full[ROWS : 2 * ROWS])
        for a, tiles in (
            (0, [v0[4 * i + b + 1, here, :] for b in range(4)]),
            (1, [v1[4 * i + b + 1, here, :] for b in range(4)]),
            (2, rest),
        ):
            for j, tile in enumerate(swap_blocks(tiles)):
                out[4 * i + j, a * ROWS : (a + 1) * ROWS, :] = tile
        return 0

    lax.fori_loop(0, rows, fold, 0)


def local_slabs(shape, right_side, phase, pressure_guess):
    across, columns = shape
    count = across * columns
    bx, by, length = right_side.shape
    planes, width = across * bx, columns * by
    f32 = jnp.float32
    order = place_of(across, columns)
    path = sorted(range(count), key=lambda device: order[device])
    up = [(path[k], path[k + 1]) for k in range(count - 1)]
    down = [(b, a) for a, b in up]
    axes = ("gx", "yz")
    params = pltpu.CompilerParams(vmem_limit_bytes=56 * 1024 * 1024)

    def struct(*dims):
        return jax.ShapeDtypeStruct(dims, f32)

    def vmem(*dims):
        return pltpu.VMEM(dims, f32)

    bricks = pl.pallas_call(
        functools.partial(pack_kernel, order),
        out_shape=struct(count, 5 * ROWS, 128),
        scratch_shapes=[vmem(3, length, 128)],
        compiler_params=params,
        name="pack",
    )(right_side, phase, pressure_guess)
    own = lax.all_to_all(bricks, axes, 0, 0)
    before = lax.ppermute(own, axes, up)
    after = lax.ppermute(own, axes, down)

    coarse = planes // 4
    fine = [struct(6, planes, WIN, width)] * 2 + [struct(planes, WIN, width)] * 4
    half = [struct(6, coarse, WIN, width)] * 2 + [struct(coarse, WIN, width)] * 3
    padded = [vmem(planes + 2, WIN + 2 * ROWS, width)] * 2
    cpadded = [vmem(coarse + 2, WIN + 2 * ROWS, width)] * 2
    *state, packed, message = pl.pallas_call(
        down_kernel,
        out_shape=fine + half + [struct(count, 2 * coarse, width), struct(coarse, ROWS, width)],
        scratch_shapes=padded * 2 + cpadded * 2 + [vmem(coarse, WIN, width), vmem(WIN, width)],
        compiler_params=params,
        name="down",
    )(own, before, after)
    gathered = lax.all_to_all(packed, axes, 0, 0)
    e_before = lax.ppermute(message, axes, up)
    e_after = lax.ppermute(message, axes, down)

    cycle = pl.pallas_call(
        functools.partial(up_kernel, columns),
        out_shape=struct(count, 3 * ROWS, 128),
        scratch_shapes=padded + cpadded + [
            vmem(coarse, WIN, width),
            vmem(2, 6, 2 * (2 * REACH + 1), coarse, width),
            vmem(WIN // 2 * coarse, width),
            vmem(WIN, width),
        ],
        compiler_params=params,
        name="up",
    )(gathered, e_before, e_after, *state)
    back = lax.all_to_all(cycle, axes, 0, 0)
    return pl.pallas_call(
        functools.partial(unpack_kernel, order),
        out_shape=[struct(bx, by, length)] * 2,
        scratch_shapes=[vmem(2, length, 128)],
        compiler_params=params,
        name="unpack",
    )(back)


def solution(mesh):
    spec = P("gx", "yz", None)
    shape = (mesh.shape["gx"], mesh.shape["yz"])

    def cycle(right_side, phase, pressure_guess):
        bx, by, length = right_side.shape
        slabs = (bx, by, shape[1]) == (4, 32, 4) and length == 2 * ROWS * shape[0] * shape[1]
        if slabs and shape[0] == 8:
            return local_slabs(shape, right_side, phase, pressure_guess)
        return local(right_side, phase, pressure_guess)

    return jax.shard_map(cycle, mesh=mesh, in_specs=(spec,) * 3, out_specs=(spec,) * 2, check_vma=False)
```

```python
import functools

import jax
import jax.numpy as jnp
from jax import lax
from jax.experimental import pallas as pl
from jax.experimental.pallas import tpu as pltpu
from jax.sharding import PartitionSpec as P

SWEEPS = 2
BOTTOM_SWEEPS = 4


def with_halo(x, sides, width):
    for axis, dim in sides:
        size, length = (lax.axis_size(axis), x.shape[dim])
        up = [(i, (i + 1) % size) for i in range(size - 1)]
        down = [(j, i) for i, j in up]
        last = lax.slice_in_dim(x, length - width, length, axis=dim)
        first = lax.slice_in_dim(x, 0, width, axis=dim)
        before = lax.ppermute(last, axis, up)
        after = lax.ppermute(first, axis, down)
        x = jnp.concatenate([before, x, after], axis=dim)
    return x


def harmonic(left, right):
    total = left + right
    safe = jnp.where(total > 0, total, 1.0)
    return jnp.where(total > 0, 2.0 * left * right / safe, 0.0)


def coefficients(padded):
    faces_x = harmonic(padded[1:], padded[:-1])
    faces_y = harmonic(padded[:, 1:], padded[:, :-1])
    centre = padded[1:-1, 1:-1]
    faces_z = harmonic(centre[:, :, 1:], centre[:, :, :-1])
    zero_plane = jnp.zeros_like(centre[:, :, :1])
    x_lower = faces_x[:-1, 1:-1]
    x_upper = faces_x[1:, 1:-1]
    y_lower = faces_y[1:-1, :-1]
    y_upper = faces_y[1:-1, 1:]
    z_lower = jnp.concatenate([zero_plane, faces_z], axis=2)
    z_upper = jnp.concatenate([faces_z, 2.0 * centre[:, :, -1:]], axis=2)
    diagonal = x_lower + x_upper + y_lower + y_upper + z_lower + z_upper
    diagonal = jnp.where(diagonal > 0, diagonal, 1.0)
    return (x_lower, x_upper, y_lower, y_upper, z_lower, z_upper, diagonal)


def shrink(coeffs):
    return tuple((item[1:-1, 1:-1] for item in coeffs))


def parity_of(extent, start_x, start_y):
    index_x = lax.broadcasted_iota(jnp.int32, extent, 0) + start_x
    index_y = lax.broadcasted_iota(jnp.int32, extent, 1) + start_y
    index_z = lax.broadcasted_iota(jnp.int32, extent, 2)
    return (index_x + index_y + index_z) % 2


def neighbours(padded, coeffs):
    centre = padded[1:-1, 1:-1]
    zero_plane = jnp.zeros_like(centre[:, :, :1])
    lower_z = jnp.concatenate([zero_plane, centre[:, :, :-1]], axis=2)
    upper_z = jnp.concatenate([centre[:, :, 1:], zero_plane], axis=2)
    beside_all = coeffs[0] * padded[:-2, 1:-1] + coeffs[1] * padded[2:, 1:-1]
    beside_all = beside_all + coeffs[2] * padded[1:-1, :-2] + coeffs[3] * padded[1:-1, 2:]
    beside_all = beside_all + coeffs[4] * lower_z + coeffs[5] * upper_z
    return (beside_all, centre)


def colour_pass(padded, source, coeffs, parity, colour):
    beside_all, centre = neighbours(padded, coeffs)
    updated = (source + beside_all) / coeffs[6]
    return jnp.where(parity == colour, updated, centre)


def residual_of(padded, source, coeffs):
    beside_all, centre = neighbours(padded, coeffs)
    return source - (coeffs[6] * centre - beside_all)


def restrict_sum(field):
    size_x, size_y, size_z = field.shape
    return 0.5 * field.reshape(size_x // 2, 2, size_y // 2, 2, size_z // 2, 2).sum(axis=(1, 3, 5))


def restrict_mean(field):
    size_x, size_y, size_z = field.shape
    return 0.125 * field.reshape(size_x // 2, 2, size_y // 2, 2, size_z // 2, 2).sum(axis=(1, 3, 5))


def inject(field):
    return jnp.repeat(jnp.repeat(jnp.repeat(field, 2, axis=0), 2, axis=1), 2, axis=2)


def rim_one(field):
    return with_halo(field, (("gx", 0), ("yz", 1)), 1)


def rim_two(field):
    return with_halo(field, (("gx", 0), ("yz", 1)), 2)


def offsets(field):
    return (lax.axis_index("gx") * field.shape[0], lax.axis_index("yz") * field.shape[1])


def prepare_plain(mobility):
    start_x, start_y = offsets(mobility)
    return (coefficients(rim_one(mobility)), parity_of(mobility.shape, start_x, start_y))


def prepare(mobility):
    start_x, start_y = offsets(mobility)
    size_x, size_y, size_z = mobility.shape
    region = coefficients(rim_two(mobility))
    loop_parity = parity_of((size_x + 2, size_y + 2, size_z), start_x - 1, start_y - 1)
    operator_set = (
        shrink(region),
        parity_of(mobility.shape, start_x, start_y),
        region,
        loop_parity,
    )
    return operator_set


def smooth_plain(field, source, operator_set, sweeps, rim):
    coeffs = operator_set[0]
    parity = operator_set[1]
    for _ in range(sweeps):
        field = colour_pass(rim(field), source, coeffs, parity, 0)
        field = colour_pass(rim(field), source, coeffs, parity, 1)
    return field


def smooth(field, source, operator_set, sweeps):
    interior, parity, region, loop_parity = operator_set
    source_loop = rim_one(source)
    for _ in range(sweeps):
        loop_field = colour_pass(rim_two(field), source_loop, region, loop_parity, 0)
        field = colour_pass(loop_field, source, interior, parity, 1)
    return field


def local(right_side, phase, pressure_guess):
    mobility = 1.0 + 999.0 * phase.astype(jnp.float32)
    level_zero = prepare(mobility)
    pressure = smooth(pressure_guess, right_side, level_zero, SWEEPS)
    fine_res = residual_of(rim_one(pressure), right_side, level_zero[0])
    source_one = restrict_sum(fine_res)
    mobility_one = restrict_mean(mobility)
    level_one = prepare(mobility_one)
    coarse_one = smooth(jnp.zeros_like(source_one), source_one, level_one, SWEEPS)
    res_one = residual_of(rim_one(coarse_one), source_one, level_one[0])
    source_two = restrict_sum(res_one)
    mobility_two = restrict_mean(mobility_one)
    level_two = prepare_plain(mobility_two)
    coarse_two = smooth_plain(
        jnp.zeros_like(source_two), source_two, level_two, BOTTOM_SWEEPS, rim_one
    )
    coarse_one = smooth(coarse_one + inject(coarse_two), source_one, level_one, SWEEPS)
    pressure = smooth(pressure + inject(coarse_one), right_side, level_zero, SWEEPS)
    residual = residual_of(rim_one(pressure), right_side, level_zero[0])
    return (pressure, residual)


ROWS = 8
WIN = 3 * ROWS
REACH = 3
MIX = 2.0 / 1001.0


def place_of(rows, columns):
    slab = []
    for g in range(rows):
        a = (g // 2) * 2 + ((g % 2) ^ ((g // 2) % 2))
        slab += [a * columns + (j if a % 2 == 0 else columns - 1 - j) for j in range(columns)]
    return slab


def slab_index(columns):
    g, j = lax.axis_index("gx"), lax.axis_index("yz")
    a = (g // 2) * 2 + (g + g // 2) % 2
    return a * columns + jnp.where(a % 2 == 0, j, columns - 1 - j)


def device_of(slab, columns):
    a, b = slab // columns, slab % columns
    g = (a // 2) * 2 + (a + a // 2) % 2
    return g * columns + jnp.where(a % 2 == 0, b, columns - 1 - b)


def lanes(shape):
    return lax.broadcasted_iota(jnp.int32, shape, len(shape) - 1)


def swap_lanes(v, step):
    width = v.shape[-1]
    up, down = pltpu.roll(v, step, 1), pltpu.roll(v, width - step, 1)
    return jnp.where((lanes(v.shape) // step) % 2 == 0, down, up)


def swap_blocks(tiles):
    block = lanes(tiles[0].shape) // 32
    low, even = block < 2, block % 2 == 0
    t = [None] * 4
    for a in (0, 1):
        t[a] = jnp.where(low, tiles[a], pltpu.roll(tiles[a + 2], 64, 1))
        t[a + 2] = jnp.where(low, pltpu.roll(tiles[a], 64, 1), tiles[a + 2])
    out = [None] * 4
    for a in (0, 2):
        out[a] = jnp.where(even, t[a], pltpu.roll(t[a + 1], 32, 1))
        out[a + 1] = jnp.where(even, pltpu.roll(t[a], 96, 1), t[a + 1])
    return out


def brick_parity(shape):
    lane = lanes(shape)
    return (lane // 32 + lane) % 2


def pack_kernel(order, source_hbm, phase_hbm, guess_hbm, out_ref, source_ref, phase_ref, guess_ref, turned, arrived):
    copies = [
        pltpu.make_async_copy(hbm, ref, arrived.at[a])
        for a, (hbm, ref) in enumerate(((source_hbm, source_ref), (phase_hbm, phase_ref), (guess_hbm, guess_ref)))
    ]
    for copy in copies:
        copy.start()
    for a, ref in enumerate((source_ref, phase_ref, guess_ref)):
        copies[a].wait()
        brick = ref[...].reshape(128, ref.shape[2])
        if a == 1:
            brick = 1.0 + 999.0 * brick.astype(jnp.float32)
        turned[a] = brick.T
    even = brick_parity((ROWS, 128)) == 0
    for device, slab in enumerate(order):
        base = 2 * ROWS * slab
        for a, at in ((1, 0), (0, 2 * ROWS), (2, 3 * ROWS)):
            low = turned[a, pl.ds(base, ROWS, stride=2), :]
            high = turned[a, pl.ds(base + 1, ROWS, stride=2), :]
            if a != 2:
                out_ref[device, at : at + ROWS, :] = jnp.where(even, low, high)
            out_ref[device, at + ROWS : at + 2 * ROWS, :] = jnp.where(even, high, low)


def unpack_kernel(order, in_ref, pressure_ref, residual_ref, turned):
    even = brick_parity((ROWS, 128)) == 0
    for device, slab in enumerate(order):
        base = 2 * ROWS * slab
        p0, p1 = in_ref[device, 0:ROWS, :], in_ref[device, ROWS : 2 * ROWS, :]
        r0 = in_ref[device, 2 * ROWS : 3 * ROWS, :]
        turned[0, pl.ds(base, ROWS, stride=2), :] = jnp.where(even, p0, p1)
        turned[0, pl.ds(base + 1, ROWS, stride=2), :] = jnp.where(even, p1, p0)
        turned[1, pl.ds(base, ROWS, stride=2), :] = jnp.where(even, r0, 0.0)
        turned[1, pl.ds(base + 1, ROWS, stride=2), :] = jnp.where(even, 0.0, r0)
    for a, ref in enumerate((pressure_ref, residual_ref)):
        ref[...] = turned[a].T.reshape(ref.shape)


KEPT = 11
MID = slice(ROWS, ROWS + WIN)
BELOW = slice(ROWS - 1, ROWS + WIN - 1)
ABOVE = slice(ROWS + 1, ROWS + WIN + 1)


def clear_edges(ref):
    planes, _, width = ref.shape
    zero = jnp.zeros((ref.shape[1], width), jnp.float32)
    ref[0] = zero
    ref[planes - 1] = zero

    def one(x, _):
        ref[x, 0:ROWS, :] = zero[:ROWS]
        ref[x, ROWS + WIN :, :] = zero[:ROWS]
        return 0

    lax.fori_loop(1, planes - 1, one, 0)


def around_fine(ref, x, low):
    centre = ref[x + 1, MID, :]
    width = centre.shape[1]
    return (
        ref[x, MID, :],
        ref[x + 2, MID, :],
        pltpu.roll(centre, 1, 1),
        pltpu.roll(centre, width - 1, 1),
        centre,
        jnp.where(low, ref[x + 1, BELOW, :], ref[x + 1, ABOVE, :]),
    )


def around_coarse(ref, i, low):
    centre = ref[i + 1, MID, :]
    width = centre.shape[1]
    return (
        ref[i + 1, BELOW, :],
        ref[i + 1, ABOVE, :],
        pltpu.roll(centre, 2, 1),
        pltpu.roll(centre, width - 2, 1),
        centre,
        jnp.where(low, ref[i, MID, :], ref[i + 2, MID, :]),
    )


def around_coarsest(planes, k, low):
    centre = planes[k + 1]
    rows, width = centre.shape
    return (
        pltpu.roll(centre, 1, 0),
        pltpu.roll(centre, rows - 1, 0),
        pltpu.roll(centre, 4, 1),
        pltpu.roll(centre, width - 4, 1),
        centre,
        jnp.where(low, planes[k], planes[k + 2]),
    )


def walls(sides, first, last):
    return sides[:2] + (jnp.where(first, 0.0, sides[2]), jnp.where(last, 0.0, sides[3])) + sides[4:]


def mean_fine(u, w):
    return jnp.where(u == w, u, u * w * MIX)


def mean_any(u, w):
    total = u + w
    return 2.0 * u * w / jnp.where(total > 0, total, 1.0)


def weights(mean, u, sides, top):
    faces = [mean(u, w) for w in sides]
    diagonal = (faces[0] + faces[1]) + (faces[2] + faces[3]) + (faces[4] + faces[5])
    diagonal = diagonal + jnp.where(top, 2.0 * u, 0.0)
    diagonal = jnp.where(diagonal > 0, diagonal, 1.0)
    inverse = 1.0 / diagonal
    return [face * inverse for face in faces], inverse, diagonal


def relax(scaled, share, sides):
    parts = [share[a] * sides[a] for a in range(6)]
    return scaled + ((parts[0] + parts[1]) + (parts[2] + parts[3]) + (parts[4] + parts[5]))


def fine_low(x_parity, colour, width):
    return (lanes((WIN, width)) + (x_parity + colour)) % 2 == 0


def coarse_low(colour, width):
    row = lax.broadcasted_iota(jnp.int32, (WIN, width), 0)
    return (row + lanes((WIN, width)) // 2 + colour) % 2 == 0


def fine_pass(colour, target, other, share, scaled):
    planes, width = share.shape[1], share.shape[3]

    def two(i, _):
        for parity in (0, 1):
            x = 2 * i + parity
            sides = around_fine(other, x, fine_low(parity, colour, width))
            target[x + 1, MID, :] = relax(scaled[x], share[:, x], sides)
        return 0

    lax.fori_loop(0, planes // 2, two, 0, unroll=4)


def coarse_pass(colour, target, other, share, scaled):
    planes, width = share.shape[1], share.shape[3]

    def one(i, _):
        sides = around_coarse(other, i, coarse_low(colour, width))
        target[i + 1, MID, :] = relax(scaled[i], share[:, i], sides)
        return 0

    lax.fori_loop(0, planes, one, 0, unroll=4)


def down_kernel(
    own, before, after,
    *refs,
):
    kept, packed = refs[: KEPT + 1], refs[KEPT + 1]
    state, work = refs[KEPT + 2 : 2 * KEPT], refs[2 * KEPT :]
    share0, share1, scaled0, scaled1, diagonal0, cshare0, cshare1, cscaled0, cscaled1 = state
    m0, m1, v0, v1, cm0, cm1, e0, e1, cdiagonal0, rest, message, done = work
    planes, width = share0.shape[1], share0.shape[3]
    coarse = planes // 4
    held = list(state) + [v1.at[1 : planes + 1, MID, :], e1.at[1 : coarse + 1, MID, :], message]
    copies = [pltpu.make_async_copy(ref, hbm, done.at[k]) for k, (ref, hbm) in enumerate(zip(held, kept))]
    for ref in (m0, m1, v0, v1, cm0, cm1, e0, e1):
        clear_edges(ref)

    def unfold(i, _):
        for slab, ref in enumerate((before, own, after)):
            at = slab * ROWS
            for a, to in enumerate((m0, m1, scaled0, scaled1, v1)):
                tiles = [ref[4 * i + j, a * ROWS : (a + 1) * ROWS, :] for j in range(4)]
                shift = 1 if a in (0, 1, 4) else 0
                for j, tile in enumerate(swap_blocks(tiles)):
                    row = at + ROWS * shift
                    to[4 * i + j + shift, row : row + ROWS, :] = tile
        return 0

    lax.fori_loop(0, planes // 4, unfold, 0)

    lane = lanes((WIN, width))

    def fine_weights(i, _):
        for parity in (0, 1):
            x = 2 * i + parity
            for colour, mine, other, share, scaled in ((0, m0, m1, share0, scaled0), (1, m1, m0, share1, scaled1)):
                low = fine_low(parity, colour, width)
                u = mine[x + 1, MID, :]
                sides = walls(around_fine(other, x, low), lane == 0, lane == width - 1)
                top = jnp.logical_and(jnp.logical_not(low), sides[5] == 0)
                shares, inverse, diagonal = weights(mean_fine, u, sides, top)
                for a in range(6):
                    share[a, x] = shares[a]
                scaled[x] = scaled[x] * inverse
                if colour == 0:
                    diagonal0[x] = diagonal
        return 0

    lax.fori_loop(0, planes // 2, fine_weights, 0)
    for copy in copies[:5]:
        copy.start()

    for _ in range(SWEEPS):
        fine_pass(0, v0, v1, share0, scaled0)
        fine_pass(1, v1, v0, share1, scaled1)
    copies[KEPT - 2].start()

    even = coarse_low(0, width)

    def restrict(i, _):
        fields, mobilities = [], []
        for half in (0, 1):
            total, mass = 0.0, 0.0
            for parity in (0, 1):
                x = 4 * i + 2 * half + parity
                sides = around_fine(v1, x, fine_low(parity, 0, width))
                total = total + diagonal0[x] * (relax(scaled0[x], share0[:, x], sides) - v0[x + 1, MID, :])
                mass = mass + (m0[x + 1, MID, :] + m1[x + 1, MID, :])
            fields.append(0.5 * (total + swap_lanes(total, 1)))
            mobilities.append(0.125 * (mass + swap_lanes(mass, 1)))
        cscaled0[i] = jnp.where(even, fields[0], fields[1])
        cscaled1[i] = jnp.where(even, fields[1], fields[0])
        cm0[i + 1, MID, :] = jnp.where(even, mobilities[0], mobilities[1])
        cm1[i + 1, MID, :] = jnp.where(even, mobilities[1], mobilities[0])
        return 0

    lax.fori_loop(0, planes // 4, restrict, 0)

    def coarse_weights(i, _):
        for colour, mine, other, share, scaled in ((0, cm0, cm1, cshare0, cscaled0), (1, cm1, cm0, cshare1, cscaled1)):
            u = mine[i + 1, MID, :]
            sides = walls(around_coarse(other, i, coarse_low(colour, width)), lane < 2, lane >= width - 2)
            shares, inverse, diagonal = weights(mean_any, u, sides, sides[1] == 0)
            for a in range(6):
                share[a, i] = shares[a]
            scaled[i] = scaled[i] * inverse
            if colour == 0:
                cdiagonal0[i] = diagonal
        e0[i + 1, MID, :] = cscaled0[i]
        return 0

    lax.fori_loop(0, planes // 4, coarse_weights, 0)
    for copy in copies[5 : KEPT - 2]:
        copy.start()

    for sweep in range(SWEEPS):
        if sweep:
            coarse_pass(0, e0, e1, cshare0, cscaled0)
        coarse_pass(1, e1, e0, cshare1, cscaled1)
    copies[KEPT - 1].start()

    here = slice(ROWS, 2 * ROWS)
    part = lanes((ROWS, width)) % 4
    row = lax.broadcasted_iota(jnp.int32, (ROWS, width), 0)
    pick = jnp.logical_and(row % 2 == 0, part == row // 2)
    first = lanes((ROWS, width)) % 2 == 0
    for i in range(coarse):
        message[i] = jnp.where(first, e1[i + 1, 2 * ROWS : 3 * ROWS, :], cscaled0[i, here, :])
    copies[KEPT].start()
    low = coarse_low(0, width)
    for i in range(coarse):
        sides = around_coarse(e1, i, low)
        rest[...] = cdiagonal0[i] * (relax(cscaled0[i], cshare0[:, i], sides) - e0[i + 1, MID, :])
        pair = rest[ROWS : 2 * ROWS, :] + rest[ROWS + 1 : 2 * ROWS + 1, :]
        pair = 0.5 * (pair + swap_lanes(pair, 2))
        packed[0, i : i + 1, :] = jnp.sum(jnp.where(pick, pair, 0.0), axis=0, keepdims=True)
        rest[...] = cm0[i + 1, MID, :] + cm1[i + 1, MID, :]
        pair = rest[ROWS : 2 * ROWS, :] + rest[ROWS + 1 : 2 * ROWS + 1, :]
        pair = 0.125 * (pair + swap_lanes(pair, 2))
        at = planes // 4 + i
        packed[0, at : at + 1, :] = jnp.sum(jnp.where(pick, pair, 0.0), axis=0, keepdims=True)
    tile = packed[0]
    for device in range(1, packed.shape[0]):
        packed[device] = tile
    for copy in copies:
        copy.wait()


def up_kernel(
    columns,
    gathered,
    *refs,
):
    kept, out = refs[: KEPT + 2], refs[KEPT + 2]
    state, work = refs[KEPT + 3 : 2 * KEPT + 1], refs[2 * KEPT + 1 :]
    share0, share1, scaled0, scaled1, diagonal0, cshare0, cshare1, cscaled0, cscaled1 = state
    v0, v1, e0, e1, before, after, bshare, coarsest, spread, done = work
    planes, width = share0.shape[1], share0.shape[3]
    held = list(state) + [v1.at[1 : planes + 1, MID, :], e1.at[1 : planes // 4 + 1, MID, :], before, after]
    copies = [pltpu.make_async_copy(hbm, ref, done.at[k]) for k, (ref, hbm) in enumerate(zip(held, kept))]
    for copy in copies[5 : KEPT - 2] + copies[KEPT - 1 :] + copies[:5] + copies[KEPT - 2 : KEPT - 1]:
        copy.start()
    count = gathered.shape[0]
    rows = planes // 4
    for ref in (v0, v1, e0, e1):
        clear_edges(ref)

    slab = slab_index(columns)
    lane = lanes((rows, width))
    part = lane % 4
    sources, mobilities = [], []
    for w in range(-REACH, REACH + 1):
        near = slab + w
        inside = jnp.logical_and(near >= 0, near < count)
        device = device_of(jnp.clip(near, 0, count - 1), columns)
        keep = jnp.where(inside, 1.0, 0.0)
        for at, into in ((0, sources), (rows, mobilities)):
            tile = gathered[device, at : at + rows, :] * keep
            for z in range(4):
                v = jnp.where(part == z, tile, 0.0)
                v = v + swap_lanes(v, 1)
                into.append(v + swap_lanes(v, 2))

    parity = (lax.broadcasted_iota(jnp.int32, (rows, width), 0) + lane // 4) % 2
    pairs = len(sources) // 2
    zero = jnp.zeros((rows, width), jnp.float32)
    low = (parity == 0, parity == 1)

    def coloured(planes_of):
        first = [jnp.where(low[0], planes_of[2 * k], planes_of[2 * k + 1]) for k in range(pairs)]
        second = [jnp.where(low[0], planes_of[2 * k + 1], planes_of[2 * k]) for k in range(pairs)]
        return [zero] + first + [zero], [zero] + second + [zero]

    source, mobility = coloured(sources), coloured(mobilities)
    row = lax.broadcasted_iota(jnp.int32, (rows, width), 0)
    scaled = ([], [])
    for k in range(pairs):
        for colour in (0, 1):
            sides = around_coarsest(mobility[1 - colour], k, low[colour])
            sides = (jnp.where(row == 0, 0.0, sides[0]), jnp.where(row == rows - 1, 0.0, sides[1])) + sides[2:]
            sides = walls(sides, lane < 4, lane >= width - 4)
            top = jnp.logical_and(jnp.logical_not(low[colour]), sides[5] == 0)
            shares, inverse, _ = weights(mean_any, mobility[colour][k + 1], sides, top)
            for a in range(6):
                bshare[colour, a, k] = shares[a]
            scaled[colour].append(source[colour][k + 1] * inverse)

    fields = [[zero] + scaled[0] + [zero], None]
    for step in range(1, 2 * BOTTOM_SWEEPS):
        colour = step % 2
        new = []
        for k in range(pairs):
            sides = around_coarsest(fields[1 - colour], k, low[colour])
            new.append(relax(scaled[colour][k], [bshare[colour, a, k] for a in range(6)], sides))
        fields[colour] = [zero] + new + [zero]

    start = 4 * REACH - ROWS // 2
    for k in range(WIN // 4):
        a, b = fields[0][start // 2 + k + 1], fields[1][start // 2 + k + 1]
        coarsest[2 * k * rows : (2 * k + 1) * rows, :] = jnp.where(low[0], a, b)
        coarsest[(2 * k + 1) * rows : (2 * k + 2) * rows, :] = jnp.where(low[0], b, a)

    for copy in copies[5 : KEPT - 2] + copies[KEPT - 1 :]:
        copy.wait()
    first = lanes((ROWS, width)) % 2 == 0
    for i in range(rows):
        half = coarsest[pl.ds(i, WIN // 2, stride=rows), :]
        spread[pl.ds(0, WIN // 2, stride=2), :] = half
        spread[pl.ds(1, WIN // 2, stride=2), :] = half
        e1[i + 1, 2 * ROWS : 3 * ROWS, :] = e1[i + 1, 2 * ROWS : 3 * ROWS, :] + spread[ROWS : 2 * ROWS, :]
        for at, ref in ((0, before), (2 * ROWS, after)):
            mixed = ref[i]
            other = swap_lanes(mixed, 1)
            e1[i + 1, ROWS + at : 2 * ROWS + at, :] = jnp.where(first, mixed, other) + spread[at : at + ROWS, :]
            cscaled0[i, at : at + ROWS, :] = jnp.where(first, other, mixed)

    for _ in range(SWEEPS):
        coarse_pass(0, e0, e1, cshare0, cscaled0)
        coarse_pass(1, e1, e0, cshare1, cscaled1)

    even = coarse_low(0, width)

    for copy in copies[:5] + copies[KEPT - 2 : KEPT - 1]:
        copy.wait()

    def correct(i, _):
        a, b = e0[i + 1, MID, :], e1[i + 1, MID, :]
        for half, add in ((0, jnp.where(even, a, b)), (1, jnp.where(even, b, a))):
            for parity in (0, 1):
                x = 4 * i + 2 * half + parity
                v1[x + 1, MID, :] = v1[x + 1, MID, :] + add
        return 0

    lax.fori_loop(0, rows, correct, 0)

    for _ in range(SWEEPS):
        fine_pass(0, v0, v1, share0, scaled0)
        fine_pass(1, v1, v0, share1, scaled1)

    here = slice(2 * ROWS, 3 * ROWS)

    def fold(i, _):
        rest = []
        for parity in range(4):
            x = 4 * i + parity
            sides = around_fine(v1, x, fine_low(parity % 2, 0, width))
            full = diagonal0[x] * (relax(scaled0[x], share0[:, x], sides) - v0[x + 1, MID, :])
            rest.append(full[ROWS : 2 * ROWS])
        for a, tiles in (
            (0, [v0[4 * i + b + 1, here, :] for b in range(4)]),
            (1, [v1[4 * i + b + 1, here, :] for b in range(4)]),
            (2, rest),
        ):
            for j, tile in enumerate(swap_blocks(tiles)):
                out[4 * i + j, a * ROWS : (a + 1) * ROWS, :] = tile
        return 0

    lax.fori_loop(0, rows, fold, 0)


def local_slabs(shape, right_side, phase, pressure_guess):
    across, columns = shape
    count = across * columns
    bx, by, length = right_side.shape
    planes, width = across * bx, columns * by
    f32 = jnp.float32
    order = place_of(across, columns)
    path = sorted(range(count), key=lambda device: order[device])
    up = [(path[k], path[k + 1]) for k in range(count - 1)]
    down = [(b, a) for a, b in up]
    axes = ("gx", "yz")
    params = pltpu.CompilerParams(vmem_limit_bytes=20 * 1024 * 1024)

    def struct(*dims):
        return jax.ShapeDtypeStruct(dims, f32)

    def vmem(*dims):
        return pltpu.VMEM(dims, f32)

    bricks = pl.pallas_call(
        functools.partial(pack_kernel, order),
        in_specs=[pl.BlockSpec(memory_space=pltpu.HBM)] * 3,
        out_shape=struct(count, 5 * ROWS, 128),
        scratch_shapes=[
            vmem(bx, by, length),
            pltpu.VMEM((bx, by, length), phase.dtype),
            vmem(bx, by, length),
            vmem(3, length, 128),
            pltpu.SemaphoreType.DMA((3,)),
        ],
        compiler_params=params,
        name="pack",
    )(*(pltpu.with_memory_space_constraint(x, pltpu.HBM) for x in (right_side, phase, pressure_guess)))
    own = lax.all_to_all(bricks, axes, 0, 0)
    before = lax.ppermute(own, axes, up)
    after = lax.ppermute(own, axes, down)

    coarse = planes // 4
    fine = [vmem(6, planes, WIN, width)] * 2 + [vmem(planes, WIN, width)] * 3
    half = [vmem(6, coarse, WIN, width)] * 2 + [vmem(coarse, WIN, width)] * 2
    kept = fine + half + [struct(planes, WIN, width), struct(coarse, WIN, width)]
    padded = [vmem(planes + 2, WIN + 2 * ROWS, width)] * 2
    cpadded = [vmem(coarse + 2, WIN + 2 * ROWS, width)] * 2
    *state, message, packed = pl.pallas_call(
        down_kernel,
        out_shape=[pltpu.HBM(x.shape, x.dtype) for x in kept + [struct(coarse, ROWS, width)]] + [struct(count, 2 * coarse, width)],
        out_specs=[pl.BlockSpec(memory_space=pltpu.HBM)] * (len(kept) + 1) + [pl.BlockSpec(memory_space=pltpu.VMEM)],
        scratch_shapes=fine + half + padded * 2 + cpadded * 2 + [
            vmem(coarse, WIN, width),
            vmem(WIN, width),
            vmem(coarse, ROWS, width),
            pltpu.SemaphoreType.DMA((len(kept) + 1,)),
        ],
        compiler_params=params,
        name="down",
    )(own, before, after)
    gathered = lax.all_to_all(packed, axes, 0, 0)
    e_before = lax.ppermute(message, axes, up)
    e_after = lax.ppermute(message, axes, down)

    cycle = pl.pallas_call(
        functools.partial(up_kernel, columns),
        out_shape=struct(count, 3 * ROWS, 128),
        in_specs=[pl.BlockSpec(memory_space=pltpu.VMEM)] + [pl.BlockSpec(memory_space=pltpu.HBM)] * (len(kept) + 2),
        scratch_shapes=fine + half + padded + cpadded + [vmem(coarse, ROWS, width)] * 2 + [
            vmem(2, 6, 2 * (2 * REACH + 1), coarse, width),
            vmem(WIN // 2 * coarse, width),
            vmem(WIN, width),
            pltpu.SemaphoreType.DMA((len(kept) + 2,)),
        ],
        compiler_params=params,
        name="up",
    )(gathered, *(pltpu.with_memory_space_constraint(x, pltpu.HBM) for x in (*state, e_before, e_after)))
    back = lax.all_to_all(cycle, axes, 0, 0)
    return pl.pallas_call(
        functools.partial(unpack_kernel, order),
        out_shape=[struct(bx, by, length)] * 2,
        scratch_shapes=[vmem(2, length, 128)],
        compiler_params=params,
        name="unpack",
    )(back)


def solution(mesh):
    spec = P("gx", "yz", None)
    shape = (mesh.shape["gx"], mesh.shape["yz"])

    def cycle(right_side, phase, pressure_guess):
        bx, by, length = right_side.shape
        slabs = (bx, by, shape[1]) == (4, 32, 4) and length == 2 * ROWS * shape[0] * shape[1]
        if slabs and shape[0] == 8:
            return local_slabs(shape, right_side, phase, pressure_guess)
        return local(right_side, phase, pressure_guess)

    return jax.shard_map(cycle, mesh=mesh, in_specs=(spec,) * 3, out_specs=(spec,) * 2, check_vma=False)
```

```python
import functools

import jax
import jax.numpy as jnp
from jax import lax
from jax.experimental import pallas as pl
from jax.experimental.pallas import tpu as pltpu
from jax.sharding import PartitionSpec as P

SWEEPS = 2
BOTTOM_SWEEPS = 4


def with_halo(x, sides, width):
    for axis, dim in sides:
        size, length = (lax.axis_size(axis), x.shape[dim])
        up = [(i, (i + 1) % size) for i in range(size - 1)]
        down = [(j, i) for i, j in up]
        last = lax.slice_in_dim(x, length - width, length, axis=dim)
        first = lax.slice_in_dim(x, 0, width, axis=dim)
        before = lax.ppermute(last, axis, up)
        after = lax.ppermute(first, axis, down)
        x = jnp.concatenate([before, x, after], axis=dim)
    return x


def harmonic(left, right):
    total = left + right
    safe = jnp.where(total > 0, total, 1.0)
    return jnp.where(total > 0, 2.0 * left * right / safe, 0.0)


def coefficients(padded):
    faces_x = harmonic(padded[1:], padded[:-1])
    faces_y = harmonic(padded[:, 1:], padded[:, :-1])
    centre = padded[1:-1, 1:-1]
    faces_z = harmonic(centre[:, :, 1:], centre[:, :, :-1])
    zero_plane = jnp.zeros_like(centre[:, :, :1])
    x_lower = faces_x[:-1, 1:-1]
    x_upper = faces_x[1:, 1:-1]
    y_lower = faces_y[1:-1, :-1]
    y_upper = faces_y[1:-1, 1:]
    z_lower = jnp.concatenate([zero_plane, faces_z], axis=2)
    z_upper = jnp.concatenate([faces_z, 2.0 * centre[:, :, -1:]], axis=2)
    diagonal = x_lower + x_upper + y_lower + y_upper + z_lower + z_upper
    diagonal = jnp.where(diagonal > 0, diagonal, 1.0)
    return (x_lower, x_upper, y_lower, y_upper, z_lower, z_upper, diagonal)


def shrink(coeffs):
    return tuple((item[1:-1, 1:-1] for item in coeffs))


def parity_of(extent, start_x, start_y):
    index_x = lax.broadcasted_iota(jnp.int32, extent, 0) + start_x
    index_y = lax.broadcasted_iota(jnp.int32, extent, 1) + start_y
    index_z = lax.broadcasted_iota(jnp.int32, extent, 2)
    return (index_x + index_y + index_z) % 2


def neighbours(padded, coeffs):
    centre = padded[1:-1, 1:-1]
    zero_plane = jnp.zeros_like(centre[:, :, :1])
    lower_z = jnp.concatenate([zero_plane, centre[:, :, :-1]], axis=2)
    upper_z = jnp.concatenate([centre[:, :, 1:], zero_plane], axis=2)
    beside_all = coeffs[0] * padded[:-2, 1:-1] + coeffs[1] * padded[2:, 1:-1]
    beside_all = beside_all + coeffs[2] * padded[1:-1, :-2] + coeffs[3] * padded[1:-1, 2:]
    beside_all = beside_all + coeffs[4] * lower_z + coeffs[5] * upper_z
    return (beside_all, centre)


def colour_pass(padded, source, coeffs, parity, colour):
    beside_all, centre = neighbours(padded, coeffs)
    updated = (source + beside_all) / coeffs[6]
    return jnp.where(parity == colour, updated, centre)


def residual_of(padded, source, coeffs):
    beside_all, centre = neighbours(padded, coeffs)
    return source - (coeffs[6] * centre - beside_all)


def restrict_sum(field):
    size_x, size_y, size_z = field.shape
    return 0.5 * field.reshape(size_x // 2, 2, size_y // 2, 2, size_z // 2, 2).sum(axis=(1, 3, 5))


def restrict_mean(field):
    size_x, size_y, size_z = field.shape
    return 0.125 * field.reshape(size_x // 2, 2, size_y // 2, 2, size_z // 2, 2).sum(axis=(1, 3, 5))


def inject(field):
    return jnp.repeat(jnp.repeat(jnp.repeat(field, 2, axis=0), 2, axis=1), 2, axis=2)


def rim_one(field):
    return with_halo(field, (("gx", 0), ("yz", 1)), 1)


def rim_two(field):
    return with_halo(field, (("gx", 0), ("yz", 1)), 2)


def offsets(field):
    return (lax.axis_index("gx") * field.shape[0], lax.axis_index("yz") * field.shape[1])


def prepare_plain(mobility):
    start_x, start_y = offsets(mobility)
    return (coefficients(rim_one(mobility)), parity_of(mobility.shape, start_x, start_y))


def prepare(mobility):
    start_x, start_y = offsets(mobility)
    size_x, size_y, size_z = mobility.shape
    region = coefficients(rim_two(mobility))
    loop_parity = parity_of((size_x + 2, size_y + 2, size_z), start_x - 1, start_y - 1)
    operator_set = (
        shrink(region),
        parity_of(mobility.shape, start_x, start_y),
        region,
        loop_parity,
    )
    return operator_set


def smooth_plain(field, source, operator_set, sweeps, rim):
    coeffs = operator_set[0]
    parity = operator_set[1]
    for _ in range(sweeps):
        field = colour_pass(rim(field), source, coeffs, parity, 0)
        field = colour_pass(rim(field), source, coeffs, parity, 1)
    return field


def smooth(field, source, operator_set, sweeps):
    interior, parity, region, loop_parity = operator_set
    source_loop = rim_one(source)
    for _ in range(sweeps):
        loop_field = colour_pass(rim_two(field), source_loop, region, loop_parity, 0)
        field = colour_pass(loop_field, source, interior, parity, 1)
    return field


def local(right_side, phase, pressure_guess):
    mobility = 1.0 + 999.0 * phase.astype(jnp.float32)
    level_zero = prepare(mobility)
    pressure = smooth(pressure_guess, right_side, level_zero, SWEEPS)
    fine_res = residual_of(rim_one(pressure), right_side, level_zero[0])
    source_one = restrict_sum(fine_res)
    mobility_one = restrict_mean(mobility)
    level_one = prepare(mobility_one)
    coarse_one = smooth(jnp.zeros_like(source_one), source_one, level_one, SWEEPS)
    res_one = residual_of(rim_one(coarse_one), source_one, level_one[0])
    source_two = restrict_sum(res_one)
    mobility_two = restrict_mean(mobility_one)
    level_two = prepare_plain(mobility_two)
    coarse_two = smooth_plain(
        jnp.zeros_like(source_two), source_two, level_two, BOTTOM_SWEEPS, rim_one
    )
    coarse_one = smooth(coarse_one + inject(coarse_two), source_one, level_one, SWEEPS)
    pressure = smooth(pressure + inject(coarse_one), right_side, level_zero, SWEEPS)
    residual = residual_of(rim_one(pressure), right_side, level_zero[0])
    return (pressure, residual)


ROWS = 8
WIN = 3 * ROWS
REACH = 3
MIX = 2.0 / 1001.0


def place_of(rows, columns):
    slab = []
    for g in range(rows):
        a = (g // 2) * 2 + ((g % 2) ^ ((g // 2) % 2))
        slab += [a * columns + (j if a % 2 == 0 else columns - 1 - j) for j in range(columns)]
    return slab


def slab_index(columns):
    g, j = lax.axis_index("gx"), lax.axis_index("yz")
    a = (g // 2) * 2 + (g + g // 2) % 2
    return a * columns + jnp.where(a % 2 == 0, j, columns - 1 - j)


def device_of(slab, columns):
    a, b = slab // columns, slab % columns
    g = (a // 2) * 2 + (a + a // 2) % 2
    return g * columns + jnp.where(a % 2 == 0, b, columns - 1 - b)


def lanes(shape):
    return lax.broadcasted_iota(jnp.int32, shape, len(shape) - 1)


def swap_lanes(v, step):
    width = v.shape[-1]
    up, down = pltpu.roll(v, step, 1), pltpu.roll(v, width - step, 1)
    return jnp.where((lanes(v.shape) // step) % 2 == 0, down, up)


def swap_blocks(tiles):
    block = lanes(tiles[0].shape) // 32
    at = [block == b for b in range(3)]

    def choose(four):
        return jnp.where(at[0], four[0], jnp.where(at[1], four[1], jnp.where(at[2], four[2], four[3])))

    turned = [choose([tiles[(b + d) % 4] for b in range(4)]) for d in range(4)]
    turned = [turned[0]] + [pltpu.roll(turned[d], 32 * d, 1) for d in (1, 2, 3)]
    return [choose([turned[(b - a) % 4] for b in range(4)]) for a in range(4)]


def brick_parity(shape):
    lane = lanes(shape)
    return (lane // 32 + lane) % 2


def pack_kernel(order, source_hbm, phase_hbm, guess_hbm, out_ref, source_ref, phase_ref, guess_ref, turned, arrived):
    copies = [
        pltpu.make_async_copy(hbm, ref, arrived.at[a])
        for a, (hbm, ref) in enumerate(((source_hbm, source_ref), (phase_hbm, phase_ref), (guess_hbm, guess_ref)))
    ]
    for copy in copies:
        copy.start()
    for a, ref in enumerate((source_ref, phase_ref, guess_ref)):
        copies[a].wait()
        brick = ref[...].reshape(128, ref.shape[2])
        if a == 1:
            brick = 1.0 + 999.0 * brick.astype(jnp.float32)
        turned[a] = brick.T
    even = brick_parity((ROWS, 128)) == 0
    for device, slab in enumerate(order):
        base = 2 * ROWS * slab
        for a, at in ((1, 0), (0, 2 * ROWS), (2, 3 * ROWS)):
            low = turned[a, pl.ds(base, ROWS, stride=2), :]
            high = turned[a, pl.ds(base + 1, ROWS, stride=2), :]
            if a != 2:
                out_ref[device, at : at + ROWS, :] = jnp.where(even, low, high)
            out_ref[device, at + ROWS : at + 2 * ROWS, :] = jnp.where(even, high, low)


def unpack_kernel(order, in_ref, pressure_ref, residual_ref, turned):
    even = brick_parity((ROWS, 128)) == 0
    for device, slab in enumerate(order):
        base = 2 * ROWS * slab
        p0, p1 = in_ref[device, 0:ROWS, :], in_ref[device, ROWS : 2 * ROWS, :]
        r0 = in_ref[device, 2 * ROWS : 3 * ROWS, :]
        turned[0, pl.ds(base, ROWS, stride=2), :] = jnp.where(even, p0, p1)
        turned[0, pl.ds(base + 1, ROWS, stride=2), :] = jnp.where(even, p1, p0)
        turned[1, pl.ds(base, ROWS, stride=2), :] = jnp.where(even, r0, 0.0)
        turned[1, pl.ds(base + 1, ROWS, stride=2), :] = jnp.where(even, 0.0, r0)
    for a, ref in enumerate((pressure_ref, residual_ref)):
        ref[...] = turned[a].T.reshape(ref.shape)


KEPT = 11
MID = slice(ROWS, ROWS + WIN)
BELOW = slice(ROWS - 1, ROWS + WIN - 1)
ABOVE = slice(ROWS + 1, ROWS + WIN + 1)


def clear_edges(ref):
    planes, _, width = ref.shape
    zero = jnp.zeros((ref.shape[1], width), jnp.float32)
    ref[0] = zero
    ref[planes - 1] = zero

    def one(x, _):
        ref[x, 0:ROWS, :] = zero[:ROWS]
        ref[x, ROWS + WIN :, :] = zero[:ROWS]
        return 0

    lax.fori_loop(1, planes - 1, one, 0)


def around_fine(ref, x, low):
    centre = ref[x + 1, MID, :]
    width = centre.shape[1]
    return (
        ref[x, MID, :],
        ref[x + 2, MID, :],
        pltpu.roll(centre, 1, 1),
        pltpu.roll(centre, width - 1, 1),
        centre,
        jnp.where(low, ref[x + 1, BELOW, :], ref[x + 1, ABOVE, :]),
    )


def around_coarse(ref, i, low):
    centre = ref[i + 1, MID, :]
    width = centre.shape[1]
    return (
        ref[i + 1, BELOW, :],
        ref[i + 1, ABOVE, :],
        pltpu.roll(centre, 2, 1),
        pltpu.roll(centre, width - 2, 1),
        centre,
        jnp.where(low, ref[i, MID, :], ref[i + 2, MID, :]),
    )


def around_coarsest(planes, k, low):
    centre = planes[k + 1]
    rows, width = centre.shape
    return (
        pltpu.roll(centre, 1, 0),
        pltpu.roll(centre, rows - 1, 0),
        pltpu.roll(centre, 4, 1),
        pltpu.roll(centre, width - 4, 1),
        centre,
        jnp.where(low, planes[k], planes[k + 2]),
    )


def walls(sides, first, last):
    return sides[:2] + (jnp.where(first, 0.0, sides[2]), jnp.where(last, 0.0, sides[3])) + sides[4:]


def mean_fine(u, w):
    return jnp.where(u == w, u, (u * MIX) * w)


def mean_any(u, w):
    total = u + w
    return 2.0 * u * w / jnp.where(total > 0, total, 1.0)


def weights(mean, u, sides, top):
    faces = [mean(u, w) for w in sides]
    diagonal = (faces[0] + faces[1]) + (faces[2] + faces[3]) + (faces[4] + faces[5])
    diagonal = diagonal + jnp.where(top, 2.0 * u, 0.0)
    diagonal = jnp.where(diagonal > 0, diagonal, 1.0)
    inverse = 1.0 / diagonal
    return [face * inverse for face in faces], inverse, diagonal


def relax(scaled, share, sides):
    parts = [share[a] * sides[a] for a in range(6)]
    return scaled + ((parts[0] + parts[1]) + (parts[2] + parts[3]) + (parts[4] + parts[5]))


def fine_low(x_parity, colour, width):
    return (lanes((WIN, width)) + (x_parity + colour)) % 2 == 0


def coarse_low(colour, width):
    row = lax.broadcasted_iota(jnp.int32, (WIN, width), 0)
    return (row + lanes((WIN, width)) // 2 + colour) % 2 == 0


def fine_pass(colour, target, other, share, scaled):
    planes, width = share.shape[1], share.shape[3]

    def two(i, _):
        for parity in (0, 1):
            x = 2 * i + parity
            sides = around_fine(other, x, fine_low(parity, colour, width))
            target[x + 1, MID, :] = relax(scaled[x], share[:, x], sides)
        return 0

    lax.fori_loop(0, planes // 2, two, 0, unroll=True)


def coarse_pass(colour, target, other, share, scaled):
    planes, width = share.shape[1], share.shape[3]

    def one(i, _):
        sides = around_coarse(other, i, coarse_low(colour, width))
        target[i + 1, MID, :] = relax(scaled[i], share[:, i], sides)
        return 0

    lax.fori_loop(0, planes, one, 0, unroll=True)


def down_kernel(
    own, before, after,
    *refs,
):
    kept, packed = refs[: KEPT + 1], refs[KEPT + 1]
    state, work = refs[KEPT + 2 : 2 * KEPT], refs[2 * KEPT :]
    share0, share1, scaled0, scaled1, diagonal0, cshare0, cshare1, cscaled0, cscaled1 = state
    m0, m1, v0, v1, cm0, cm1, e0, e1, cdiagonal0, rest, message, done = work
    planes, width = share0.shape[1], share0.shape[3]
    coarse = planes // 4
    held = list(state) + [v1.at[1 : planes + 1, MID, :], e1.at[1 : coarse + 1, MID, :], message]
    copies = [pltpu.make_async_copy(ref, hbm, done.at[k]) for k, (ref, hbm) in enumerate(zip(held, kept))]
    for ref in (m0, m1, v0, v1, cm0, cm1, e0, e1):
        clear_edges(ref)

    def unfold(i, _):
        for slab, ref in enumerate((before, own, after)):
            at = slab * ROWS
            for a, to in enumerate((m0, m1, scaled0, scaled1, v1)):
                tiles = [ref[4 * i + j, a * ROWS : (a + 1) * ROWS, :] for j in range(4)]
                shift = 1 if a in (0, 1, 4) else 0
                for j, tile in enumerate(swap_blocks(tiles)):
                    row = at + ROWS * shift
                    to[4 * i + j + shift, row : row + ROWS, :] = tile
        return 0

    lax.fori_loop(0, planes // 4, unfold, 0, unroll=True)

    lane = lanes((WIN, width))

    def fine_weights(i, _):
        for parity in (0, 1):
            x = 2 * i + parity
            for colour, mine, other, share, scaled in ((0, m0, m1, share0, scaled0), (1, m1, m0, share1, scaled1)):
                low = fine_low(parity, colour, width)
                u = mine[x + 1, MID, :]
                sides = walls(around_fine(other, x, low), lane == 0, lane == width - 1)
                top = jnp.logical_and(jnp.logical_not(low), sides[5] == 0)
                shares, inverse, diagonal = weights(mean_fine, u, sides, top)
                for a in range(6):
                    share[a, x] = shares[a]
                scaled[x] = scaled[x] * inverse
                if colour == 0:
                    diagonal0[x] = diagonal
        return 0

    lax.fori_loop(0, planes // 2, fine_weights, 0, unroll=2)
    for copy in copies[:5]:
        copy.start()

    for _ in range(SWEEPS):
        fine_pass(0, v0, v1, share0, scaled0)
        fine_pass(1, v1, v0, share1, scaled1)
    copies[KEPT - 2].start()

    even = coarse_low(0, width)

    def restrict(i, _):
        fields, mobilities = [], []
        for half in (0, 1):
            total, mass = 0.0, 0.0
            for parity in (0, 1):
                x = 4 * i + 2 * half + parity
                sides = around_fine(v1, x, fine_low(parity, 0, width))
                total = total + diagonal0[x] * (relax(scaled0[x], share0[:, x], sides) - v0[x + 1, MID, :])
                mass = mass + (m0[x + 1, MID, :] + m1[x + 1, MID, :])
            fields.append(0.5 * (total + swap_lanes(total, 1)))
            mobilities.append(0.125 * (mass + swap_lanes(mass, 1)))
        cscaled0[i] = jnp.where(even, fields[0], fields[1])
        cscaled1[i] = jnp.where(even, fields[1], fields[0])
        cm0[i + 1, MID, :] = jnp.where(even, mobilities[0], mobilities[1])
        cm1[i + 1, MID, :] = jnp.where(even, mobilities[1], mobilities[0])
        return 0

    lax.fori_loop(0, planes // 4, restrict, 0, unroll=2)

    def coarse_weights(i, _):
        for colour, mine, other, share, scaled in ((0, cm0, cm1, cshare0, cscaled0), (1, cm1, cm0, cshare1, cscaled1)):
            u = mine[i + 1, MID, :]
            sides = walls(around_coarse(other, i, coarse_low(colour, width)), lane < 2, lane >= width - 2)
            shares, inverse, diagonal = weights(mean_any, u, sides, sides[1] == 0)
            for a in range(6):
                share[a, i] = shares[a]
            scaled[i] = scaled[i] * inverse
            if colour == 0:
                cdiagonal0[i] = diagonal
        e0[i + 1, MID, :] = cscaled0[i]
        return 0

    lax.fori_loop(0, planes // 4, coarse_weights, 0, unroll=True)
    for copy in copies[5 : KEPT - 2]:
        copy.start()

    for sweep in range(SWEEPS):
        if sweep:
            coarse_pass(0, e0, e1, cshare0, cscaled0)
        coarse_pass(1, e1, e0, cshare1, cscaled1)
    copies[KEPT - 1].start()

    here = slice(ROWS, 2 * ROWS)
    part = lanes((ROWS, width)) % 4
    row = lax.broadcasted_iota(jnp.int32, (ROWS, width), 0)
    pick = jnp.logical_and(row % 2 == 0, part == row // 2)
    first = lanes((ROWS, width)) % 2 == 0
    for i in range(coarse):
        message[i] = jnp.where(first, e1[i + 1, 2 * ROWS : 3 * ROWS, :], cscaled0[i, here, :])
    copies[KEPT].start()
    low = coarse_low(0, width)
    for i in range(coarse):
        sides = around_coarse(e1, i, low)
        rest[...] = cdiagonal0[i] * (relax(cscaled0[i], cshare0[:, i], sides) - e0[i + 1, MID, :])
        pair = rest[ROWS : 2 * ROWS, :] + rest[ROWS + 1 : 2 * ROWS + 1, :]
        pair = 0.5 * (pair + swap_lanes(pair, 2))
        packed[0, i : i + 1, :] = jnp.sum(jnp.where(pick, pair, 0.0), axis=0, keepdims=True)
        rest[...] = cm0[i + 1, MID, :] + cm1[i + 1, MID, :]
        pair = rest[ROWS : 2 * ROWS, :] + rest[ROWS + 1 : 2 * ROWS + 1, :]
        pair = 0.125 * (pair + swap_lanes(pair, 2))
        at = planes // 4 + i
        packed[0, at : at + 1, :] = jnp.sum(jnp.where(pick, pair, 0.0), axis=0, keepdims=True)
    tile = packed[0]
    for device in range(1, packed.shape[0]):
        packed[device] = tile
    for copy in copies:
        copy.wait()


def up_kernel(
    columns,
    gathered,
    *refs,
):
    kept, out = refs[: KEPT + 2], refs[KEPT + 2]
    state, work = refs[KEPT + 3 : 2 * KEPT + 1], refs[2 * KEPT + 1 :]
    share0, share1, scaled0, scaled1, diagonal0, cshare0, cshare1, cscaled0, cscaled1 = state
    v0, v1, e0, e1, before, after, bshare, coarsest, spread, done = work
    planes, width = share0.shape[1], share0.shape[3]
    held = list(state) + [v1.at[1 : planes + 1, MID, :], e1.at[1 : planes // 4 + 1, MID, :], before, after]
    copies = [pltpu.make_async_copy(hbm, ref, done.at[k]) for k, (ref, hbm) in enumerate(zip(held, kept))]
    for copy in copies[5 : KEPT - 2] + copies[KEPT - 1 :] + copies[:5] + copies[KEPT - 2 : KEPT - 1]:
        copy.start()
    count = gathered.shape[0]
    rows = planes // 4
    for ref in (v0, v1, e0, e1):
        clear_edges(ref)

    slab = slab_index(columns)
    lane = lanes((rows, width))
    part = lane % 4
    sources, mobilities = [], []
    for w in range(-REACH, REACH + 1):
        near = slab + w
        inside = jnp.logical_and(near >= 0, near < count)
        device = device_of(jnp.clip(near, 0, count - 1), columns)
        keep = jnp.where(inside, 1.0, 0.0)
        for at, into in ((0, sources), (rows, mobilities)):
            tile = gathered[device, at : at + rows, :] * keep
            for z in range(4):
                v = jnp.where(part == z, tile, 0.0)
                v = v + swap_lanes(v, 1)
                into.append(v + swap_lanes(v, 2))

    parity = (lax.broadcasted_iota(jnp.int32, (rows, width), 0) + lane // 4) % 2
    pairs = len(sources) // 2
    zero = jnp.zeros((rows, width), jnp.float32)
    low = (parity == 0, parity == 1)

    def coloured(planes_of):
        first = [jnp.where(low[0], planes_of[2 * k], planes_of[2 * k + 1]) for k in range(pairs)]
        second = [jnp.where(low[0], planes_of[2 * k + 1], planes_of[2 * k]) for k in range(pairs)]
        return [zero] + first + [zero], [zero] + second + [zero]

    source, mobility = coloured(sources), coloured(mobilities)
    row = lax.broadcasted_iota(jnp.int32, (rows, width), 0)
    scaled = ([], [])
    for k in range(pairs):
        for colour in (0, 1):
            sides = around_coarsest(mobility[1 - colour], k, low[colour])
            sides = (jnp.where(row == 0, 0.0, sides[0]), jnp.where(row == rows - 1, 0.0, sides[1])) + sides[2:]
            sides = walls(sides, lane < 4, lane >= width - 4)
            top = jnp.logical_and(jnp.logical_not(low[colour]), sides[5] == 0)
            shares, inverse, _ = weights(mean_any, mobility[colour][k + 1], sides, top)
            for a in range(6):
                bshare[colour, a, k] = shares[a]
            scaled[colour].append(source[colour][k + 1] * inverse)

    fields = [[zero] + scaled[0] + [zero], None]
    for step in range(1, 2 * BOTTOM_SWEEPS):
        colour = step % 2
        new = []
        for k in range(pairs):
            sides = around_coarsest(fields[1 - colour], k, low[colour])
            new.append(relax(scaled[colour][k], [bshare[colour, a, k] for a in range(6)], sides))
        fields[colour] = [zero] + new + [zero]

    start = 4 * REACH - ROWS // 2
    for k in range(WIN // 4):
        a, b = fields[0][start // 2 + k + 1], fields[1][start // 2 + k + 1]
        coarsest[2 * k * rows : (2 * k + 1) * rows, :] = jnp.where(low[0], a, b)
        coarsest[(2 * k + 1) * rows : (2 * k + 2) * rows, :] = jnp.where(low[0], b, a)

    for copy in copies[5 : KEPT - 2] + copies[KEPT - 1 :]:
        copy.wait()
    first = lanes((ROWS, width)) % 2 == 0
    for i in range(rows):
        half = coarsest[pl.ds(i, WIN // 2, stride=rows), :]
        spread[pl.ds(0, WIN // 2, stride=2), :] = half
        spread[pl.ds(1, WIN // 2, stride=2), :] = half
        e1[i + 1, 2 * ROWS : 3 * ROWS, :] = e1[i + 1, 2 * ROWS : 3 * ROWS, :] + spread[ROWS : 2 * ROWS, :]
        for at, ref in ((0, before), (2 * ROWS, after)):
            mixed = ref[i]
            other = swap_lanes(mixed, 1)
            e1[i + 1, ROWS + at : 2 * ROWS + at, :] = jnp.where(first, mixed, other) + spread[at : at + ROWS, :]
            cscaled0[i, at : at + ROWS, :] = jnp.where(first, other, mixed)

    for _ in range(SWEEPS):
        coarse_pass(0, e0, e1, cshare0, cscaled0)
        coarse_pass(1, e1, e0, cshare1, cscaled1)

    even = coarse_low(0, width)

    for copy in copies[:5] + copies[KEPT - 2 : KEPT - 1]:
        copy.wait()

    def correct(i, _):
        a, b = e0[i + 1, MID, :], e1[i + 1, MID, :]
        for half, add in ((0, jnp.where(even, a, b)), (1, jnp.where(even, b, a))):
            for parity in (0, 1):
                x = 4 * i + 2 * half + parity
                v1[x + 1, MID, :] = v1[x + 1, MID, :] + add
        return 0

    lax.fori_loop(0, rows, correct, 0)

    for _ in range(SWEEPS):
        fine_pass(0, v0, v1, share0, scaled0)
        fine_pass(1, v1, v0, share1, scaled1)

    here = slice(2 * ROWS, 3 * ROWS)

    def fold(i, _):
        rest = []
        for parity in range(4):
            x = 4 * i + parity
            sides = around_fine(v1, x, fine_low(parity % 2, 0, width))
            full = diagonal0[x] * (relax(scaled0[x], share0[:, x], sides) - v0[x + 1, MID, :])
            rest.append(full[ROWS : 2 * ROWS])
        for a, tiles in (
            (0, [v0[4 * i + b + 1, here, :] for b in range(4)]),
            (1, [v1[4 * i + b + 1, here, :] for b in range(4)]),
            (2, rest),
        ):
            for j, tile in enumerate(swap_blocks(tiles)):
                out[4 * i + j, a * ROWS : (a + 1) * ROWS, :] = tile
        return 0

    lax.fori_loop(0, rows, fold, 0, unroll=True)


def local_slabs(shape, right_side, phase, pressure_guess):
    across, columns = shape
    count = across * columns
    bx, by, length = right_side.shape
    planes, width = across * bx, columns * by
    f32 = jnp.float32
    order = place_of(across, columns)
    path = sorted(range(count), key=lambda device: order[device])
    up = [(path[k], path[k + 1]) for k in range(count - 1)]
    down = [(b, a) for a, b in up]
    axes = ("gx", "yz")
    params = pltpu.CompilerParams(vmem_limit_bytes=20 * 1024 * 1024)

    def struct(*dims):
        return jax.ShapeDtypeStruct(dims, f32)

    def vmem(*dims):
        return pltpu.VMEM(dims, f32)

    bricks = pl.pallas_call(
        functools.partial(pack_kernel, order),
        in_specs=[pl.BlockSpec(memory_space=pltpu.HBM)] * 3,
        out_shape=struct(count, 5 * ROWS, 128),
        scratch_shapes=[
            vmem(bx, by, length),
            pltpu.VMEM((bx, by, length), phase.dtype),
            vmem(bx, by, length),
            vmem(3, length, 128),
            pltpu.SemaphoreType.DMA((3,)),
        ],
        compiler_params=params,
        name="pack",
    )(*(pltpu.with_memory_space_constraint(x, pltpu.HBM) for x in (right_side, phase, pressure_guess)))
    own = lax.all_to_all(bricks, axes, 0, 0)
    before = lax.ppermute(own, axes, up)
    after = lax.ppermute(own, axes, down)

    coarse = planes // 4
    fine = [vmem(6, planes, WIN, width)] * 2 + [vmem(planes, WIN, width)] * 3
    half = [vmem(6, coarse, WIN, width)] * 2 + [vmem(coarse, WIN, width)] * 2
    kept = fine + half + [struct(planes, WIN, width), struct(coarse, WIN, width)]
    padded = [vmem(planes + 2, WIN + 2 * ROWS, width)] * 2
    cpadded = [vmem(coarse + 2, WIN + 2 * ROWS, width)] * 2
    *state, message, packed = pl.pallas_call(
        down_kernel,
        out_shape=[pltpu.HBM(x.shape, x.dtype) for x in kept + [struct(coarse, ROWS, width)]] + [struct(count, 2 * coarse, width)],
        out_specs=[pl.BlockSpec(memory_space=pltpu.HBM)] * (len(kept) + 1) + [pl.BlockSpec(memory_space=pltpu.VMEM)],
        scratch_shapes=fine + half + padded * 2 + cpadded * 2 + [
            vmem(coarse, WIN, width),
            vmem(WIN, width),
            vmem(coarse, ROWS, width),
            pltpu.SemaphoreType.DMA((len(kept) + 1,)),
        ],
        compiler_params=params,
        name="down",
    )(own, before, after)
    gathered = lax.all_to_all(packed, axes, 0, 0)
    e_before = lax.ppermute(message, axes, up)
    e_after = lax.ppermute(message, axes, down)

    cycle = pl.pallas_call(
        functools.partial(up_kernel, columns),
        out_shape=struct(count, 3 * ROWS, 128),
        in_specs=[pl.BlockSpec(memory_space=pltpu.VMEM)] + [pl.BlockSpec(memory_space=pltpu.HBM)] * (len(kept) + 2),
        scratch_shapes=fine + half + padded + cpadded + [vmem(coarse, ROWS, width)] * 2 + [
            vmem(2, 6, 2 * (2 * REACH + 1), coarse, width),
            vmem(WIN // 2 * coarse, width),
            vmem(WIN, width),
            pltpu.SemaphoreType.DMA((len(kept) + 2,)),
        ],
        compiler_params=params,
        name="up",
    )(gathered, *(pltpu.with_memory_space_constraint(x, pltpu.HBM) for x in (*state, e_before, e_after)))
    back = lax.all_to_all(cycle, axes, 0, 0)
    return pl.pallas_call(
        functools.partial(unpack_kernel, order),
        out_shape=[struct(bx, by, length)] * 2,
        scratch_shapes=[vmem(2, length, 128)],
        compiler_params=params,
        name="unpack",
    )(back)


def solution(mesh):
    spec = P("gx", "yz", None)
    shape = (mesh.shape["gx"], mesh.shape["yz"])

    def cycle(right_side, phase, pressure_guess):
        bx, by, length = right_side.shape
        slabs = (bx, by, shape[1]) == (4, 32, 4) and length == 2 * ROWS * shape[0] * shape[1]
        if slabs and shape[0] == 8:
            return local_slabs(shape, right_side, phase, pressure_guess)
        return local(right_side, phase, pressure_guess)

    return jax.shard_map(cycle, mesh=mesh, in_specs=(spec,) * 3, out_specs=(spec,) * 2, check_vma=False)
```

```python
import functools

import jax
import jax.numpy as jnp
from jax import lax
from jax.experimental import pallas as pl
from jax.experimental.pallas import tpu as pltpu
from jax.sharding import PartitionSpec as P

SWEEPS = 2
BOTTOM_SWEEPS = 4


def with_halo(x, sides, width):
    for axis, dim in sides:
        size, length = (lax.axis_size(axis), x.shape[dim])
        up = [(i, (i + 1) % size) for i in range(size - 1)]
        down = [(j, i) for i, j in up]
        last = lax.slice_in_dim(x, length - width, length, axis=dim)
        first = lax.slice_in_dim(x, 0, width, axis=dim)
        before = lax.ppermute(last, axis, up)
        after = lax.ppermute(first, axis, down)
        x = jnp.concatenate([before, x, after], axis=dim)
    return x


def harmonic(left, right):
    total = left + right
    safe = jnp.where(total > 0, total, 1.0)
    return jnp.where(total > 0, 2.0 * left * right / safe, 0.0)


def coefficients(padded):
    faces_x = harmonic(padded[1:], padded[:-1])
    faces_y = harmonic(padded[:, 1:], padded[:, :-1])
    centre = padded[1:-1, 1:-1]
    faces_z = harmonic(centre[:, :, 1:], centre[:, :, :-1])
    zero_plane = jnp.zeros_like(centre[:, :, :1])
    x_lower = faces_x[:-1, 1:-1]
    x_upper = faces_x[1:, 1:-1]
    y_lower = faces_y[1:-1, :-1]
    y_upper = faces_y[1:-1, 1:]
    z_lower = jnp.concatenate([zero_plane, faces_z], axis=2)
    z_upper = jnp.concatenate([faces_z, 2.0 * centre[:, :, -1:]], axis=2)
    diagonal = x_lower + x_upper + y_lower + y_upper + z_lower + z_upper
    diagonal = jnp.where(diagonal > 0, diagonal, 1.0)
    return (x_lower, x_upper, y_lower, y_upper, z_lower, z_upper, diagonal)


def shrink(coeffs):
    return tuple((item[1:-1, 1:-1] for item in coeffs))


def parity_of(extent, start_x, start_y):
    index_x = lax.broadcasted_iota(jnp.int32, extent, 0) + start_x
    index_y = lax.broadcasted_iota(jnp.int32, extent, 1) + start_y
    index_z = lax.broadcasted_iota(jnp.int32, extent, 2)
    return (index_x + index_y + index_z) % 2


def neighbours(padded, coeffs):
    centre = padded[1:-1, 1:-1]
    zero_plane = jnp.zeros_like(centre[:, :, :1])
    lower_z = jnp.concatenate([zero_plane, centre[:, :, :-1]], axis=2)
    upper_z = jnp.concatenate([centre[:, :, 1:], zero_plane], axis=2)
    beside_all = coeffs[0] * padded[:-2, 1:-1] + coeffs[1] * padded[2:, 1:-1]
    beside_all = beside_all + coeffs[2] * padded[1:-1, :-2] + coeffs[3] * padded[1:-1, 2:]
    beside_all = beside_all + coeffs[4] * lower_z + coeffs[5] * upper_z
    return (beside_all, centre)


def colour_pass(padded, source, coeffs, parity, colour):
    beside_all, centre = neighbours(padded, coeffs)
    updated = (source + beside_all) / coeffs[6]
    return jnp.where(parity == colour, updated, centre)


def residual_of(padded, source, coeffs):
    beside_all, centre = neighbours(padded, coeffs)
    return source - (coeffs[6] * centre - beside_all)


def restrict_sum(field):
    size_x, size_y, size_z = field.shape
    return 0.5 * field.reshape(size_x // 2, 2, size_y // 2, 2, size_z // 2, 2).sum(axis=(1, 3, 5))


def restrict_mean(field):
    size_x, size_y, size_z = field.shape
    return 0.125 * field.reshape(size_x // 2, 2, size_y // 2, 2, size_z // 2, 2).sum(axis=(1, 3, 5))


def inject(field):
    return jnp.repeat(jnp.repeat(jnp.repeat(field, 2, axis=0), 2, axis=1), 2, axis=2)


def rim_one(field):
    return with_halo(field, (("gx", 0), ("yz", 1)), 1)


def rim_two(field):
    return with_halo(field, (("gx", 0), ("yz", 1)), 2)


def offsets(field):
    return (lax.axis_index("gx") * field.shape[0], lax.axis_index("yz") * field.shape[1])


def prepare_plain(mobility):
    start_x, start_y = offsets(mobility)
    return (coefficients(rim_one(mobility)), parity_of(mobility.shape, start_x, start_y))


def prepare(mobility):
    start_x, start_y = offsets(mobility)
    size_x, size_y, size_z = mobility.shape
    region = coefficients(rim_two(mobility))
    loop_parity = parity_of((size_x + 2, size_y + 2, size_z), start_x - 1, start_y - 1)
    operator_set = (
        shrink(region),
        parity_of(mobility.shape, start_x, start_y),
        region,
        loop_parity,
    )
    return operator_set


def smooth_plain(field, source, operator_set, sweeps, rim):
    coeffs = operator_set[0]
    parity = operator_set[1]
    for _ in range(sweeps):
        field = colour_pass(rim(field), source, coeffs, parity, 0)
        field = colour_pass(rim(field), source, coeffs, parity, 1)
    return field


def smooth(field, source, operator_set, sweeps):
    interior, parity, region, loop_parity = operator_set
    source_loop = rim_one(source)
    for _ in range(sweeps):
        loop_field = colour_pass(rim_two(field), source_loop, region, loop_parity, 0)
        field = colour_pass(loop_field, source, interior, parity, 1)
    return field


def local(right_side, phase, pressure_guess):
    mobility = 1.0 + 999.0 * phase.astype(jnp.float32)
    level_zero = prepare(mobility)
    pressure = smooth(pressure_guess, right_side, level_zero, SWEEPS)
    fine_res = residual_of(rim_one(pressure), right_side, level_zero[0])
    source_one = restrict_sum(fine_res)
    mobility_one = restrict_mean(mobility)
    level_one = prepare(mobility_one)
    coarse_one = smooth(jnp.zeros_like(source_one), source_one, level_one, SWEEPS)
    res_one = residual_of(rim_one(coarse_one), source_one, level_one[0])
    source_two = restrict_sum(res_one)
    mobility_two = restrict_mean(mobility_one)
    level_two = prepare_plain(mobility_two)
    coarse_two = smooth_plain(
        jnp.zeros_like(source_two), source_two, level_two, BOTTOM_SWEEPS, rim_one
    )
    coarse_one = smooth(coarse_one + inject(coarse_two), source_one, level_one, SWEEPS)
    pressure = smooth(pressure + inject(coarse_one), right_side, level_zero, SWEEPS)
    residual = residual_of(rim_one(pressure), right_side, level_zero[0])
    return (pressure, residual)


ROWS = 8
WIN = 3 * ROWS
REACH = 3
MIX = 2.0 / 1001.0


def place_of(rows, columns):
    slab = []
    for g in range(rows):
        a = (g // 2) * 2 + ((g % 2) ^ ((g // 2) % 2))
        slab += [a * columns + (j if a % 2 == 0 else columns - 1 - j) for j in range(columns)]
    return slab


def slab_index(columns):
    g, j = lax.axis_index("gx"), lax.axis_index("yz")
    a = (g // 2) * 2 + (g + g // 2) % 2
    return a * columns + jnp.where(a % 2 == 0, j, columns - 1 - j)


def device_of(slab, columns):
    a, b = slab // columns, slab % columns
    g = (a // 2) * 2 + (a + a // 2) % 2
    return g * columns + jnp.where(a % 2 == 0, b, columns - 1 - b)


def lanes(shape):
    return lax.broadcasted_iota(jnp.int32, shape, len(shape) - 1)


def swap_lanes(v, step):
    width = v.shape[-1]
    up, down = pltpu.roll(v, step, 1), pltpu.roll(v, width - step, 1)
    return jnp.where((lanes(v.shape) // step) % 2 == 0, down, up)


def swap_blocks(tiles):
    block = lanes(tiles[0].shape) // 32
    at = [block == b for b in range(3)]

    def choose(four):
        return jnp.where(at[0], four[0], jnp.where(at[1], four[1], jnp.where(at[2], four[2], four[3])))

    turned = [choose([tiles[(b + d) % 4] for b in range(4)]) for d in range(4)]
    turned = [turned[0]] + [pltpu.roll(turned[d], 32 * d, 1) for d in (1, 2, 3)]
    return [choose([turned[(b - a) % 4] for b in range(4)]) for a in range(4)]


def brick_parity(shape):
    lane = lanes(shape)
    return (lane // 32 + lane) % 2


def pack_kernel(order, source_hbm, phase_hbm, guess_hbm, out_ref, source_ref, phase_ref, guess_ref, turned, arrived):
    copies = [
        pltpu.make_async_copy(hbm, ref, arrived.at[a])
        for a, (hbm, ref) in enumerate(((source_hbm, source_ref), (phase_hbm, phase_ref), (guess_hbm, guess_ref)))
    ]
    for copy in copies:
        copy.start()
    for a, ref in enumerate((source_ref, phase_ref, guess_ref)):
        copies[a].wait()
        brick = ref[...].reshape(128, ref.shape[2])
        if a == 1:
            brick = 1.0 + 999.0 * brick.astype(jnp.float32)
        turned[a] = brick.T
    even = brick_parity((ROWS, 128)) == 0
    for device, slab in enumerate(order):
        base = 2 * ROWS * slab
        for a, at in ((1, 0), (0, 2 * ROWS), (2, 3 * ROWS)):
            low = turned[a, pl.ds(base, ROWS, stride=2), :]
            high = turned[a, pl.ds(base + 1, ROWS, stride=2), :]
            if a != 2:
                out_ref[device, at : at + ROWS, :] = jnp.where(even, low, high)
            out_ref[device, at + ROWS : at + 2 * ROWS, :] = jnp.where(even, high, low)


def unpack_kernel(order, in_ref, pressure_ref, residual_ref, turned):
    even = brick_parity((ROWS, 128)) == 0
    for device, slab in enumerate(order):
        base = 2 * ROWS * slab
        p0, p1 = in_ref[device, 0:ROWS, :], in_ref[device, ROWS : 2 * ROWS, :]
        r0 = in_ref[device, 2 * ROWS : 3 * ROWS, :]
        turned[0, pl.ds(base, ROWS, stride=2), :] = jnp.where(even, p0, p1)
        turned[0, pl.ds(base + 1, ROWS, stride=2), :] = jnp.where(even, p1, p0)
        turned[1, pl.ds(base, ROWS, stride=2), :] = jnp.where(even, r0, 0.0)
        turned[1, pl.ds(base + 1, ROWS, stride=2), :] = jnp.where(even, 0.0, r0)
    for a, ref in enumerate((pressure_ref, residual_ref)):
        ref[...] = turned[a].T.reshape(ref.shape)


KEPT = 11
ALL = (0, WIN)
INNER = (ROWS // 2, WIN - ROWS // 2)
OWN = (ROWS, 2 * ROWS)
MID = slice(ROWS, ROWS + WIN)


def shifted(rows, by):
    return slice(ROWS + rows[0] + by, ROWS + rows[1] + by)


def clear_edges(ref):
    planes, _, width = ref.shape
    zero = jnp.zeros((ref.shape[1], width), jnp.float32)
    ref[0] = zero
    ref[planes - 1] = zero

    def one(x, _):
        ref[x, 0:ROWS, :] = zero[:ROWS]
        ref[x, ROWS + WIN :, :] = zero[:ROWS]
        return 0

    lax.fori_loop(1, planes - 1, one, 0)


def around_fine(ref, x, low, rows=ALL):
    here = shifted(rows, 0)
    centre = ref[x + 1, here, :]
    width = centre.shape[1]
    return (
        ref[x, here, :],
        ref[x + 2, here, :],
        pltpu.roll(centre, 1, 1),
        pltpu.roll(centre, width - 1, 1),
        centre,
        jnp.where(low, ref[x + 1, shifted(rows, -1), :], ref[x + 1, shifted(rows, 1), :]),
    )


def around_coarse(ref, i, low, rows=ALL):
    here = shifted(rows, 0)
    centre = ref[i + 1, here, :]
    width = centre.shape[1]
    return (
        ref[i + 1, shifted(rows, -1), :],
        ref[i + 1, shifted(rows, 1), :],
        pltpu.roll(centre, 2, 1),
        pltpu.roll(centre, width - 2, 1),
        centre,
        jnp.where(low, ref[i, here, :], ref[i + 2, here, :]),
    )


def around_coarsest(planes, k, low):
    centre = planes[k + 1]
    rows, width = centre.shape
    return (
        pltpu.roll(centre, 1, 0),
        pltpu.roll(centre, rows - 1, 0),
        pltpu.roll(centre, 4, 1),
        pltpu.roll(centre, width - 4, 1),
        centre,
        jnp.where(low, planes[k], planes[k + 2]),
    )


def walls(sides, first, last):
    return sides[:2] + (jnp.where(first, 0.0, sides[2]), jnp.where(last, 0.0, sides[3])) + sides[4:]


def mean_fine(u, w):
    return jnp.where(u == w, u, (u * MIX) * w)


def mean_any(u, w):
    total = u + w
    return 2.0 * u * w / jnp.where(total > 0, total, 1.0)


def weights(mean, u, sides, top):
    faces = [mean(u, w) for w in sides]
    diagonal = (faces[0] + faces[1]) + (faces[2] + faces[3]) + (faces[4] + faces[5])
    diagonal = diagonal + jnp.where(top, 2.0 * u, 0.0)
    diagonal = jnp.where(diagonal > 0, diagonal, 1.0)
    inverse = 1.0 / diagonal
    return [face * inverse for face in faces], inverse, diagonal


def relax(scaled, share, sides):
    parts = [share[a] * sides[a] for a in range(6)]
    return scaled + ((parts[0] + parts[1]) + (parts[2] + parts[3]) + (parts[4] + parts[5]))


def fine_low(x_parity, colour, width, rows=ALL):
    return (lanes((rows[1] - rows[0], width)) + (x_parity + colour)) % 2 == 0


def coarse_low(colour, width, rows=ALL):
    shape = (rows[1] - rows[0], width)
    row = lax.broadcasted_iota(jnp.int32, shape, 0) + rows[0]
    return (row + lanes(shape) // 2 + colour) % 2 == 0


def fine_pass(colour, target, other, share, scaled, rows=ALL):
    planes, width = share.shape[1], share.shape[3]
    part = slice(*rows)

    def two(i, _):
        for parity in (0, 1):
            x = 2 * i + parity
            sides = around_fine(other, x, fine_low(parity, colour, width, rows), rows)
            target[x + 1, shifted(rows, 0), :] = relax(scaled[x, part, :], share[:, x, part, :], sides)
        return 0

    lax.fori_loop(0, planes // 2, two, 0, unroll=True)


def coarse_pass(colour, target, other, share, scaled, rows=ALL):
    planes, width = share.shape[1], share.shape[3]
    part = slice(*rows)

    def one(i, _):
        sides = around_coarse(other, i, coarse_low(colour, width, rows), rows)
        target[i + 1, shifted(rows, 0), :] = relax(scaled[i, part, :], share[:, i, part, :], sides)
        return 0

    lax.fori_loop(0, planes, one, 0, unroll=True)


def neighbour_rows(columns):
    near = jnp.where(slab_index(columns) % 2 == 0, 2 * ROWS, 0)
    return pl.multiple_of(near, ROWS), pl.multiple_of(2 * ROWS - near, ROWS)


def unfold_slabs(places, arrays, planes):
    def unfold(i, _):
        for ref, start, at in places:
            for first, store in arrays:
                tiles = [ref[4 * i + j, start + first : start + first + ROWS, :] for j in range(4)]
                for j, tile in enumerate(swap_blocks(tiles)):
                    store(4 * i + j, at, tile)
        return 0

    lax.fori_loop(0, planes // 4, unfold, 0, unroll=True)


def padded_store(ref):
    def store(x, at, tile):
        ref[x + 1, pl.ds(at + ROWS, ROWS), :] = tile

    return store


def scaled_store(ref, factor):
    def store(x, at, tile):
        rows = pl.ds(at, ROWS)
        ref[x, rows, :] = tile * factor[x, rows, :]

    return store


def pair_sum(ref):
    return ref[ROWS : 2 * ROWS, :] + ref[ROWS + 1 : 2 * ROWS + 1, :]


def picked(width):
    row = lax.broadcasted_iota(jnp.int32, (ROWS, width), 0)
    return jnp.logical_and(row % 2 == 0, lanes((ROWS, width)) % 4 == row // 2)


def weights_kernel(columns, own, near, far, *refs):
    share0, share1, inverse0, inverse1, diagonal0, cshare0, cshare1, cinverse0, cinverse1, cdiagonal0, packed = refs[:11]
    kept, (m0, m1, cm0, cm1, rest, done) = refs[11:16], refs[16:]
    held = (share0, share1, diagonal0, cshare0, cshare1)
    copies = [pltpu.make_async_copy(ref, hbm, done.at[k]) for k, (ref, hbm) in enumerate(zip(held, kept))]
    planes, width = share0.shape[1], share0.shape[3]
    for ref in (m0, m1, cm0, cm1):
        clear_edges(ref)
    near_at, far_at = neighbour_rows(columns)
    places = ((own, 0, ROWS), (near, 0, near_at), (far, 0, far_at))
    unfold_slabs(places, ((0, padded_store(m0)), (ROWS, padded_store(m1))), planes)

    lane = lanes((WIN, width))

    def fine_weights(i, _):
        for parity in (0, 1):
            x = 2 * i + parity
            for colour, mine, other, share, factor in ((0, m0, m1, share0, inverse0), (1, m1, m0, share1, inverse1)):
                low = fine_low(parity, colour, width)
                u = mine[x + 1, MID, :]
                sides = walls(around_fine(other, x, low), lane == 0, lane == width - 1)
                top = jnp.logical_and(jnp.logical_not(low), sides[5] == 0)
                shares, inverse, diagonal = weights(mean_fine, u, sides, top)
                for a in range(6):
                    share[a, x] = shares[a]
                factor[x] = inverse
                if colour == 0:
                    diagonal0[x] = diagonal
        return 0

    lax.fori_loop(0, planes // 2, fine_weights, 0, unroll=2)
    for copy in copies[:3]:
        copy.start()

    even = coarse_low(0, width)

    def restrict(i, _):
        mobilities = []
        for half in (0, 1):
            x = 4 * i + 2 * half
            mass = (m0[x + 1, MID, :] + m1[x + 1, MID, :]) + (m0[x + 2, MID, :] + m1[x + 2, MID, :])
            mobilities.append(0.125 * (mass + swap_lanes(mass, 1)))
        cm0[i + 1, MID, :] = jnp.where(even, mobilities[0], mobilities[1])
        cm1[i + 1, MID, :] = jnp.where(even, mobilities[1], mobilities[0])
        return 0

    lax.fori_loop(0, planes // 4, restrict, 0, unroll=2)

    def coarse_weights(i, _):
        for colour, mine, other, share, factor in ((0, cm0, cm1, cshare0, cinverse0), (1, cm1, cm0, cshare1, cinverse1)):
            u = mine[i + 1, MID, :]
            sides = walls(around_coarse(other, i, coarse_low(colour, width)), lane < 2, lane >= width - 2)
            shares, inverse, diagonal = weights(mean_any, u, sides, sides[1] == 0)
            for a in range(6):
                share[a, i] = shares[a]
            factor[i] = inverse
            if colour == 0:
                cdiagonal0[i] = diagonal
        return 0

    lax.fori_loop(0, planes // 4, coarse_weights, 0, unroll=True)
    for copy in copies[3:]:
        copy.start()

    pick = picked(width)
    for i in range(planes // 4):
        rest[...] = cm0[i + 1, MID, :] + cm1[i + 1, MID, :]
        pair = pair_sum(rest)
        pair = 0.125 * (pair + swap_lanes(pair, 2))
        packed[i : i + 1, :] = jnp.sum(jnp.where(pick, pair, 0.0), axis=0, keepdims=True)
    for copy in copies:
        copy.wait()


def down_kernel(
    columns,
    share0, share1, inverse0, inverse1, diagonal0,
    cshare0, cshare1, cinverse0, cinverse1, cdiagonal0, coarsest,
    own, near, far,
    *refs,
):
    kept, packed = refs[:7], refs[7]
    scaled0, scaled1, cscaled0, cscaled1, v0, v1, e0, e1, rest, message, done = refs[8:]
    planes, width = share0.shape[1], share0.shape[3]
    coarse = planes // 4
    held = (scaled0, scaled1, cscaled0, cscaled1, v1.at[1 : planes + 1, MID, :], e1.at[1 : coarse + 1, MID, :], message)
    copies = [pltpu.make_async_copy(ref, hbm, done.at[k]) for k, (ref, hbm) in enumerate(zip(held, kept))]
    for ref in (v0, v1, e0, e1):
        clear_edges(ref)
    near_at, far_at = neighbour_rows(columns)
    places = ((own, 2 * ROWS, ROWS), (near, 2 * ROWS, near_at), (far, 0, far_at))
    arrays = (
        (0, scaled_store(scaled0, inverse0)),
        (ROWS, scaled_store(scaled1, inverse1)),
        (2 * ROWS, padded_store(v1)),
    )
    unfold_slabs(places, arrays, planes)
    for copy in copies[:2]:
        copy.start()

    for _ in range(SWEEPS):
        fine_pass(0, v0, v1, share0, scaled0)
        fine_pass(1, v1, v0, share1, scaled1)
    copies[4].start()

    part = slice(*INNER)
    even = coarse_low(0, width, INNER)

    def restrict(i, _):
        fields = []
        for half in (0, 1):
            total = 0.0
            for parity in (0, 1):
                x = 4 * i + 2 * half + parity
                sides = around_fine(v1, x, fine_low(parity, 0, width, INNER), INNER)
                updated = relax(scaled0[x, part, :], share0[:, x, part, :], sides)
                total = total + diagonal0[x, part, :] * (updated - v0[x + 1, shifted(INNER, 0), :])
            fields.append(0.5 * (total + swap_lanes(total, 1)))
        first = jnp.where(even, fields[0], fields[1]) * cinverse0[i, part, :]
        cscaled0[i, part, :] = first
        e0[i + 1, shifted(INNER, 0), :] = first
        cscaled1[i, part, :] = jnp.where(even, fields[1], fields[0]) * cinverse1[i, part, :]
        return 0

    lax.fori_loop(0, coarse, restrict, 0, unroll=2)
    for copy in copies[2:4]:
        copy.start()

    for sweep in range(SWEEPS):
        if sweep:
            coarse_pass(0, e0, e1, cshare0, cscaled0, INNER)
        coarse_pass(1, e1, e0, cshare1, cscaled1, INNER)
    copies[5].start()

    first = lanes((ROWS, width)) % 2 == 0
    for i in range(coarse):
        message[i, 0:ROWS, :] = jnp.where(first, e1[i + 1, 2 * ROWS : 3 * ROWS, :], cscaled0[i, ROWS : 2 * ROWS, :])
        message[i, ROWS : 2 * ROWS, :] = cscaled1[i, ROWS : 2 * ROWS, :]
    copies[6].start()

    pick = picked(width)
    low = coarse_low(0, width, OWN)
    part = slice(*OWN)
    for i in range(coarse):
        sides = around_coarse(e1, i, low, OWN)
        updated = relax(cscaled0[i, part, :], cshare0[:, i, part, :], sides)
        rest[part, :] = cdiagonal0[i, part, :] * (updated - e0[i + 1, shifted(OWN, 0), :])
        pair = pair_sum(rest)
        pair = 0.5 * (pair + swap_lanes(pair, 2))
        packed[0, i : i + 1, :] = jnp.sum(jnp.where(pick, pair, 0.0), axis=0, keepdims=True)
    packed[0, coarse : 2 * coarse, :] = coarsest[...]
    tile = packed[0]
    for device in range(1, packed.shape[0]):
        packed[device] = tile
    for copy in copies:
        copy.wait()


def up_kernel(
    columns,
    gathered,
    *refs,
):
    kept, out = refs[: KEPT + 2], refs[KEPT + 2]
    state, work = refs[KEPT + 3 : 2 * KEPT + 1], refs[2 * KEPT + 1 :]
    share0, share1, scaled0, scaled1, diagonal0, cshare0, cshare1, cscaled0, cscaled1 = state
    v0, v1, e0, e1, near, far, bshare, coarsest, spread, done = work
    planes, width = share0.shape[1], share0.shape[3]
    held = list(state) + [v1.at[1 : planes + 1, MID, :], e1.at[1 : planes // 4 + 1, MID, :], near, far]
    copies = [pltpu.make_async_copy(hbm, ref, done.at[k]) for k, (ref, hbm) in enumerate(zip(held, kept))]
    for copy in copies[5 : KEPT - 2] + copies[KEPT - 1 :] + copies[:5] + copies[KEPT - 2 : KEPT - 1]:
        copy.start()
    count = gathered.shape[0]
    rows = planes // 4
    for ref in (v0, v1, e0, e1):
        clear_edges(ref)

    slab = slab_index(columns)
    lane = lanes((rows, width))
    part = lane % 4
    sources, mobilities = [], []
    for w in range(-REACH, REACH + 1):
        other = slab + w
        inside = jnp.logical_and(other >= 0, other < count)
        device = device_of(jnp.clip(other, 0, count - 1), columns)
        keep = jnp.where(inside, 1.0, 0.0)
        for at, into in ((0, sources), (rows, mobilities)):
            tile = gathered[device, at : at + rows, :] * keep
            for z in range(4):
                v = jnp.where(part == z, tile, 0.0)
                v = v + swap_lanes(v, 1)
                into.append(v + swap_lanes(v, 2))

    parity = (lax.broadcasted_iota(jnp.int32, (rows, width), 0) + lane // 4) % 2
    pairs = len(sources) // 2
    zero = jnp.zeros((rows, width), jnp.float32)
    low = (parity == 0, parity == 1)

    def coloured(planes_of):
        first = [jnp.where(low[0], planes_of[2 * k], planes_of[2 * k + 1]) for k in range(pairs)]
        second = [jnp.where(low[0], planes_of[2 * k + 1], planes_of[2 * k]) for k in range(pairs)]
        return [zero] + first + [zero], [zero] + second + [zero]

    source, mobility = coloured(sources), coloured(mobilities)
    row = lax.broadcasted_iota(jnp.int32, (rows, width), 0)
    scaled = ([], [])
    for k in range(pairs):
        for colour in (0, 1):
            sides = around_coarsest(mobility[1 - colour], k, low[colour])
            sides = (jnp.where(row == 0, 0.0, sides[0]), jnp.where(row == rows - 1, 0.0, sides[1])) + sides[2:]
            sides = walls(sides, lane < 4, lane >= width - 4)
            top = jnp.logical_and(jnp.logical_not(low[colour]), sides[5] == 0)
            shares, inverse, _ = weights(mean_any, mobility[colour][k + 1], sides, top)
            for a in range(6):
                bshare[colour, a, k] = shares[a]
            scaled[colour].append(source[colour][k + 1] * inverse)

    fields = [[zero] + scaled[0] + [zero], None]
    for step in range(1, 2 * BOTTOM_SWEEPS):
        colour = step % 2
        new = []
        for k in range(pairs):
            sides = around_coarsest(fields[1 - colour], k, low[colour])
            new.append(relax(scaled[colour][k], [bshare[colour, a, k] for a in range(6)], sides))
        fields[colour] = [zero] + new + [zero]

    start = 4 * REACH - ROWS // 2
    for k in range(WIN // 4):
        a, b = fields[0][start // 2 + k + 1], fields[1][start // 2 + k + 1]
        coarsest[2 * k * rows : (2 * k + 1) * rows, :] = jnp.where(low[0], a, b)
        coarsest[(2 * k + 1) * rows : (2 * k + 2) * rows, :] = jnp.where(low[0], b, a)

    for copy in copies[5 : KEPT - 2] + copies[KEPT - 1 :]:
        copy.wait()
    near_at, far_at = neighbour_rows(columns)
    first = lanes((ROWS, width)) % 2 == 0
    for i in range(rows):
        half = coarsest[pl.ds(i, WIN // 2, stride=rows), :]
        spread[pl.ds(0, WIN // 2, stride=2), :] = half
        spread[pl.ds(1, WIN // 2, stride=2), :] = half
        e1[i + 1, 2 * ROWS : 3 * ROWS, :] = e1[i + 1, 2 * ROWS : 3 * ROWS, :] + spread[ROWS : 2 * ROWS, :]
        for at, ref in ((near_at, near), (far_at, far)):
            mixed = ref[i, 0:ROWS, :]
            other = swap_lanes(mixed, 1)
            e1[i + 1, pl.ds(at + ROWS, ROWS), :] = jnp.where(first, mixed, other) + spread[pl.ds(at, ROWS), :]
            cscaled0[i, pl.ds(at, ROWS), :] = jnp.where(first, other, mixed)
            cscaled1[i, pl.ds(at, ROWS), :] = ref[i, ROWS : 2 * ROWS, :]

    for _ in range(SWEEPS):
        coarse_pass(0, e0, e1, cshare0, cscaled0)
        coarse_pass(1, e1, e0, cshare1, cscaled1)

    even = coarse_low(0, width, INNER)

    for copy in copies[:5] + copies[KEPT - 2 : KEPT - 1]:
        copy.wait()

    here = shifted(INNER, 0)

    def correct(i, _):
        a, b = e0[i + 1, here, :], e1[i + 1, here, :]
        for half, add in ((0, jnp.where(even, a, b)), (1, jnp.where(even, b, a))):
            for parity in (0, 1):
                x = 4 * i + 2 * half + parity
                v1[x + 1, here, :] = v1[x + 1, here, :] + add
        return 0

    lax.fori_loop(0, rows, correct, 0)

    for _ in range(SWEEPS):
        fine_pass(0, v0, v1, share0, scaled0, INNER)
        fine_pass(1, v1, v0, share1, scaled1, INNER)

    here, part = shifted(OWN, 0), slice(*OWN)

    def fold(i, _):
        rest = []
        for parity in range(4):
            x = 4 * i + parity
            sides = around_fine(v1, x, fine_low(parity % 2, 0, width, OWN), OWN)
            updated = relax(scaled0[x, part, :], share0[:, x, part, :], sides)
            rest.append(diagonal0[x, part, :] * (updated - v0[x + 1, here, :]))
        for a, tiles in (
            (0, [v0[4 * i + b + 1, here, :] for b in range(4)]),
            (1, [v1[4 * i + b + 1, here, :] for b in range(4)]),
            (2, rest),
        ):
            for j, tile in enumerate(swap_blocks(tiles)):
                out[4 * i + j, a * ROWS : (a + 1) * ROWS, :] = tile
        return 0

    lax.fori_loop(0, rows, fold, 0, unroll=True)


def local_slabs(shape, right_side, phase, pressure_guess):
    across, columns = shape
    count = across * columns
    bx, by, length = right_side.shape
    planes, width = across * bx, columns * by
    f32 = jnp.float32
    order = place_of(across, columns)
    path = sorted(range(count), key=lambda device: order[device])
    near = [pair for k in range(0, count, 2) for pair in ((path[k], path[k + 1]), (path[k + 1], path[k]))]
    far = [pair for k in range(1, count - 1, 2) for pair in ((path[k], path[k + 1]), (path[k + 1], path[k]))]
    axes = ("gx", "yz")
    params = pltpu.CompilerParams(vmem_limit_bytes=20 * 1024 * 1024)

    def struct(*dims):
        return jax.ShapeDtypeStruct(dims, f32)

    def vmem(*dims):
        return pltpu.VMEM(dims, f32)

    bricks = pl.pallas_call(
        functools.partial(pack_kernel, order),
        in_specs=[pl.BlockSpec(memory_space=pltpu.HBM)] * 3,
        out_shape=struct(count, 5 * ROWS, 128),
        scratch_shapes=[
            vmem(bx, by, length),
            pltpu.VMEM((bx, by, length), phase.dtype),
            vmem(bx, by, length),
            vmem(3, length, 128),
            pltpu.SemaphoreType.DMA((3,)),
        ],
        compiler_params=params,
        name="pack",
    )(*(pltpu.with_memory_space_constraint(x, pltpu.HBM) for x in (right_side, phase, pressure_guess)))
    own = lax.all_to_all(bricks, axes, 0, 0)
    mobility, fields = own[:, : 2 * ROWS], own[:, 2 * ROWS :]
    mobility_far = lax.ppermute(mobility, axes, far)
    own_near = lax.ppermute(own, axes, near)
    fields_far = lax.ppermute(fields, axes, far)

    coarse = planes // 4
    share, cshare = (6, planes, WIN, width), (6, coarse, WIN, width)
    plane, cplane = (planes, WIN, width), (coarse, WIN, width)
    padded = [vmem(planes + 2, WIN + 2 * ROWS, width)] * 2
    cpadded = [vmem(coarse + 2, WIN + 2 * ROWS, width)] * 2

    def hbm(*shapes):
        return [pltpu.HBM(dims, f32) for dims in shapes], [pl.BlockSpec(memory_space=pltpu.HBM)] * len(shapes)

    def near_core(*shapes):
        return [struct(*dims) for dims in shapes], [pl.BlockSpec(memory_space=pltpu.VMEM)] * len(shapes)

    first = near_core(share, share, plane, plane, plane, cshare, cshare, cplane, cplane, cplane, (coarse, width))
    second = hbm(share, share, plane, cshare, cshare)
    *made, share0, share1, diagonal0, cshare0, cshare1 = pl.pallas_call(
        functools.partial(weights_kernel, columns),
        out_shape=first[0] + second[0],
        out_specs=first[1] + second[1],
        scratch_shapes=padded + cpadded + [vmem(WIN, width), pltpu.SemaphoreType.DMA((5,))],
        compiler_params=params,
        cost_estimate=pl.CostEstimate(flops=20_000_000_000, bytes_accessed=100_000_000, transcendentals=0),
        name="weights",
    )(own, own_near, mobility_far)

    first = hbm(plane, plane, cplane, cplane, plane, cplane, (coarse, 2 * ROWS, width))
    second = near_core((count, 2 * coarse, width))
    scaled0, scaled1, cscaled0, cscaled1, field1, cfield1, message, packed = pl.pallas_call(
        functools.partial(down_kernel, columns),
        out_shape=first[0] + second[0],
        out_specs=first[1] + second[1],
        scratch_shapes=[vmem(*plane)] * 2 + [vmem(*cplane)] * 2 + padded + cpadded + [
            vmem(WIN, width),
            vmem(coarse, 2 * ROWS, width),
            pltpu.SemaphoreType.DMA((7,)),
        ],
        compiler_params=params,
        name="down",
    )(*made, own, own_near, fields_far)
    state = (share0, share1, scaled0, scaled1, diagonal0, cshare0, cshare1, cscaled0, cscaled1, field1, cfield1)
    fine = [vmem(*share)] * 2 + [vmem(*plane)] * 3
    half = [vmem(*cshare)] * 2 + [vmem(*cplane)] * 2
    gathered = lax.all_to_all(packed, axes, 0, 0)
    message_far = lax.ppermute(message, axes, far)
    message_near = lax.ppermute(message, axes, near)

    cycle = pl.pallas_call(
        functools.partial(up_kernel, columns),
        out_shape=struct(count, 3 * ROWS, 128),
        in_specs=[pl.BlockSpec(memory_space=pltpu.VMEM)] + [pl.BlockSpec(memory_space=pltpu.HBM)] * (KEPT + 2),
        scratch_shapes=fine + half + padded + cpadded + [vmem(coarse, 2 * ROWS, width)] * 2 + [
            vmem(2, 6, 2 * (2 * REACH + 1), coarse, width),
            vmem(WIN // 2 * coarse, width),
            vmem(WIN, width),
            pltpu.SemaphoreType.DMA((KEPT + 2,)),
        ],
        compiler_params=params,
        name="up",
    )(gathered, *(pltpu.with_memory_space_constraint(x, pltpu.HBM) for x in (*state, message_near, message_far)))
    back = lax.all_to_all(cycle, axes, 0, 0)
    return pl.pallas_call(
        functools.partial(unpack_kernel, order),
        out_shape=[struct(bx, by, length)] * 2,
        scratch_shapes=[vmem(2, length, 128)],
        compiler_params=params,
        name="unpack",
    )(back)


def solution(mesh):
    spec = P("gx", "yz", None)
    shape = (mesh.shape["gx"], mesh.shape["yz"])

    def cycle(right_side, phase, pressure_guess):
        bx, by, length = right_side.shape
        slabs = (bx, by, shape[1]) == (4, 32, 4) and length == 2 * ROWS * shape[0] * shape[1]
        if slabs and shape[0] == 8:
            return local_slabs(shape, right_side, phase, pressure_guess)
        return local(right_side, phase, pressure_guess)

    return jax.shard_map(cycle, mesh=mesh, in_specs=(spec,) * 3, out_specs=(spec,) * 2, check_vma=False)
```

```python
import functools

import jax
import jax.numpy as jnp
from jax import lax
from jax.experimental import pallas as pl
from jax.experimental.pallas import tpu as pltpu
from jax.sharding import PartitionSpec as P

SWEEPS = 2
BOTTOM_SWEEPS = 4


def with_halo(x, sides, width):
    for axis, dim in sides:
        size, length = (lax.axis_size(axis), x.shape[dim])
        up = [(i, (i + 1) % size) for i in range(size - 1)]
        down = [(j, i) for i, j in up]
        last = lax.slice_in_dim(x, length - width, length, axis=dim)
        first = lax.slice_in_dim(x, 0, width, axis=dim)
        before = lax.ppermute(last, axis, up)
        after = lax.ppermute(first, axis, down)
        x = jnp.concatenate([before, x, after], axis=dim)
    return x


def harmonic(left, right):
    total = left + right
    safe = jnp.where(total > 0, total, 1.0)
    return jnp.where(total > 0, 2.0 * left * right / safe, 0.0)


def coefficients(padded):
    faces_x = harmonic(padded[1:], padded[:-1])
    faces_y = harmonic(padded[:, 1:], padded[:, :-1])
    centre = padded[1:-1, 1:-1]
    faces_z = harmonic(centre[:, :, 1:], centre[:, :, :-1])
    zero_plane = jnp.zeros_like(centre[:, :, :1])
    x_lower = faces_x[:-1, 1:-1]
    x_upper = faces_x[1:, 1:-1]
    y_lower = faces_y[1:-1, :-1]
    y_upper = faces_y[1:-1, 1:]
    z_lower = jnp.concatenate([zero_plane, faces_z], axis=2)
    z_upper = jnp.concatenate([faces_z, 2.0 * centre[:, :, -1:]], axis=2)
    diagonal = x_lower + x_upper + y_lower + y_upper + z_lower + z_upper
    diagonal = jnp.where(diagonal > 0, diagonal, 1.0)
    return (x_lower, x_upper, y_lower, y_upper, z_lower, z_upper, diagonal)


def shrink(coeffs):
    return tuple((item[1:-1, 1:-1] for item in coeffs))


def parity_of(extent, start_x, start_y):
    index_x = lax.broadcasted_iota(jnp.int32, extent, 0) + start_x
    index_y = lax.broadcasted_iota(jnp.int32, extent, 1) + start_y
    index_z = lax.broadcasted_iota(jnp.int32, extent, 2)
    return (index_x + index_y + index_z) % 2


def neighbours(padded, coeffs):
    centre = padded[1:-1, 1:-1]
    zero_plane = jnp.zeros_like(centre[:, :, :1])
    lower_z = jnp.concatenate([zero_plane, centre[:, :, :-1]], axis=2)
    upper_z = jnp.concatenate([centre[:, :, 1:], zero_plane], axis=2)
    beside_all = coeffs[0] * padded[:-2, 1:-1] + coeffs[1] * padded[2:, 1:-1]
    beside_all = beside_all + coeffs[2] * padded[1:-1, :-2] + coeffs[3] * padded[1:-1, 2:]
    beside_all = beside_all + coeffs[4] * lower_z + coeffs[5] * upper_z
    return (beside_all, centre)


def colour_pass(padded, source, coeffs, parity, colour):
    beside_all, centre = neighbours(padded, coeffs)
    updated = (source + beside_all) / coeffs[6]
    return jnp.where(parity == colour, updated, centre)


def residual_of(padded, source, coeffs):
    beside_all, centre = neighbours(padded, coeffs)
    return source - (coeffs[6] * centre - beside_all)


def restrict_sum(field):
    size_x, size_y, size_z = field.shape
    return 0.5 * field.reshape(size_x // 2, 2, size_y // 2, 2, size_z // 2, 2).sum(axis=(1, 3, 5))


def restrict_mean(field):
    size_x, size_y, size_z = field.shape
    return 0.125 * field.reshape(size_x // 2, 2, size_y // 2, 2, size_z // 2, 2).sum(axis=(1, 3, 5))


def inject(field):
    return jnp.repeat(jnp.repeat(jnp.repeat(field, 2, axis=0), 2, axis=1), 2, axis=2)


def rim_one(field):
    return with_halo(field, (("gx", 0), ("yz", 1)), 1)


def rim_two(field):
    return with_halo(field, (("gx", 0), ("yz", 1)), 2)


def offsets(field):
    return (lax.axis_index("gx") * field.shape[0], lax.axis_index("yz") * field.shape[1])


def prepare_plain(mobility):
    start_x, start_y = offsets(mobility)
    return (coefficients(rim_one(mobility)), parity_of(mobility.shape, start_x, start_y))


def prepare(mobility):
    start_x, start_y = offsets(mobility)
    size_x, size_y, size_z = mobility.shape
    region = coefficients(rim_two(mobility))
    loop_parity = parity_of((size_x + 2, size_y + 2, size_z), start_x - 1, start_y - 1)
    operator_set = (
        shrink(region),
        parity_of(mobility.shape, start_x, start_y),
        region,
        loop_parity,
    )
    return operator_set


def smooth_plain(field, source, operator_set, sweeps, rim):
    coeffs = operator_set[0]
    parity = operator_set[1]
    for _ in range(sweeps):
        field = colour_pass(rim(field), source, coeffs, parity, 0)
        field = colour_pass(rim(field), source, coeffs, parity, 1)
    return field


def smooth(field, source, operator_set, sweeps):
    interior, parity, region, loop_parity = operator_set
    source_loop = rim_one(source)
    for _ in range(sweeps):
        loop_field = colour_pass(rim_two(field), source_loop, region, loop_parity, 0)
        field = colour_pass(loop_field, source, interior, parity, 1)
    return field


def local(right_side, phase, pressure_guess):
    mobility = 1.0 + 999.0 * phase.astype(jnp.float32)
    level_zero = prepare(mobility)
    pressure = smooth(pressure_guess, right_side, level_zero, SWEEPS)
    fine_res = residual_of(rim_one(pressure), right_side, level_zero[0])
    source_one = restrict_sum(fine_res)
    mobility_one = restrict_mean(mobility)
    level_one = prepare(mobility_one)
    coarse_one = smooth(jnp.zeros_like(source_one), source_one, level_one, SWEEPS)
    res_one = residual_of(rim_one(coarse_one), source_one, level_one[0])
    source_two = restrict_sum(res_one)
    mobility_two = restrict_mean(mobility_one)
    level_two = prepare_plain(mobility_two)
    coarse_two = smooth_plain(
        jnp.zeros_like(source_two), source_two, level_two, BOTTOM_SWEEPS, rim_one
    )
    coarse_one = smooth(coarse_one + inject(coarse_two), source_one, level_one, SWEEPS)
    pressure = smooth(pressure + inject(coarse_one), right_side, level_zero, SWEEPS)
    residual = residual_of(rim_one(pressure), right_side, level_zero[0])
    return (pressure, residual)


ROWS = 8
WIN = 3 * ROWS
REACH = 3
MIX = 2.0 / 1001.0


def place_of(rows, columns):
    slab = []
    for g in range(rows):
        a = (g // 2) * 2 + ((g % 2) ^ ((g // 2) % 2))
        slab += [a * columns + (j if a % 2 == 0 else columns - 1 - j) for j in range(columns)]
    return slab


def slab_index(columns):
    g, j = lax.axis_index("gx"), lax.axis_index("yz")
    a = (g // 2) * 2 + (g + g // 2) % 2
    return a * columns + jnp.where(a % 2 == 0, j, columns - 1 - j)


def device_of(slab, columns):
    a, b = slab // columns, slab % columns
    g = (a // 2) * 2 + (a + a // 2) % 2
    return g * columns + jnp.where(a % 2 == 0, b, columns - 1 - b)


def lanes(shape):
    return lax.broadcasted_iota(jnp.int32, shape, len(shape) - 1)


def swap_lanes(v, step):
    width = v.shape[-1]
    up, down = pltpu.roll(v, step, 1), pltpu.roll(v, width - step, 1)
    return jnp.where((lanes(v.shape) // step) % 2 == 0, down, up)


def swap_blocks(tiles):
    block = lanes(tiles[0].shape) // 32
    at = [block == b for b in range(3)]

    def choose(four):
        return jnp.where(at[0], four[0], jnp.where(at[1], four[1], jnp.where(at[2], four[2], four[3])))

    turned = [choose([tiles[(b + d) % 4] for b in range(4)]) for d in range(4)]
    turned = [turned[0]] + [pltpu.roll(turned[d], 32 * d, 1) for d in (1, 2, 3)]
    return [choose([turned[(b - a) % 4] for b in range(4)]) for a in range(4)]


def brick_parity(shape):
    lane = lanes(shape)
    return (lane // 32 + lane) % 2


def pack_kernel(order, source_hbm, phase_hbm, guess_hbm, out_ref, source_ref, phase_ref, guess_ref, turned, arrived):
    copies = [
        pltpu.make_async_copy(hbm, ref, arrived.at[a])
        for a, (hbm, ref) in enumerate(((source_hbm, source_ref), (phase_hbm, phase_ref), (guess_hbm, guess_ref)))
    ]
    for copy in copies:
        copy.start()
    for a, ref in enumerate((source_ref, phase_ref, guess_ref)):
        copies[a].wait()
        brick = ref[...].reshape(128, ref.shape[2])
        if a == 1:
            brick = 1.0 + 999.0 * brick.astype(jnp.float32)
        turned[a] = brick.T
    even = brick_parity((ROWS, 128)) == 0
    for device, slab in enumerate(order):
        base = 2 * ROWS * slab
        for a, at in ((1, 0), (0, 2 * ROWS), (2, 3 * ROWS)):
            low = turned[a, pl.ds(base, ROWS, stride=2), :]
            high = turned[a, pl.ds(base + 1, ROWS, stride=2), :]
            if a != 2:
                out_ref[device, at : at + ROWS, :] = jnp.where(even, low, high)
            out_ref[device, at + ROWS : at + 2 * ROWS, :] = jnp.where(even, high, low)


def unpack_kernel(order, in_ref, pressure_ref, residual_ref, turned):
    even = brick_parity((ROWS, 128)) == 0
    for device, slab in enumerate(order):
        base = 2 * ROWS * slab
        p0, p1 = in_ref[device, 0:ROWS, :], in_ref[device, ROWS : 2 * ROWS, :]
        r0 = in_ref[device, 2 * ROWS : 3 * ROWS, :]
        turned[0, pl.ds(base, ROWS, stride=2), :] = jnp.where(even, p0, p1)
        turned[0, pl.ds(base + 1, ROWS, stride=2), :] = jnp.where(even, p1, p0)
        turned[1, pl.ds(base, ROWS, stride=2), :] = jnp.where(even, r0, 0.0)
        turned[1, pl.ds(base + 1, ROWS, stride=2), :] = jnp.where(even, 0.0, r0)
    for a, ref in enumerate((pressure_ref, residual_ref)):
        ref[...] = turned[a].T.reshape(ref.shape)


ALL = (0, WIN)
INNER = (ROWS // 2, WIN - ROWS // 2)
OWN = (ROWS, 2 * ROWS)
MID = slice(ROWS, ROWS + WIN)


def shifted(rows, by):
    return slice(ROWS + rows[0] + by, ROWS + rows[1] + by)


def within(ref, rows):
    start = (WIN - ref.shape[-2]) // 2
    return slice(rows[0] - start, rows[1] - start)


def clear_outside(ref):
    planes, rows, width = ref.shape
    for plane in (0, planes - 1):
        ref[plane] = jnp.zeros((rows, width), jnp.float32)


def around_fine(ref, x, low, rows=ALL):
    here = shifted(rows, 0)
    centre = ref[x + 1, here, :]
    width = centre.shape[1]
    return (
        ref[x, here, :],
        ref[x + 2, here, :],
        pltpu.roll(centre, 1, 1),
        pltpu.roll(centre, width - 1, 1),
        centre,
        jnp.where(low, ref[x + 1, shifted(rows, -1), :], ref[x + 1, shifted(rows, 1), :]),
    )


def around_coarse(ref, i, low, rows=ALL):
    here = shifted(rows, 0)
    centre = ref[i + 1, here, :]
    width = centre.shape[1]
    return (
        ref[i + 1, shifted(rows, -1), :],
        ref[i + 1, shifted(rows, 1), :],
        pltpu.roll(centre, 2, 1),
        pltpu.roll(centre, width - 2, 1),
        centre,
        jnp.where(low, ref[i, here, :], ref[i + 2, here, :]),
    )


def around_coarsest(planes, k, low):
    centre = planes[k + 1]
    rows, width = centre.shape
    return (
        pltpu.roll(centre, 1, 0),
        pltpu.roll(centre, rows - 1, 0),
        pltpu.roll(centre, 4, 1),
        pltpu.roll(centre, width - 4, 1),
        centre,
        jnp.where(low, planes[k], planes[k + 2]),
    )


def walls(sides, first, last):
    return sides[:2] + (jnp.where(first, 0.0, sides[2]), jnp.where(last, 0.0, sides[3])) + sides[4:]


def mean_fine(u, w):
    return jnp.where(u == w, u, (u * MIX) * w)


def mean_any(u, w):
    total = u + w
    return 2.0 * u * w / jnp.where(total > 0, total, 1.0)


def weights(mean, u, sides, top):
    faces = [mean(u, w) for w in sides]
    diagonal = (faces[0] + faces[1]) + (faces[2] + faces[3]) + (faces[4] + faces[5])
    diagonal = diagonal + jnp.where(top, 2.0 * u, 0.0)
    diagonal = jnp.where(diagonal > 0, diagonal, 1.0)
    inverse = 1.0 / diagonal
    return [face * inverse for face in faces], inverse, diagonal


def relax(scaled, share, sides):
    parts = [share[a] * sides[a] for a in range(6)]
    return scaled + ((parts[0] + parts[1]) + (parts[2] + parts[3]) + (parts[4] + parts[5]))


def fine_low(x_parity, colour, width, rows=ALL):
    return (lanes((rows[1] - rows[0], width)) + (x_parity + colour)) % 2 == 0


def coarse_low(colour, width, rows=ALL):
    shape = (rows[1] - rows[0], width)
    row = lax.broadcasted_iota(jnp.int32, shape, 0) + rows[0]
    return (row + lanes(shape) // 2 + colour) % 2 == 0


def fine_pass(colour, target, other, share, scaled, rows=ALL):
    planes, width = share.shape[1], share.shape[3]
    part, held = slice(*rows), within(share, rows)

    def two(i, _):
        for parity in (0, 1):
            x = 2 * i + parity
            sides = around_fine(other, x, fine_low(parity, colour, width, rows), rows)
            target[x + 1, shifted(rows, 0), :] = relax(scaled[x, part, :], share[:, x, held, :], sides)
        return 0

    lax.fori_loop(0, planes // 2, two, 0, unroll=True)


def coarse_pass(colour, target, other, share, scaled, rows=ALL):
    planes, width = share.shape[1], share.shape[3]
    part = slice(*rows)

    def one(i, _):
        sides = around_coarse(other, i, coarse_low(colour, width, rows), rows)
        target[i + 1, shifted(rows, 0), :] = relax(scaled[i, part, :], share[:, i, part, :], sides)
        return 0

    lax.fori_loop(0, planes, one, 0, unroll=True)


def neighbour_rows(columns):
    near = jnp.where(slab_index(columns) % 2 == 0, 2 * ROWS, 0)
    return pl.multiple_of(near, ROWS), pl.multiple_of(2 * ROWS - near, ROWS)


def unfold_slabs(places, arrays, planes):
    def unfold(i, _):
        for ref, start, at in places:
            for first, store in arrays:
                tiles = [ref[4 * i + j, start + first : start + first + ROWS, :] for j in range(4)]
                for j, tile in enumerate(swap_blocks(tiles)):
                    store(4 * i + j, at, tile)
        return 0

    lax.fori_loop(0, planes // 4, unfold, 0, unroll=True)


def padded_store(ref):
    def store(x, at, tile):
        ref[x + 1, pl.ds(at + ROWS, ROWS), :] = tile

    return store


def scaled_store(ref, factor):
    def store(x, at, tile):
        rows = pl.ds(at, ROWS)
        ref[x, rows, :] = tile * factor[x, rows, :]

    return store


def pair_sum(ref):
    return ref[ROWS : 2 * ROWS, :] + ref[ROWS + 1 : 2 * ROWS + 1, :]


def picked(width):
    row = lax.broadcasted_iota(jnp.int32, (ROWS, width), 0)
    return jnp.logical_and(row % 2 == 0, lanes((ROWS, width)) % 4 == row // 2)


def fine_weights(m0, m1, outputs, diagonal0, rows):
    planes, width = m0.shape[0] - 2, m0.shape[2]
    lane = lanes((rows[1] - rows[0], width))

    def fine(i, _):
        for parity in (0, 1):
            x = 2 * i + parity
            for colour, mine, other in ((0, m0, m1), (1, m1, m0)):
                low = fine_low(parity, colour, width, rows)
                u = mine[x + 1, shifted(rows, 0), :]
                sides = walls(around_fine(other, x, low, rows), lane == 0, lane == width - 1)
                top = jnp.logical_and(jnp.logical_not(low), sides[5] == 0)
                shares, inverse, diagonal = weights(mean_fine, u, sides, top)
                share, factor = outputs[colour]
                for a in range(6):
                    share[a, x] = shares[a]
                if factor is not None:
                    factor[x] = inverse
                if colour == 0:
                    diagonal0[x] = diagonal
        return 0

    lax.fori_loop(0, planes // 2, fine, 0, unroll=2)


def coarse_weights(cm0, cm1, outputs, diagonal0):
    planes, width = cm0.shape[0] - 2, cm0.shape[2]
    lane = lanes((WIN, width))

    def coarse(i, _):
        for colour, mine, other in ((0, cm0, cm1), (1, cm1, cm0)):
            u = mine[i + 1, MID, :]
            sides = walls(around_coarse(other, i, coarse_low(colour, width)), lane < 2, lane >= width - 2)
            shares, inverse, diagonal = weights(mean_any, u, sides, sides[1] == 0)
            share, factor = outputs[colour]
            for a in range(6):
                share[a, i] = shares[a]
            if factor is not None:
                factor[i] = inverse
            if colour == 0 and diagonal0 is not None:
                diagonal0[i] = diagonal
        return 0

    lax.fori_loop(0, planes, coarse, 0, unroll=True)


def weights_kernel(columns, own, near, far, *refs):
    share0, share1, inverse0, inverse1, diagonal0, cshare0, cshare1, cinverse0, cinverse1, cdiagonal0, packed = refs[:11]
    kept, (m0, m1, cm0, cm1, rest, done) = refs[11:15], refs[15:]
    copies = [pltpu.make_async_copy(ref, hbm, done.at[k]) for k, (ref, hbm) in enumerate(zip((m0, m1, cm0, cm1), kept))]
    planes, width = share0.shape[1], share0.shape[3]
    for ref in (m0, m1, cm0, cm1):
        clear_outside(ref)
    near_at, far_at = neighbour_rows(columns)
    places = ((own, 0, ROWS), (near, 0, near_at), (far, 0, far_at))
    unfold_slabs(places, ((0, padded_store(m0)), (ROWS, padded_store(m1))), planes)
    for copy in copies[:2]:
        copy.start()

    even = coarse_low(0, width)

    def restrict(i, _):
        mobilities = []
        for half in (0, 1):
            x = 4 * i + 2 * half
            mass = (m0[x + 1, MID, :] + m1[x + 1, MID, :]) + (m0[x + 2, MID, :] + m1[x + 2, MID, :])
            mobilities.append(0.125 * (mass + swap_lanes(mass, 1)))
        cm0[i + 1, MID, :] = jnp.where(even, mobilities[0], mobilities[1])
        cm1[i + 1, MID, :] = jnp.where(even, mobilities[1], mobilities[0])
        return 0

    lax.fori_loop(0, planes // 4, restrict, 0, unroll=2)
    for copy in copies[2:]:
        copy.start()
    fine_weights(m0, m1, ((share0, inverse0), (share1, inverse1)), diagonal0, ALL)
    coarse_weights(cm0, cm1, ((cshare0, cinverse0), (cshare1, cinverse1)), cdiagonal0)

    pick = picked(width)
    for i in range(planes // 4):
        rest[...] = cm0[i + 1, MID, :] + cm1[i + 1, MID, :]
        pair = pair_sum(rest)
        pair = 0.125 * (pair + swap_lanes(pair, 2))
        packed[i : i + 1, :] = jnp.sum(jnp.where(pick, pair, 0.0), axis=0, keepdims=True)
    for copy in copies:
        copy.wait()


def again_kernel(*refs):
    kept, made = refs[:4], refs[5:10]
    share0, share1 = made[:2]
    diagonal0, cshare0, cshare1, m0, m1, cm0, cm1, done = refs[10:]
    copies = [pltpu.make_async_copy(hbm, ref, done.at[k]) for k, (ref, hbm) in enumerate(zip((m0, m1, cm0, cm1), kept))]
    held = (diagonal0, cshare0, cshare1)
    copies += [pltpu.make_async_copy(ref, hbm, done.at[4 + k]) for k, (ref, hbm) in enumerate(zip(held, made[2:]))]
    for copy in copies[:4]:
        copy.start()
    for copy in copies[:4]:
        copy.wait()
    coarse_weights(cm0, cm1, ((cshare0, None), (cshare1, None)), None)
    for copy in copies[5:]:
        copy.start()
    fine_weights(m0, m1, ((share0, None), (share1, None)), diagonal0, INNER)
    copies[4].start()
    for copy in copies[4:]:
        copy.wait()


def down_kernel(
    columns,
    share0, share1, inverse0, inverse1, diagonal0,
    cshare0, cshare1, cinverse0, cinverse1, cdiagonal0, coarsest,
    own, near, far,
    *refs,
):
    kept, packed = refs[:7], refs[7]
    scaled0, scaled1, cscaled0, cscaled1, v0, v1, e0, e1, rest, message, done = refs[8:]
    planes, width = share0.shape[1], share0.shape[3]
    coarse = planes // 4
    held = (scaled0, scaled1, cscaled0, cscaled1, v1.at[1 : planes + 1, MID, :], e1.at[1 : coarse + 1, MID, :], message)
    copies = [pltpu.make_async_copy(ref, hbm, done.at[k]) for k, (ref, hbm) in enumerate(zip(held, kept))]
    for ref in (v0, v1, e0, e1):
        clear_outside(ref)
    near_at, far_at = neighbour_rows(columns)
    places = ((own, 2 * ROWS, ROWS), (near, 2 * ROWS, near_at), (far, 0, far_at))
    arrays = (
        (0, scaled_store(scaled0, inverse0)),
        (ROWS, scaled_store(scaled1, inverse1)),
        (2 * ROWS, padded_store(v1)),
    )
    unfold_slabs(places, arrays, planes)
    for copy in copies[:2]:
        copy.start()

    for _ in range(SWEEPS):
        fine_pass(0, v0, v1, share0, scaled0)
        fine_pass(1, v1, v0, share1, scaled1)
    copies[4].start()

    part = slice(*INNER)
    even = coarse_low(0, width, INNER)

    def restrict(i, _):
        fields = []
        for half in (0, 1):
            total = 0.0
            for parity in (0, 1):
                x = 4 * i + 2 * half + parity
                sides = around_fine(v1, x, fine_low(parity, 0, width, INNER), INNER)
                updated = relax(scaled0[x, part, :], share0[:, x, part, :], sides)
                total = total + diagonal0[x, part, :] * (updated - v0[x + 1, shifted(INNER, 0), :])
            fields.append(0.5 * (total + swap_lanes(total, 1)))
        first = jnp.where(even, fields[0], fields[1]) * cinverse0[i, part, :]
        cscaled0[i, part, :] = first
        e0[i + 1, shifted(INNER, 0), :] = first
        cscaled1[i, part, :] = jnp.where(even, fields[1], fields[0]) * cinverse1[i, part, :]
        return 0

    lax.fori_loop(0, coarse, restrict, 0, unroll=2)
    for copy in copies[2:4]:
        copy.start()

    for sweep in range(SWEEPS):
        if sweep:
            coarse_pass(0, e0, e1, cshare0, cscaled0, INNER)
        coarse_pass(1, e1, e0, cshare1, cscaled1, INNER)
    copies[5].start()

    first = lanes((ROWS, width)) % 2 == 0
    for i in range(coarse):
        message[i, 0:ROWS, :] = jnp.where(first, e1[i + 1, 2 * ROWS : 3 * ROWS, :], cscaled0[i, ROWS : 2 * ROWS, :])
        message[i, ROWS : 2 * ROWS, :] = cscaled1[i, ROWS : 2 * ROWS, :]
    copies[6].start()

    pick = picked(width)
    low = coarse_low(0, width, OWN)
    part = slice(*OWN)
    for i in range(coarse):
        sides = around_coarse(e1, i, low, OWN)
        updated = relax(cscaled0[i, part, :], cshare0[:, i, part, :], sides)
        rest[part, :] = cdiagonal0[i, part, :] * (updated - e0[i + 1, shifted(OWN, 0), :])
        pair = pair_sum(rest)
        pair = 0.5 * (pair + swap_lanes(pair, 2))
        packed[0, i : i + 1, :] = jnp.sum(jnp.where(pick, pair, 0.0), axis=0, keepdims=True)
    packed[0, coarse : 2 * coarse, :] = coarsest[...]
    tile = packed[0]
    for device in range(1, packed.shape[0]):
        packed[device] = tile
    for copy in copies:
        copy.wait()


def up_kernel(
    columns,
    gathered, share0, share1,
    *refs,
):
    kept, out, held, work = refs[:11], refs[11], refs[12:19], refs[19:]
    cscaled0, cscaled1, cshare0, cshare1, scaled0, scaled1, diagonal0 = held
    v0, v1, e0, e1, near, far, bshare, coarsest, spread, done = work
    planes, width = share0.shape[1], share0.shape[3]
    count = gathered.shape[0]
    rows = planes // 4
    held = (near, far, e1.at[1 : rows + 1, MID, :]) + held[:4] + (v1.at[1 : planes + 1, MID, :],) + held[4:]
    copies = [pltpu.make_async_copy(hbm, ref, done.at[k]) for k, (ref, hbm) in enumerate(zip(held, kept))]
    early, late = copies[:7], copies[7:]
    for copy in early + late:
        copy.start()
    for ref in (v0, v1, e0, e1):
        clear_outside(ref)

    slab = slab_index(columns)
    lane = lanes((rows, width))
    part = lane % 4
    sources, mobilities = [], []
    for w in range(-REACH, REACH + 1):
        other = slab + w
        inside = jnp.logical_and(other >= 0, other < count)
        device = device_of(jnp.clip(other, 0, count - 1), columns)
        keep = jnp.where(inside, 1.0, 0.0)
        for at, into in ((0, sources), (rows, mobilities)):
            tile = gathered[device, at : at + rows, :] * keep
            for z in range(4):
                v = jnp.where(part == z, tile, 0.0)
                v = v + swap_lanes(v, 1)
                into.append(v + swap_lanes(v, 2))

    parity = (lax.broadcasted_iota(jnp.int32, (rows, width), 0) + lane // 4) % 2
    pairs = len(sources) // 2
    zero = jnp.zeros((rows, width), jnp.float32)
    low = (parity == 0, parity == 1)

    def coloured(planes_of):
        first = [jnp.where(low[0], planes_of[2 * k], planes_of[2 * k + 1]) for k in range(pairs)]
        second = [jnp.where(low[0], planes_of[2 * k + 1], planes_of[2 * k]) for k in range(pairs)]
        return [zero] + first + [zero], [zero] + second + [zero]

    source, mobility = coloured(sources), coloured(mobilities)
    row = lax.broadcasted_iota(jnp.int32, (rows, width), 0)
    scaled = ([], [])
    for k in range(pairs):
        for colour in (0, 1):
            sides = around_coarsest(mobility[1 - colour], k, low[colour])
            sides = (jnp.where(row == 0, 0.0, sides[0]), jnp.where(row == rows - 1, 0.0, sides[1])) + sides[2:]
            sides = walls(sides, lane < 4, lane >= width - 4)
            top = jnp.logical_and(jnp.logical_not(low[colour]), sides[5] == 0)
            shares, inverse, _ = weights(mean_any, mobility[colour][k + 1], sides, top)
            for a in range(6):
                bshare[colour, a, k] = shares[a]
            scaled[colour].append(source[colour][k + 1] * inverse)

    fields = [[zero] + scaled[0] + [zero], None]
    for step in range(1, 2 * BOTTOM_SWEEPS):
        colour = step % 2
        new = []
        for k in range(pairs):
            sides = around_coarsest(fields[1 - colour], k, low[colour])
            new.append(relax(scaled[colour][k], [bshare[colour, a, k] for a in range(6)], sides))
        fields[colour] = [zero] + new + [zero]

    start = 4 * REACH - ROWS // 2
    for k in range(WIN // 4):
        a, b = fields[0][start // 2 + k + 1], fields[1][start // 2 + k + 1]
        coarsest[2 * k * rows : (2 * k + 1) * rows, :] = jnp.where(low[0], a, b)
        coarsest[(2 * k + 1) * rows : (2 * k + 2) * rows, :] = jnp.where(low[0], b, a)

    for copy in early:
        copy.wait()
    near_at, far_at = neighbour_rows(columns)
    first = lanes((ROWS, width)) % 2 == 0
    for i in range(rows):
        half = coarsest[pl.ds(i, WIN // 2, stride=rows), :]
        spread[pl.ds(0, WIN // 2, stride=2), :] = half
        spread[pl.ds(1, WIN // 2, stride=2), :] = half
        e1[i + 1, 2 * ROWS : 3 * ROWS, :] = e1[i + 1, 2 * ROWS : 3 * ROWS, :] + spread[ROWS : 2 * ROWS, :]
        for at, ref in ((near_at, near), (far_at, far)):
            mixed = ref[i, 0:ROWS, :]
            other = swap_lanes(mixed, 1)
            e1[i + 1, pl.ds(at + ROWS, ROWS), :] = jnp.where(first, mixed, other) + spread[pl.ds(at, ROWS), :]
            cscaled0[i, pl.ds(at, ROWS), :] = jnp.where(first, other, mixed)
            cscaled1[i, pl.ds(at, ROWS), :] = ref[i, ROWS : 2 * ROWS, :]

    for _ in range(SWEEPS):
        coarse_pass(0, e0, e1, cshare0, cscaled0)
        coarse_pass(1, e1, e0, cshare1, cscaled1)

    even = coarse_low(0, width, INNER)

    for copy in late:
        copy.wait()

    here = shifted(INNER, 0)

    def correct(i, _):
        a, b = e0[i + 1, here, :], e1[i + 1, here, :]
        for half, add in ((0, jnp.where(even, a, b)), (1, jnp.where(even, b, a))):
            for parity in (0, 1):
                x = 4 * i + 2 * half + parity
                v1[x + 1, here, :] = v1[x + 1, here, :] + add
        return 0

    lax.fori_loop(0, rows, correct, 0)

    for _ in range(SWEEPS):
        fine_pass(0, v0, v1, share0, scaled0, INNER)
        fine_pass(1, v1, v0, share1, scaled1, INNER)

    here, part, own = shifted(OWN, 0), slice(*OWN), within(share0, OWN)

    def fold(i, _):
        rest = []
        for parity in range(4):
            x = 4 * i + parity
            sides = around_fine(v1, x, fine_low(parity % 2, 0, width, OWN), OWN)
            updated = relax(scaled0[x, part, :], share0[:, x, own, :], sides)
            rest.append(diagonal0[x, own, :] * (updated - v0[x + 1, here, :]))
        for a, tiles in (
            (0, [v0[4 * i + b + 1, here, :] for b in range(4)]),
            (1, [v1[4 * i + b + 1, here, :] for b in range(4)]),
            (2, rest),
        ):
            for j, tile in enumerate(swap_blocks(tiles)):
                out[4 * i + j, a * ROWS : (a + 1) * ROWS, :] = tile
        return 0

    lax.fori_loop(0, rows, fold, 0, unroll=True)


def local_slabs(shape, right_side, phase, pressure_guess):
    across, columns = shape
    count = across * columns
    bx, by, length = right_side.shape
    planes, width = across * bx, columns * by
    f32 = jnp.float32
    order = place_of(across, columns)
    path = sorted(range(count), key=lambda device: order[device])
    near = [pair for k in range(0, count, 2) for pair in ((path[k], path[k + 1]), (path[k + 1], path[k]))]
    far = [pair for k in range(1, count - 1, 2) for pair in ((path[k], path[k + 1]), (path[k + 1], path[k]))]
    axes = ("gx", "yz")
    cost = pl.CostEstimate(flops=20_000_000_000, bytes_accessed=100_000_000, transcendentals=0)
    params = pltpu.CompilerParams(vmem_limit_bytes=20 * 1024 * 1024)

    def struct(*dims):
        return jax.ShapeDtypeStruct(dims, f32)

    def vmem(*dims):
        return pltpu.VMEM(dims, f32)

    bricks = pl.pallas_call(
        functools.partial(pack_kernel, order),
        in_specs=[pl.BlockSpec(memory_space=pltpu.HBM)] * 3,
        out_shape=struct(count, 5 * ROWS, 128),
        scratch_shapes=[
            vmem(bx, by, length),
            pltpu.VMEM((bx, by, length), phase.dtype),
            vmem(bx, by, length),
            vmem(3, length, 128),
            pltpu.SemaphoreType.DMA((3,)),
        ],
        compiler_params=params,
        name="pack",
    )(*(pltpu.with_memory_space_constraint(x, pltpu.HBM) for x in (right_side, phase, pressure_guess)))
    own = lax.all_to_all(bricks, axes, 0, 0)
    mobility, fields = own[:, : 2 * ROWS], own[:, 2 * ROWS :]
    mobility_far = lax.ppermute(mobility, axes, far)
    own_near = lax.ppermute(own, axes, near)
    fields_far = lax.ppermute(fields, axes, far)

    coarse = planes // 4
    share, cshare = (6, planes, WIN, width), (6, coarse, WIN, width)
    plane, cplane = (planes, WIN, width), (coarse, WIN, width)
    padded = [vmem(planes + 2, WIN + 2 * ROWS, width)] * 2
    cpadded = [vmem(coarse + 2, WIN + 2 * ROWS, width)] * 2

    def hbm(*shapes):
        return [pltpu.HBM(dims, f32) for dims in shapes], [pl.BlockSpec(memory_space=pltpu.HBM)] * len(shapes)

    def near_core(*shapes):
        return [struct(*dims) for dims in shapes], [pl.BlockSpec(memory_space=pltpu.VMEM)] * len(shapes)

    first = near_core(share, share, plane, plane, plane, cshare, cshare, cplane, cplane, cplane, (coarse, width))
    second = hbm((planes + 2, WIN + 2 * ROWS, width), (planes + 2, WIN + 2 * ROWS, width), (coarse + 2, WIN + 2 * ROWS, width), (coarse + 2, WIN + 2 * ROWS, width))
    *made, m0, m1, cm0, cm1 = pl.pallas_call(
        functools.partial(weights_kernel, columns),
        out_shape=first[0] + second[0],
        out_specs=first[1] + second[1],
        scratch_shapes=padded + cpadded + [vmem(WIN, width), pltpu.SemaphoreType.DMA((4,))],
        compiler_params=params,
        cost_estimate=cost,
        name="weights",
    )(own, own_near, mobility_far)

    first = hbm(plane, plane, cplane, cplane, plane, cplane, (coarse, 2 * ROWS, width))
    second = near_core((count, 2 * coarse, width))
    scaled0, scaled1, cscaled0, cscaled1, field1, cfield1, message, packed = pl.pallas_call(
        functools.partial(down_kernel, columns),
        out_shape=first[0] + second[0],
        out_specs=first[1] + second[1],
        scratch_shapes=[vmem(*plane)] * 2 + [vmem(*cplane)] * 2 + padded + cpadded + [
            vmem(WIN, width),
            vmem(coarse, 2 * ROWS, width),
            pltpu.SemaphoreType.DMA((7,)),
        ],
        compiler_params=params,
        name="down",
    )(*made, own, own_near, fields_far)
    gathered = lax.all_to_all(packed, axes, 0, 0)
    message_far = lax.ppermute(message, axes, far)
    message_near = lax.ppermute(message, axes, near)

    def in_hbm(*arrays):
        return [pltpu.with_memory_space_constraint(x, pltpu.HBM) for x in arrays]

    middle = (planes, INNER[1] - INNER[0], width)
    made = [(6,) + middle, (6,) + middle, middle, cshare, cshare]
    first, second = near_core(*made[:2]), hbm(*made[2:])
    share0, share1, diagonal0, cshare0, cshare1 = pl.pallas_call(
        again_kernel,
        out_shape=first[0] + second[0],
        in_specs=[pl.BlockSpec(memory_space=pltpu.HBM)] * 5,
        out_specs=first[1] + second[1],
        scratch_shapes=[vmem(*dims) for dims in made[2:]] + padded + cpadded + [pltpu.SemaphoreType.DMA((7,))],
        compiler_params=params,
        cost_estimate=pl.CostEstimate(flops=1_000_000_000, bytes_accessed=1_000_000, transcendentals=0),
        name="again",
    )(*in_hbm(m0, m1, cm0, cm1, message))

    kept = (message_near, message_far, cfield1, cscaled0, cscaled1, cshare0, cshare1, field1)
    kept += (scaled0, scaled1, diagonal0)
    cycle = pl.pallas_call(
        functools.partial(up_kernel, columns),
        out_shape=struct(count, 3 * ROWS, 128),
        in_specs=[pl.BlockSpec(memory_space=pltpu.VMEM)] * 3 + [pl.BlockSpec(memory_space=pltpu.HBM)] * len(kept),
        scratch_shapes=[vmem(*dims) for dims in (cplane, cplane, cshare, cshare, plane, plane, middle)] + padded + cpadded + [vmem(coarse, 2 * ROWS, width)] * 2 + [
            vmem(2, 6, 2 * (2 * REACH + 1), coarse, width),
            vmem(WIN // 2 * coarse, width),
            vmem(WIN, width),
            pltpu.SemaphoreType.DMA((len(kept),)),
        ],
        compiler_params=params,
        name="up",
    )(gathered, share0, share1, *in_hbm(*kept))
    back = lax.all_to_all(cycle, axes, 0, 0)
    return pl.pallas_call(
        functools.partial(unpack_kernel, order),
        out_shape=[struct(bx, by, length)] * 2,
        scratch_shapes=[vmem(2, length, 128)],
        compiler_params=params,
        name="unpack",
    )(back)


def solution(mesh):
    spec = P("gx", "yz", None)
    shape = (mesh.shape["gx"], mesh.shape["yz"])

    def cycle(right_side, phase, pressure_guess):
        bx, by, length = right_side.shape
        slabs = (bx, by, shape[1]) == (4, 32, 4) and length == 2 * ROWS * shape[0] * shape[1]
        if slabs and shape[0] == 8:
            return local_slabs(shape, right_side, phase, pressure_guess)
        return local(right_side, phase, pressure_guess)

    return jax.shard_map(cycle, mesh=mesh, in_specs=(spec,) * 3, out_specs=(spec,) * 2, check_vma=False)
```

```python
import functools

import jax
import jax.numpy as jnp
from jax import lax
from jax.experimental import pallas as pl
from jax.experimental.pallas import tpu as pltpu
from jax.sharding import PartitionSpec as P

SWEEPS = 2
BOTTOM_SWEEPS = 4


def with_halo(x, sides, width):
    for axis, dim in sides:
        size, length = (lax.axis_size(axis), x.shape[dim])
        up = [(i, (i + 1) % size) for i in range(size - 1)]
        down = [(j, i) for i, j in up]
        last = lax.slice_in_dim(x, length - width, length, axis=dim)
        first = lax.slice_in_dim(x, 0, width, axis=dim)
        before = lax.ppermute(last, axis, up)
        after = lax.ppermute(first, axis, down)
        x = jnp.concatenate([before, x, after], axis=dim)
    return x


def harmonic(left, right):
    total = left + right
    safe = jnp.where(total > 0, total, 1.0)
    return jnp.where(total > 0, 2.0 * left * right / safe, 0.0)


def coefficients(padded):
    faces_x = harmonic(padded[1:], padded[:-1])
    faces_y = harmonic(padded[:, 1:], padded[:, :-1])
    centre = padded[1:-1, 1:-1]
    faces_z = harmonic(centre[:, :, 1:], centre[:, :, :-1])
    zero_plane = jnp.zeros_like(centre[:, :, :1])
    x_lower = faces_x[:-1, 1:-1]
    x_upper = faces_x[1:, 1:-1]
    y_lower = faces_y[1:-1, :-1]
    y_upper = faces_y[1:-1, 1:]
    z_lower = jnp.concatenate([zero_plane, faces_z], axis=2)
    z_upper = jnp.concatenate([faces_z, 2.0 * centre[:, :, -1:]], axis=2)
    diagonal = x_lower + x_upper + y_lower + y_upper + z_lower + z_upper
    diagonal = jnp.where(diagonal > 0, diagonal, 1.0)
    return (x_lower, x_upper, y_lower, y_upper, z_lower, z_upper, diagonal)


def shrink(coeffs):
    return tuple((item[1:-1, 1:-1] for item in coeffs))


def parity_of(extent, start_x, start_y):
    index_x = lax.broadcasted_iota(jnp.int32, extent, 0) + start_x
    index_y = lax.broadcasted_iota(jnp.int32, extent, 1) + start_y
    index_z = lax.broadcasted_iota(jnp.int32, extent, 2)
    return (index_x + index_y + index_z) % 2


def neighbours(padded, coeffs):
    centre = padded[1:-1, 1:-1]
    zero_plane = jnp.zeros_like(centre[:, :, :1])
    lower_z = jnp.concatenate([zero_plane, centre[:, :, :-1]], axis=2)
    upper_z = jnp.concatenate([centre[:, :, 1:], zero_plane], axis=2)
    beside_all = coeffs[0] * padded[:-2, 1:-1] + coeffs[1] * padded[2:, 1:-1]
    beside_all = beside_all + coeffs[2] * padded[1:-1, :-2] + coeffs[3] * padded[1:-1, 2:]
    beside_all = beside_all + coeffs[4] * lower_z + coeffs[5] * upper_z
    return (beside_all, centre)


def colour_pass(padded, source, coeffs, parity, colour):
    beside_all, centre = neighbours(padded, coeffs)
    updated = (source + beside_all) / coeffs[6]
    return jnp.where(parity == colour, updated, centre)


def residual_of(padded, source, coeffs):
    beside_all, centre = neighbours(padded, coeffs)
    return source - (coeffs[6] * centre - beside_all)


def restrict_sum(field):
    size_x, size_y, size_z = field.shape
    return 0.5 * field.reshape(size_x // 2, 2, size_y // 2, 2, size_z // 2, 2).sum(axis=(1, 3, 5))


def restrict_mean(field):
    size_x, size_y, size_z = field.shape
    return 0.125 * field.reshape(size_x // 2, 2, size_y // 2, 2, size_z // 2, 2).sum(axis=(1, 3, 5))


def inject(field):
    return jnp.repeat(jnp.repeat(jnp.repeat(field, 2, axis=0), 2, axis=1), 2, axis=2)


def rim_one(field):
    return with_halo(field, (("gx", 0), ("yz", 1)), 1)


def rim_two(field):
    return with_halo(field, (("gx", 0), ("yz", 1)), 2)


def offsets(field):
    return (lax.axis_index("gx") * field.shape[0], lax.axis_index("yz") * field.shape[1])


def prepare_plain(mobility):
    start_x, start_y = offsets(mobility)
    return (coefficients(rim_one(mobility)), parity_of(mobility.shape, start_x, start_y))


def prepare(mobility):
    start_x, start_y = offsets(mobility)
    size_x, size_y, size_z = mobility.shape
    region = coefficients(rim_two(mobility))
    loop_parity = parity_of((size_x + 2, size_y + 2, size_z), start_x - 1, start_y - 1)
    operator_set = (
        shrink(region),
        parity_of(mobility.shape, start_x, start_y),
        region,
        loop_parity,
    )
    return operator_set


def smooth_plain(field, source, operator_set, sweeps, rim):
    coeffs = operator_set[0]
    parity = operator_set[1]
    for _ in range(sweeps):
        field = colour_pass(rim(field), source, coeffs, parity, 0)
        field = colour_pass(rim(field), source, coeffs, parity, 1)
    return field


def smooth(field, source, operator_set, sweeps):
    interior, parity, region, loop_parity = operator_set
    source_loop = rim_one(source)
    for _ in range(sweeps):
        loop_field = colour_pass(rim_two(field), source_loop, region, loop_parity, 0)
        field = colour_pass(loop_field, source, interior, parity, 1)
    return field


def local(right_side, phase, pressure_guess):
    mobility = 1.0 + 999.0 * phase.astype(jnp.float32)
    level_zero = prepare(mobility)
    pressure = smooth(pressure_guess, right_side, level_zero, SWEEPS)
    fine_res = residual_of(rim_one(pressure), right_side, level_zero[0])
    source_one = restrict_sum(fine_res)
    mobility_one = restrict_mean(mobility)
    level_one = prepare(mobility_one)
    coarse_one = smooth(jnp.zeros_like(source_one), source_one, level_one, SWEEPS)
    res_one = residual_of(rim_one(coarse_one), source_one, level_one[0])
    source_two = restrict_sum(res_one)
    mobility_two = restrict_mean(mobility_one)
    level_two = prepare_plain(mobility_two)
    coarse_two = smooth_plain(
        jnp.zeros_like(source_two), source_two, level_two, BOTTOM_SWEEPS, rim_one
    )
    coarse_one = smooth(coarse_one + inject(coarse_two), source_one, level_one, SWEEPS)
    pressure = smooth(pressure + inject(coarse_one), right_side, level_zero, SWEEPS)
    residual = residual_of(rim_one(pressure), right_side, level_zero[0])
    return (pressure, residual)


ROWS = 8
WIN = 3 * ROWS
REACH = 3
MIX = 2.0 / 1001.0


def place_of(rows, columns):
    slab = []
    for g in range(rows):
        a = (g // 2) * 2 + ((g % 2) ^ ((g // 2) % 2))
        slab += [a * columns + (j if a % 2 == 0 else columns - 1 - j) for j in range(columns)]
    return slab


def slab_index(columns):
    g, j = lax.axis_index("gx"), lax.axis_index("yz")
    a = (g // 2) * 2 + (g + g // 2) % 2
    return a * columns + jnp.where(a % 2 == 0, j, columns - 1 - j)


def device_of(slab, columns):
    a, b = slab // columns, slab % columns
    g = (a // 2) * 2 + (a + a // 2) % 2
    return g * columns + jnp.where(a % 2 == 0, b, columns - 1 - b)


def lanes(shape):
    return lax.broadcasted_iota(jnp.int32, shape, len(shape) - 1)


def swap_lanes(v, step):
    width = v.shape[-1]
    up, down = pltpu.roll(v, step, 1), pltpu.roll(v, width - step, 1)
    return jnp.where((lanes(v.shape) // step) % 2 == 0, down, up)


def swap_blocks(tiles):
    block = lanes(tiles[0].shape) // 32
    at = [block == b for b in range(3)]

    def choose(four):
        return jnp.where(at[0], four[0], jnp.where(at[1], four[1], jnp.where(at[2], four[2], four[3])))

    turned = [choose([tiles[(b + d) % 4] for b in range(4)]) for d in range(4)]
    turned = [turned[0]] + [pltpu.roll(turned[d], 32 * d, 1) for d in (1, 2, 3)]
    return [choose([turned[(b - a) % 4] for b in range(4)]) for a in range(4)]


def brick_parity(shape):
    lane = lanes(shape)
    return (lane // 32 + lane) % 2


def pack_kernel(order, source_hbm, phase_hbm, guess_hbm, out_ref, source_ref, phase_ref, guess_ref, turned, arrived):
    copies = [
        pltpu.make_async_copy(hbm, ref, arrived.at[a])
        for a, (hbm, ref) in enumerate(((source_hbm, source_ref), (phase_hbm, phase_ref), (guess_hbm, guess_ref)))
    ]
    for copy in copies:
        copy.start()
    for a, ref in enumerate((source_ref, phase_ref, guess_ref)):
        copies[a].wait()
        brick = ref[...].reshape(128, ref.shape[2])
        if a == 1:
            brick = 1.0 + 999.0 * brick.astype(jnp.float32)
        turned[a] = brick.T
    even = brick_parity((ROWS, 128)) == 0
    for device, slab in enumerate(order):
        base = 2 * ROWS * slab
        for a, at in ((1, 0), (0, 2 * ROWS), (2, 3 * ROWS)):
            low = turned[a, pl.ds(base, ROWS, stride=2), :]
            high = turned[a, pl.ds(base + 1, ROWS, stride=2), :]
            if a != 2:
                out_ref[device, at : at + ROWS, :] = jnp.where(even, low, high)
            out_ref[device, at + ROWS : at + 2 * ROWS, :] = jnp.where(even, high, low)


def unpack_kernel(order, in_ref, pressure_ref, residual_ref, turned):
    even = brick_parity((ROWS, 128)) == 0
    for device, slab in enumerate(order):
        base = 2 * ROWS * slab
        p0, p1 = in_ref[device, 0:ROWS, :], in_ref[device, ROWS : 2 * ROWS, :]
        r0 = in_ref[device, 2 * ROWS : 3 * ROWS, :]
        turned[0, pl.ds(base, ROWS, stride=2), :] = jnp.where(even, p0, p1)
        turned[0, pl.ds(base + 1, ROWS, stride=2), :] = jnp.where(even, p1, p0)
        turned[1, pl.ds(base, ROWS, stride=2), :] = jnp.where(even, r0, 0.0)
        turned[1, pl.ds(base + 1, ROWS, stride=2), :] = jnp.where(even, 0.0, r0)
    for a, ref in enumerate((pressure_ref, residual_ref)):
        ref[...] = turned[a].T.reshape(ref.shape)


FACE_ROWS = (1, WIN - 1)
INNER = (ROWS // 2, WIN - ROWS // 2)
OWN = (ROWS, 2 * ROWS)


def wider(rows, by):
    return (rows[0] - by, rows[1] + by)


def at(ref, rows, by=0):
    start = (WIN - ref.shape[-2]) // 2
    return slice(rows[0] - start + by, rows[1] - start + by)


def beyond(ref, i, low, rows, *lead):
    return jnp.where(low, ref[(*lead, i, at(ref, rows, -1))], ref[(*lead, i, at(ref, rows, 1))])


def add_up(terms):
    while len(terms) > 1:
        terms = [sum(terms[k : k + 2]) for k in range(0, len(terms), 2)]
    return terms[0]


def around_coarsest(planes, k, low):
    centre = planes[k + 1]
    rows, width = centre.shape
    return (
        pltpu.roll(centre, 1, 0),
        pltpu.roll(centre, rows - 1, 0),
        pltpu.roll(centre, 4, 1),
        pltpu.roll(centre, width - 4, 1),
        centre,
        jnp.where(low, planes[k], planes[k + 2]),
    )


def walls(sides, first, last):
    return sides[:2] + (jnp.where(first, 0.0, sides[2]), jnp.where(last, 0.0, sides[3])) + sides[4:]


def mean_fine(u, w):
    return jnp.where(u == w, u, (u * MIX) * w)


def mean_any(u, w):
    total = u + w
    return 2.0 * u * w / jnp.where(total > 0, total, 1.0)


def weights(mean, u, sides, top):
    faces = [mean(u, w) for w in sides]
    diagonal = (faces[0] + faces[1]) + (faces[2] + faces[3]) + (faces[4] + faces[5])
    diagonal = diagonal + jnp.where(top, 2.0 * u, 0.0)
    diagonal = jnp.where(diagonal > 0, diagonal, 1.0)
    inverse = 1.0 / diagonal
    return [face * inverse for face in faces], inverse, diagonal


def relax(scaled, share, sides):
    parts = [share[a] * sides[a] for a in range(6)]
    return scaled + ((parts[0] + parts[1]) + (parts[2] + parts[3]) + (parts[4] + parts[5]))


def fine_low(x, colour, width, rows):
    return (lanes((rows[1] - rows[0], width)) + (x + colour) % 2) % 2 == 0


def coarse_low(colour, width, rows):
    shape = (rows[1] - rows[0], width)
    row = lax.broadcasted_iota(jnp.int32, shape, 0) + rows[0]
    return (row + lanes(shape) // 2 + colour) % 2 == 0


def fine_sides(v, x, low, rows):
    here = at(v, rows)
    centre = v[x, here, :]
    width = centre.shape[1]
    return (
        v[x - 1, here, :] if x > 0 else None,
        v[x + 1, here, :] if x + 1 < v.shape[0] else None,
        pltpu.roll(centre, 1, 1),
        pltpu.roll(centre, width - 1, 1),
        centre,
        beyond(v, x, low, rows),
    )


def fine_flow(colour, face, v, x, rows):
    planes, width = face.shape[1], face.shape[3]
    part = at(face, rows)
    low = fine_low(x, colour, width, rows)
    if colour == 0:
        sides = fine_sides(v, x, low, rows)
        return add_up([face[a, x, part, :] * side for a, side in enumerate(sides) if side is not None])

    def carried(a, plane):
        values = face[a, plane, part, :]
        return values if v is None else values * v[plane, at(v, rows), :]

    away = beyond(face, x, low, rows, 5)
    terms = [
        pltpu.roll(carried(3, x), 1, 1),
        pltpu.roll(carried(2, x), width - 1, 1),
        carried(4, x),
        away if v is None else away * beyond(v, x, low, rows),
    ]
    if x > 0:
        terms.append(carried(1, x - 1))
    if x + 1 < planes:
        terms.append(carried(0, x + 1))
    return add_up(terms)


def coarse_sides(v, i, low, rows):
    here = at(v, rows)
    centre = v[i, here, :]
    width = centre.shape[1]
    below = v[i - 1, here, :] if i > 0 else jnp.zeros_like(centre)
    above = v[i + 1, here, :] if i + 1 < v.shape[0] else jnp.zeros_like(centre)
    return (
        v[i, at(v, rows, -1), :],
        v[i, at(v, rows, 1), :],
        pltpu.roll(centre, 2, 1),
        pltpu.roll(centre, width - 2, 1),
        centre,
        jnp.where(low, below, above),
    )


def coarse_flow(colour, face, v, i, rows):
    planes, width = face.shape[1], face.shape[3]
    low = coarse_low(colour, width, rows)
    if colour == 0:
        sides = coarse_sides(v, i, low, rows)
        return add_up([face[a, i, at(face, rows), :] * side for a, side in enumerate(sides)])

    def carried(a, plane, by=0):
        values = face[a, plane, at(face, rows, by), :]
        return values if v is None else values * v[plane, at(v, rows, by), :]

    centre = carried(4, i)
    below = carried(5, i - 1) if i > 0 else jnp.zeros_like(centre)
    above = carried(5, i + 1) if i + 1 < planes else jnp.zeros_like(centre)
    return add_up(
        [
            carried(1, i, -1),
            carried(0, i, 1),
            pltpu.roll(carried(3, i), 2, 1),
            pltpu.roll(carried(2, i), width - 2, 1),
            centre,
            jnp.where(low, below, above),
        ]
    )


def renew(flow, colour, target, other, face, inverse, scaled, rows):
    for x in range(face.shape[1]):
        moved = inverse[x, at(inverse, rows), :] * flow(colour, face, other, x, rows)
        target[x, at(target, rows), :] = scaled[x, at(scaled, rows), :] + moved


def rest_of(flow, v0, v1, face, inverse0, scaled0, x, rows):
    factor = inverse0[x, at(inverse0, rows), :]
    updated = scaled0[x, at(scaled0, rows), :] + factor * flow(0, face, v1, x, rows)
    return (updated - v0[x, at(v0, rows), :]) / factor


def one_over(diagonal):
    return 1.0 / jnp.where(diagonal > 0, diagonal, 1.0)


def fine_faces(m0, m1, face, inverse0, inverse1):
    planes, width = face.shape[1], face.shape[3]
    rows = FACE_ROWS
    here = at(face, rows)
    lane = lanes((rows[1] - rows[0], width))
    for x in range(planes):
        low = fine_low(x, 0, width, rows)
        u = m0[x, here, :]
        sides = walls(fine_sides(m1, x, low, rows), lane == 0, lane == width - 1)
        terms = []
        for a, side in enumerate(sides):
            value = jnp.zeros_like(u) if side is None else mean_fine(u, side)
            face[a, x, here, :] = value
            terms.append(value)
        top = jnp.logical_and(jnp.logical_not(low), sides[5] == 0)
        inverse0[x, here, :] = one_over(add_up(terms) + jnp.where(top, 2.0 * u, 0.0))
    rows = wider(rows, -1)
    for x in range(planes):
        low = fine_low(x, 1, width, rows)
        top = jnp.logical_and(jnp.logical_not(low), m0[x, at(m0, rows, 1), :] == 0)
        total = fine_flow(1, face, None, x, rows) + jnp.where(top, 2.0 * m1[x, at(m1, rows), :], 0.0)
        inverse1[x, at(inverse1, rows), :] = one_over(total)


def coarse_faces(m0, m1, face, inverse0, inverse1):
    planes, width = face.shape[1], face.shape[3]
    rows = FACE_ROWS
    here = at(face, rows)
    lane = lanes((rows[1] - rows[0], width))
    for i in range(planes):
        u = m0[i, here, :]
        sides = walls(coarse_sides(m1, i, coarse_low(0, width, rows), rows), lane < 2, lane >= width - 2)
        terms = []
        for a, side in enumerate(sides):
            value = mean_any(u, side)
            face[a, i, here, :] = value
            terms.append(value)
        inverse0[i, here, :] = one_over(add_up(terms) + jnp.where(sides[1] == 0, 2.0 * u, 0.0))
    rows = wider(rows, -1)
    for i in range(planes):
        top = jnp.where(m0[i, at(m0, rows, 1), :] == 0, 2.0 * m1[i, at(m1, rows), :], 0.0)
        inverse1[i, at(inverse1, rows), :] = one_over(coarse_flow(1, face, None, i, rows) + top)


def neighbour_rows(columns):
    near = jnp.where(slab_index(columns) % 2 == 0, 2 * ROWS, 0)
    return pl.multiple_of(near, ROWS), pl.multiple_of(2 * ROWS - near, ROWS)


def unfold_slabs(places, arrays, planes):
    def unfold(i, _):
        for ref, start, at in places:
            for first, store in arrays:
                tiles = [ref[4 * i + j, start + first : start + first + ROWS, :] for j in range(4)]
                for j, tile in enumerate(swap_blocks(tiles)):
                    store(4 * i + j, at, tile)
        return 0

    lax.fori_loop(0, planes // 4, unfold, 0, unroll=True)


def plain_store(ref):
    def store(x, row, tile):
        ref[x, pl.ds(row, ROWS), :] = tile

    return store


def scaled_store(ref, factor):
    def store(x, row, tile):
        part = pl.ds(row, ROWS)
        ref[x, part, :] = tile * factor[x, part, :]

    return store


def pair_sum(ref):
    return ref[ROWS : 2 * ROWS, :] + ref[ROWS + 1 : 2 * ROWS + 1, :]


def picked(width):
    row = lax.broadcasted_iota(jnp.int32, (ROWS, width), 0)
    return jnp.logical_and(row % 2 == 0, lanes((ROWS, width)) % 4 == row // 2)


def weights_kernel(
    columns,
    own, near, far,
    face, inverse0, inverse1, cface, cinverse0, cinverse1, coarsest,
    m0, m1, cm0, cm1, rest,
):
    planes, width = face.shape[1], face.shape[3]
    near_at, far_at = neighbour_rows(columns)
    places = ((own, 0, ROWS), (near, 0, near_at), (far, 0, far_at))
    unfold_slabs(places, ((0, plain_store(m0)), (ROWS, plain_store(m1))), planes)
    fine_faces(m0, m1, face, inverse0, inverse1)
    even = coarse_low(0, width, (0, WIN))
    for i in range(planes // 4):
        mobilities = []
        for x in (4 * i, 4 * i + 2):
            mass = (m0[x] + m1[x]) + (m0[x + 1] + m1[x + 1])
            mobilities.append(0.125 * (mass + swap_lanes(mass, 1)))
        cm0[i] = jnp.where(even, mobilities[0], mobilities[1])
        cm1[i] = jnp.where(even, mobilities[1], mobilities[0])
    coarse_faces(cm0, cm1, cface, cinverse0, cinverse1)
    pick = picked(width)
    for i in range(planes // 4):
        rest[...] = cm0[i] + cm1[i]
        pair = pair_sum(rest)
        pair = 0.125 * (pair + swap_lanes(pair, 2))
        coarsest[i : i + 1, :] = jnp.sum(jnp.where(pick, pair, 0.0), axis=0, keepdims=True)


def down_kernel(
    columns,
    face, inverse0, inverse1, cface, cinverse0, cinverse1, coarsest,
    own, near, far,
    *refs,
):
    state, cstate, message_hbm, packed_hbm = refs[:4]
    scaled0, scaled1, cscaled0, cscaled1, v0, v1, e0, e1, rest, message, packed, done = refs[4:]
    planes, width = face.shape[1], face.shape[3]
    coarse = planes // 4
    middle = slice(*INNER)
    held = [(face.at[:, :, middle, :], state.at[0:6])]
    held += [(ref.at[:, middle, :], state.at[6 + k]) for k, ref in enumerate((inverse0, inverse1, scaled0, scaled1, v1))]
    held += [(cface, cstate.at[0:6])]
    held += [(ref, cstate.at[6 + k]) for k, ref in enumerate((cinverse0, cinverse1, cscaled0, cscaled1, e1))]
    held += [(message, message_hbm)]
    copies = [pltpu.make_async_copy(ref, out, done.at[k]) for k, (ref, out) in enumerate(held)]
    for copy in copies[:3] + copies[6:9]:
        copy.start()
    near_at, far_at = neighbour_rows(columns)
    places = ((own, 2 * ROWS, ROWS), (near, 2 * ROWS, near_at), (far, 0, far_at))
    arrays = (
        (0, scaled_store(scaled0, inverse0)),
        (ROWS, scaled_store(scaled1, inverse1)),
        (2 * ROWS, plain_store(v1)),
    )
    unfold_slabs(places, arrays, planes)
    for copy in copies[3:5]:
        copy.start()

    renew(fine_flow, 0, v0, v1, face, inverse0, scaled0, (1, WIN - 1))
    renew(fine_flow, 1, v1, v0, face, inverse1, scaled1, (2, WIN - 2))
    renew(fine_flow, 0, v0, v1, face, inverse0, scaled0, (3, WIN - 3))
    renew(fine_flow, 1, v1, v0, face, inverse1, scaled1, (3, WIN - 3))
    copies[5].start()

    even = coarse_low(0, width, INNER)
    for i in range(coarse):
        fields = []
        for x in (4 * i, 4 * i + 2):
            total = rest_of(fine_flow, v0, v1, face, inverse0, scaled0, x, INNER)
            total = total + rest_of(fine_flow, v0, v1, face, inverse0, scaled0, x + 1, INNER)
            fields.append(0.5 * (total + swap_lanes(total, 1)))
        first = jnp.where(even, fields[0], fields[1]) * cinverse0[i, middle, :]
        cscaled0[i, middle, :] = first
        e0[i, middle, :] = first
        cscaled1[i, middle, :] = jnp.where(even, fields[1], fields[0]) * cinverse1[i, middle, :]
    for copy in copies[9:11]:
        copy.start()

    renew(coarse_flow, 1, e1, e0, cface, cinverse1, cscaled1, wider(INNER, -1))
    renew(coarse_flow, 0, e0, e1, cface, cinverse0, cscaled0, wider(INNER, -2))
    renew(coarse_flow, 1, e1, e0, cface, cinverse1, cscaled1, wider(OWN, 1))
    copies[11].start()

    pick = picked(width)
    for i in range(coarse):
        rest[slice(*OWN), :] = rest_of(coarse_flow, e0, e1, cface, cinverse0, cscaled0, i, OWN)
        pair = pair_sum(rest)
        pair = 0.5 * (pair + swap_lanes(pair, 2))
        packed[0, i : i + 1, :] = jnp.sum(jnp.where(pick, pair, 0.0), axis=0, keepdims=True)
    packed[0, coarse : 2 * coarse, :] = coarsest[...]
    tile = packed[0]
    for device in range(1, packed.shape[0]):
        packed[device] = tile
    sent = pltpu.make_async_copy(packed, packed_hbm, done.at[13])
    sent.start()

    first = lanes((ROWS, width)) % 2 == 0
    here = slice(*OWN)
    for i in range(coarse):
        message[i, 0:ROWS, :] = jnp.where(first, e1[i, here, :], cscaled0[i, here, :])
        message[i, ROWS : 2 * ROWS, :] = cscaled1[i, here, :]
    copies[12].start()
    for copy in copies:
        copy.wait()
    sent.wait()


def up_kernel(
    columns,
    gathered, state, cstate_hbm, near_hbm, far_hbm,
    out,
    cstate, v0, v1, e0, near, far, bshare, coarsest, spread, done,
):
    planes, width = state.shape[1], state.shape[3]
    count = gathered.shape[0]
    rows = planes // 4
    face, (inverse0, inverse1, scaled0, scaled1, field1) = state, [state.at[k] for k in range(6, 11)]
    cface, (cinverse0, cinverse1, cscaled0, cscaled1, e1) = cstate, [cstate.at[k] for k in range(6, 11)]
    held = ((cstate_hbm, cstate), (near_hbm, near), (far_hbm, far))
    copies = [pltpu.make_async_copy(hbm, ref, done.at[k]) for k, (hbm, ref) in enumerate(held)]
    for copy in copies:
        copy.start()

    slab = slab_index(columns)
    lane = lanes((rows, width))
    part = lane % 4
    sources, mobilities = [], []
    for w in range(-REACH, REACH + 1):
        other = slab + w
        inside = jnp.logical_and(other >= 0, other < count)
        device = device_of(jnp.clip(other, 0, count - 1), columns)
        keep = jnp.where(inside, 1.0, 0.0)
        for part_of, into in ((slice(0, rows), sources), (slice(rows, 2 * rows), mobilities)):
            tile = gathered[device, part_of, :] * keep
            for z in range(4):
                v = jnp.where(part == z, tile, 0.0)
                v = v + swap_lanes(v, 1)
                into.append(v + swap_lanes(v, 2))

    parity = (lax.broadcasted_iota(jnp.int32, (rows, width), 0) + lane // 4) % 2
    pairs = len(sources) // 2
    zero = jnp.zeros((rows, width), jnp.float32)
    low = (parity == 0, parity == 1)

    def coloured(planes_of):
        first = [jnp.where(low[0], planes_of[2 * k], planes_of[2 * k + 1]) for k in range(pairs)]
        second = [jnp.where(low[0], planes_of[2 * k + 1], planes_of[2 * k]) for k in range(pairs)]
        return [zero] + first + [zero], [zero] + second + [zero]

    source, mobility = coloured(sources), coloured(mobilities)
    row = lax.broadcasted_iota(jnp.int32, (rows, width), 0)
    scaled = ([], [])
    for k in range(pairs):
        for colour in (0, 1):
            sides = around_coarsest(mobility[1 - colour], k, low[colour])
            sides = (jnp.where(row == 0, 0.0, sides[0]), jnp.where(row == rows - 1, 0.0, sides[1])) + sides[2:]
            sides = walls(sides, lane < 4, lane >= width - 4)
            top = jnp.logical_and(jnp.logical_not(low[colour]), sides[5] == 0)
            shares, inverse, _ = weights(mean_any, mobility[colour][k + 1], sides, top)
            for a in range(6):
                bshare[colour, a, k] = shares[a]
            scaled[colour].append(source[colour][k + 1] * inverse)

    fields = [[zero] + scaled[0] + [zero], None]
    for step in range(1, 2 * BOTTOM_SWEEPS):
        colour = step % 2
        new = []
        for k in range(pairs):
            sides = around_coarsest(fields[1 - colour], k, low[colour])
            new.append(relax(scaled[colour][k], [bshare[colour, a, k] for a in range(6)], sides))
        fields[colour] = [zero] + new + [zero]

    start = 4 * REACH - ROWS // 2
    for k in range(WIN // 4):
        a, b = fields[0][start // 2 + k + 1], fields[1][start // 2 + k + 1]
        coarsest[2 * k * rows : (2 * k + 1) * rows, :] = jnp.where(low[0], a, b)
        coarsest[(2 * k + 1) * rows : (2 * k + 2) * rows, :] = jnp.where(low[0], b, a)

    for copy in copies:
        copy.wait()
    near_at, far_at = neighbour_rows(columns)
    here = slice(*OWN)
    first = lanes((ROWS, width)) % 2 == 0
    for i in range(rows):
        half = coarsest[pl.ds(i, WIN // 2, stride=rows), :]
        spread[pl.ds(0, WIN // 2, stride=2), :] = half
        spread[pl.ds(1, WIN // 2, stride=2), :] = half
        e1[i, here, :] = e1[i, here, :] + spread[here, :]
        for row, ref in ((near_at, near), (far_at, far)):
            mixed = ref[i, 0:ROWS, :]
            other = swap_lanes(mixed, 1)
            part = pl.ds(row, ROWS)
            e1[i, part, :] = jnp.where(first, mixed, other) + spread[part, :]
            cscaled0[i, part, :] = jnp.where(first, other, mixed)
            cscaled1[i, part, :] = ref[i, ROWS : 2 * ROWS, :]

    renew(coarse_flow, 0, e0, e1, cface, cinverse0, cscaled0, (1, WIN - 1))
    renew(coarse_flow, 1, e1, e0, cface, cinverse1, cscaled1, (2, WIN - 2))
    renew(coarse_flow, 0, e0, e1, cface, cinverse0, cscaled0, (3, WIN - 3))
    renew(coarse_flow, 1, e1, e0, cface, cinverse1, cscaled1, INNER)

    even = coarse_low(0, width, INNER)
    for i in range(rows):
        a, b = e0[i, at(e0, INNER), :], e1[i, at(e1, INNER), :]
        for half, add in ((0, jnp.where(even, a, b)), (1, jnp.where(even, b, a))):
            for x in (4 * i + 2 * half, 4 * i + 2 * half + 1):
                v1[x] = field1[x] + add

    renew(fine_flow, 0, v0, v1, face, inverse0, scaled0, wider(INNER, -1))
    renew(fine_flow, 1, v1, v0, face, inverse1, scaled1, wider(INNER, -2))
    renew(fine_flow, 0, v0, v1, face, inverse0, scaled0, wider(OWN, 1))
    renew(fine_flow, 1, v1, v0, face, inverse1, scaled1, wider(OWN, 1))

    for i in range(rows):
        planes_of = range(4 * i, 4 * i + 4)
        rest = [rest_of(fine_flow, v0, v1, face, inverse0, scaled0, x, OWN) for x in planes_of]
        for a, tiles in (
            (0, [v0[x, at(v0, OWN), :] for x in planes_of]),
            (1, [v1[x, at(v1, OWN), :] for x in planes_of]),
            (2, rest),
        ):
            for j, tile in enumerate(swap_blocks(tiles)):
                out[4 * i + j, a * ROWS : (a + 1) * ROWS, :] = tile


def local_slabs(shape, right_side, phase, pressure_guess):
    across, columns = shape
    count = across * columns
    bx, by, length = right_side.shape
    planes, width = across * bx, columns * by
    f32 = jnp.float32
    order = place_of(across, columns)
    path = sorted(range(count), key=lambda device: order[device])
    near = [pair for k in range(0, count, 2) for pair in ((path[k], path[k + 1]), (path[k + 1], path[k]))]
    far = [pair for k in range(1, count - 1, 2) for pair in ((path[k], path[k + 1]), (path[k + 1], path[k]))]
    axes = ("gx", "yz")
    cost = pl.CostEstimate(flops=20_000_000_000, bytes_accessed=100_000_000, transcendentals=0)
    params = pltpu.CompilerParams(vmem_limit_bytes=20 * 1024 * 1024)

    def struct(*dims):
        return jax.ShapeDtypeStruct(dims, f32)

    def vmem(*dims):
        return pltpu.VMEM(dims, f32)

    bricks = pl.pallas_call(
        functools.partial(pack_kernel, order),
        in_specs=[pl.BlockSpec(memory_space=pltpu.HBM)] * 3,
        out_shape=struct(count, 5 * ROWS, 128),
        scratch_shapes=[
            vmem(bx, by, length),
            pltpu.VMEM((bx, by, length), phase.dtype),
            vmem(bx, by, length),
            vmem(3, length, 128),
            pltpu.SemaphoreType.DMA((3,)),
        ],
        compiler_params=params,
        name="pack",
    )(*(pltpu.with_memory_space_constraint(x, pltpu.HBM) for x in (right_side, phase, pressure_guess)))
    own = lax.all_to_all(bricks, axes, 0, 0)
    mobility, fields = own[:, : 2 * ROWS], own[:, 2 * ROWS :]
    mobility_far = lax.ppermute(mobility, axes, far)
    own_near = lax.ppermute(own, axes, near)
    fields_far = lax.ppermute(fields, axes, far)

    coarse = planes // 4
    face, plane = (6, planes, WIN, width), (planes, WIN, width)
    cface, cplane = (6, coarse, WIN, width), (coarse, WIN, width)
    height = INNER[1] - INNER[0]
    iplane = (planes, height, width)
    letter = (coarse, 2 * ROWS, width)

    def in_hbm(*arrays):
        return [pltpu.with_memory_space_constraint(x, pltpu.HBM) for x in arrays]

    def far_outs(*shapes):
        return [pltpu.HBM(dims, f32) for dims in shapes], [pl.BlockSpec(memory_space=pltpu.HBM)] * len(shapes)

    def near_outs(*shapes):
        return [struct(*dims) for dims in shapes], [pl.BlockSpec(memory_space=pltpu.VMEM)] * len(shapes)

    made = pl.pallas_call(
        functools.partial(weights_kernel, columns),
        out_shape=near_outs(face, plane, plane, cface, cplane, cplane, (coarse, width))[0],
        scratch_shapes=[vmem(*plane)] * 2 + [vmem(*cplane)] * 2 + [vmem(WIN, width)],
        compiler_params=params,
        cost_estimate=cost,
        name="weights",
    )(own, own_near, mobility_far)

    first = near_outs((11, planes, height, width))
    second = far_outs((11, coarse, WIN, width), letter, (count, 2 * coarse, width))
    state, cstate, message, packed = pl.pallas_call(
        functools.partial(down_kernel, columns),
        out_shape=first[0] + second[0],
        out_specs=first[1] + second[1],
        scratch_shapes=[vmem(*plane)] * 2 + [vmem(*cplane)] * 2 + [vmem(*plane)] * 2 + [vmem(*cplane)] * 2 + [
            vmem(WIN, width),
            vmem(*letter),
            vmem(count, 2 * coarse, width),
            pltpu.SemaphoreType.DMA((14,)),
        ],
        compiler_params=params,
        name="down",
    )(*made, own, own_near, fields_far)
    gathered = lax.all_to_all(packed, axes, 0, 0)
    message_far = lax.ppermute(message, axes, far)
    message_near = lax.ppermute(message, axes, near)

    cycle = pl.pallas_call(
        functools.partial(up_kernel, columns),
        out_shape=struct(count, 3 * ROWS, 128),
        in_specs=[pl.BlockSpec(memory_space=pltpu.VMEM)] * 2 + [pl.BlockSpec(memory_space=pltpu.HBM)] * 3,
        scratch_shapes=[vmem(11, *cplane)] + [vmem(*iplane)] * 2 + [vmem(*cplane)] + [vmem(*letter)] * 2 + [
            vmem(2, 6, 2 * (2 * REACH + 1), coarse, width),
            vmem(WIN // 2 * coarse, width),
            vmem(WIN, width),
            pltpu.SemaphoreType.DMA((3,)),
        ],
        compiler_params=params,
        name="up",
    )(gathered, state, *in_hbm(cstate, message_near, message_far))
    back = lax.all_to_all(cycle, axes, 0, 0)
    return pl.pallas_call(
        functools.partial(unpack_kernel, order),
        out_shape=[struct(bx, by, length)] * 2,
        scratch_shapes=[vmem(2, length, 128)],
        compiler_params=params,
        name="unpack",
    )(back)


def solution(mesh):
    spec = P("gx", "yz", None)
    shape = (mesh.shape["gx"], mesh.shape["yz"])

    def cycle(right_side, phase, pressure_guess):
        bx, by, length = right_side.shape
        slabs = (bx, by, shape[1]) == (4, 32, 4) and length == 2 * ROWS * shape[0] * shape[1]
        if slabs and shape[0] == 8:
            return local_slabs(shape, right_side, phase, pressure_guess)
        return local(right_side, phase, pressure_guess)

    return jax.shard_map(cycle, mesh=mesh, in_specs=(spec,) * 3, out_specs=(spec,) * 2, check_vma=False)
```

```python
import functools

import jax
import jax.numpy as jnp
from jax import lax
from jax.experimental import pallas as pl
from jax.experimental.pallas import tpu as pltpu
from jax.sharding import PartitionSpec as P

SWEEPS = 2
BOTTOM_SWEEPS = 4


def with_halo(x, sides, width):
    for axis, dim in sides:
        size, length = (lax.axis_size(axis), x.shape[dim])
        up = [(i, (i + 1) % size) for i in range(size - 1)]
        down = [(j, i) for i, j in up]
        last = lax.slice_in_dim(x, length - width, length, axis=dim)
        first = lax.slice_in_dim(x, 0, width, axis=dim)
        before = lax.ppermute(last, axis, up)
        after = lax.ppermute(first, axis, down)
        x = jnp.concatenate([before, x, after], axis=dim)
    return x


def harmonic(left, right):
    total = left + right
    safe = jnp.where(total > 0, total, 1.0)
    return jnp.where(total > 0, 2.0 * left * right / safe, 0.0)


def coefficients(padded):
    faces_x = harmonic(padded[1:], padded[:-1])
    faces_y = harmonic(padded[:, 1:], padded[:, :-1])
    centre = padded[1:-1, 1:-1]
    faces_z = harmonic(centre[:, :, 1:], centre[:, :, :-1])
    zero_plane = jnp.zeros_like(centre[:, :, :1])
    x_lower = faces_x[:-1, 1:-1]
    x_upper = faces_x[1:, 1:-1]
    y_lower = faces_y[1:-1, :-1]
    y_upper = faces_y[1:-1, 1:]
    z_lower = jnp.concatenate([zero_plane, faces_z], axis=2)
    z_upper = jnp.concatenate([faces_z, 2.0 * centre[:, :, -1:]], axis=2)
    diagonal = x_lower + x_upper + y_lower + y_upper + z_lower + z_upper
    diagonal = jnp.where(diagonal > 0, diagonal, 1.0)
    return (x_lower, x_upper, y_lower, y_upper, z_lower, z_upper, diagonal)


def shrink(coeffs):
    return tuple((item[1:-1, 1:-1] for item in coeffs))


def parity_of(extent, start_x, start_y):
    index_x = lax.broadcasted_iota(jnp.int32, extent, 0) + start_x
    index_y = lax.broadcasted_iota(jnp.int32, extent, 1) + start_y
    index_z = lax.broadcasted_iota(jnp.int32, extent, 2)
    return (index_x + index_y + index_z) % 2


def neighbours(padded, coeffs):
    centre = padded[1:-1, 1:-1]
    zero_plane = jnp.zeros_like(centre[:, :, :1])
    lower_z = jnp.concatenate([zero_plane, centre[:, :, :-1]], axis=2)
    upper_z = jnp.concatenate([centre[:, :, 1:], zero_plane], axis=2)
    beside_all = coeffs[0] * padded[:-2, 1:-1] + coeffs[1] * padded[2:, 1:-1]
    beside_all = beside_all + coeffs[2] * padded[1:-1, :-2] + coeffs[3] * padded[1:-1, 2:]
    beside_all = beside_all + coeffs[4] * lower_z + coeffs[5] * upper_z
    return (beside_all, centre)


def colour_pass(padded, source, coeffs, parity, colour):
    beside_all, centre = neighbours(padded, coeffs)
    updated = (source + beside_all) / coeffs[6]
    return jnp.where(parity == colour, updated, centre)


def residual_of(padded, source, coeffs):
    beside_all, centre = neighbours(padded, coeffs)
    return source - (coeffs[6] * centre - beside_all)


def restrict_sum(field):
    size_x, size_y, size_z = field.shape
    return 0.5 * field.reshape(size_x // 2, 2, size_y // 2, 2, size_z // 2, 2).sum(axis=(1, 3, 5))


def restrict_mean(field):
    size_x, size_y, size_z = field.shape
    return 0.125 * field.reshape(size_x // 2, 2, size_y // 2, 2, size_z // 2, 2).sum(axis=(1, 3, 5))


def inject(field):
    return jnp.repeat(jnp.repeat(jnp.repeat(field, 2, axis=0), 2, axis=1), 2, axis=2)


def rim_one(field):
    return with_halo(field, (("gx", 0), ("yz", 1)), 1)


def rim_two(field):
    return with_halo(field, (("gx", 0), ("yz", 1)), 2)


def offsets(field):
    return (lax.axis_index("gx") * field.shape[0], lax.axis_index("yz") * field.shape[1])


def prepare_plain(mobility):
    start_x, start_y = offsets(mobility)
    return (coefficients(rim_one(mobility)), parity_of(mobility.shape, start_x, start_y))


def prepare(mobility):
    start_x, start_y = offsets(mobility)
    size_x, size_y, size_z = mobility.shape
    region = coefficients(rim_two(mobility))
    loop_parity = parity_of((size_x + 2, size_y + 2, size_z), start_x - 1, start_y - 1)
    operator_set = (
        shrink(region),
        parity_of(mobility.shape, start_x, start_y),
        region,
        loop_parity,
    )
    return operator_set


def smooth_plain(field, source, operator_set, sweeps, rim):
    coeffs = operator_set[0]
    parity = operator_set[1]
    for _ in range(sweeps):
        field = colour_pass(rim(field), source, coeffs, parity, 0)
        field = colour_pass(rim(field), source, coeffs, parity, 1)
    return field


def smooth(field, source, operator_set, sweeps):
    interior, parity, region, loop_parity = operator_set
    source_loop = rim_one(source)
    for _ in range(sweeps):
        loop_field = colour_pass(rim_two(field), source_loop, region, loop_parity, 0)
        field = colour_pass(loop_field, source, interior, parity, 1)
    return field


def local(right_side, phase, pressure_guess):
    mobility = 1.0 + 999.0 * phase.astype(jnp.float32)
    level_zero = prepare(mobility)
    pressure = smooth(pressure_guess, right_side, level_zero, SWEEPS)
    fine_res = residual_of(rim_one(pressure), right_side, level_zero[0])
    source_one = restrict_sum(fine_res)
    mobility_one = restrict_mean(mobility)
    level_one = prepare(mobility_one)
    coarse_one = smooth(jnp.zeros_like(source_one), source_one, level_one, SWEEPS)
    res_one = residual_of(rim_one(coarse_one), source_one, level_one[0])
    source_two = restrict_sum(res_one)
    mobility_two = restrict_mean(mobility_one)
    level_two = prepare_plain(mobility_two)
    coarse_two = smooth_plain(
        jnp.zeros_like(source_two), source_two, level_two, BOTTOM_SWEEPS, rim_one
    )
    coarse_one = smooth(coarse_one + inject(coarse_two), source_one, level_one, SWEEPS)
    pressure = smooth(pressure + inject(coarse_one), right_side, level_zero, SWEEPS)
    residual = residual_of(rim_one(pressure), right_side, level_zero[0])
    return (pressure, residual)


ROWS = 8
WIN = 3 * ROWS
REACH = 3
MIX = 2.0 / 1001.0


def place_of(rows, columns):
    slab = []
    for g in range(rows):
        a = (g // 2) * 2 + ((g % 2) ^ ((g // 2) % 2))
        slab += [a * columns + (j if a % 2 == 0 else columns - 1 - j) for j in range(columns)]
    return slab


def slab_index(columns):
    g, j = lax.axis_index("gx"), lax.axis_index("yz")
    a = (g // 2) * 2 + (g + g // 2) % 2
    return a * columns + jnp.where(a % 2 == 0, j, columns - 1 - j)


def device_of(slab, columns):
    a, b = slab // columns, slab % columns
    g = (a // 2) * 2 + (a + a // 2) % 2
    return g * columns + jnp.where(a % 2 == 0, b, columns - 1 - b)


def lanes(shape):
    return lax.broadcasted_iota(jnp.int32, shape, len(shape) - 1)


def swap_lanes(v, step):
    width = v.shape[-1]
    up, down = pltpu.roll(v, step, 1), pltpu.roll(v, width - step, 1)
    return jnp.where((lanes(v.shape) // step) % 2 == 0, down, up)


def swap_blocks(tiles):
    block = lanes(tiles[0].shape) // 32
    at = [block == b for b in range(3)]

    def choose(four):
        return jnp.where(at[0], four[0], jnp.where(at[1], four[1], jnp.where(at[2], four[2], four[3])))

    turned = [choose([tiles[(b + d) % 4] for b in range(4)]) for d in range(4)]
    turned = [turned[0]] + [pltpu.roll(turned[d], 32 * d, 1) for d in (1, 2, 3)]
    return [choose([turned[(b - a) % 4] for b in range(4)]) for a in range(4)]


def brick_parity(shape):
    lane = lanes(shape)
    return (lane // 32 + lane) % 2


def pack_kernel(order, source_hbm, phase_hbm, guess_hbm, out_ref, source_ref, phase_ref, guess_ref, turned, arrived):
    copies = [
        pltpu.make_async_copy(hbm, ref, arrived.at[a])
        for a, (hbm, ref) in enumerate(((source_hbm, source_ref), (phase_hbm, phase_ref), (guess_hbm, guess_ref)))
    ]
    for copy in copies:
        copy.start()
    for a, ref in enumerate((source_ref, phase_ref, guess_ref)):
        copies[a].wait()
        brick = ref[...].reshape(128, ref.shape[2])
        if a == 1:
            brick = 1.0 + 999.0 * brick.astype(jnp.float32)
        turned[a] = brick.T
    even = brick_parity((ROWS, 128)) == 0
    for device, slab in enumerate(order):
        base = 2 * ROWS * slab
        for a, row in ((1, 0), (2, ROWS), (0, 3 * ROWS)):
            low = turned[a, pl.ds(base, ROWS, stride=2), :]
            high = turned[a, pl.ds(base + 1, ROWS, stride=2), :]
            if a != 2:
                out_ref[device, row : row + ROWS, :] = jnp.where(even, low, high)
            out_ref[device, row + ROWS : row + 2 * ROWS, :] = jnp.where(even, high, low)


def unpack_kernel(order, in_ref, pressure_ref, residual_ref, turned):
    even = brick_parity((ROWS, 128)) == 0
    for device, slab in enumerate(order):
        base = 2 * ROWS * slab
        p0, p1 = in_ref[device, 0:ROWS, :], in_ref[device, ROWS : 2 * ROWS, :]
        r0 = in_ref[device, 2 * ROWS : 3 * ROWS, :]
        turned[0, pl.ds(base, ROWS, stride=2), :] = jnp.where(even, p0, p1)
        turned[0, pl.ds(base + 1, ROWS, stride=2), :] = jnp.where(even, p1, p0)
        turned[1, pl.ds(base, ROWS, stride=2), :] = jnp.where(even, r0, 0.0)
        turned[1, pl.ds(base + 1, ROWS, stride=2), :] = jnp.where(even, 0.0, r0)
    for a, ref in enumerate((pressure_ref, residual_ref)):
        ref[...] = turned[a].T.reshape(ref.shape)


FACE_ROWS = (1, WIN - 1)
INNER = (ROWS // 2, WIN - ROWS // 2)
OWN = (ROWS, 2 * ROWS)


def wider(rows, by):
    return (rows[0] - by, rows[1] + by)


def at(ref, rows, by=0):
    start = (WIN - ref.shape[-2]) // 2
    return slice(rows[0] - start + by, rows[1] - start + by)


def beyond(ref, i, low, rows, *lead):
    return jnp.where(low, ref[(*lead, i, at(ref, rows, -1))], ref[(*lead, i, at(ref, rows, 1))])


def add_up(terms):
    while len(terms) > 1:
        terms = [sum(terms[k : k + 2]) for k in range(0, len(terms), 2)]
    return terms[0]


def around_coarsest(planes, k, low):
    centre = planes[k + 1]
    rows, width = centre.shape
    return (
        pltpu.roll(centre, 1, 0),
        pltpu.roll(centre, rows - 1, 0),
        pltpu.roll(centre, 4, 1),
        pltpu.roll(centre, width - 4, 1),
        centre,
        jnp.where(low, planes[k], planes[k + 2]),
    )


def walls(sides, first, last):
    return sides[:2] + (jnp.where(first, 0.0, sides[2]), jnp.where(last, 0.0, sides[3])) + sides[4:]


def mean_fine(u, w):
    return jnp.where(u == w, u, (u * MIX) * w)


def mean_any(u, w):
    total = u + w
    return 2.0 * u * w / jnp.where(total > 0, total, 1.0)


def weights(mean, u, sides, top):
    faces = [mean(u, w) for w in sides]
    diagonal = (faces[0] + faces[1]) + (faces[2] + faces[3]) + (faces[4] + faces[5])
    diagonal = diagonal + jnp.where(top, 2.0 * u, 0.0)
    diagonal = jnp.where(diagonal > 0, diagonal, 1.0)
    inverse = 1.0 / diagonal
    return [face * inverse for face in faces], inverse, diagonal


def relax(scaled, share, sides):
    parts = [share[a] * sides[a] for a in range(6)]
    return scaled + ((parts[0] + parts[1]) + (parts[2] + parts[3]) + (parts[4] + parts[5]))


def fine_low(x, colour, width, rows):
    return (lanes((rows[1] - rows[0], width)) + (x + colour) % 2) % 2 == 0


def coarse_low(colour, width, rows):
    shape = (rows[1] - rows[0], width)
    row = lax.broadcasted_iota(jnp.int32, shape, 0) + rows[0]
    return (row + lanes(shape) // 2 + colour) % 2 == 0


def loader(v, rows):
    seen = {}

    def load(x):
        if x not in seen:
            seen[x] = v[x, at(v, rows), :]
        return seen[x]

    return load


def fine_sides(v, load, x, low, rows):
    centre = load(x)
    width = centre.shape[1]
    return (
        load(x - 1) if x > 0 else None,
        load(x + 1) if x + 1 < v.shape[0] else None,
        pltpu.roll(centre, 1, 1),
        pltpu.roll(centre, width - 1, 1),
        centre,
        beyond(v, x, low, rows),
    )


def fine_flow(colour, face, v, x, rows, load=None):
    planes, width = face.shape[1], face.shape[3]
    part = at(face, rows)
    low = fine_low(x, colour, width, rows)
    if v is not None and load is None:
        load = loader(v, rows)
    if colour == 0:
        sides = fine_sides(v, load, x, low, rows)
        return add_up([face[a, x, part, :] * side for a, side in enumerate(sides) if side is not None])

    def carried(a, plane):
        values = face[a, plane, part, :]
        return values if v is None else values * load(plane)

    away = beyond(face, x, low, rows, 5)
    terms = [
        pltpu.roll(carried(3, x), 1, 1),
        pltpu.roll(carried(2, x), width - 1, 1),
        carried(4, x),
        away if v is None else away * beyond(v, x, low, rows),
    ]
    if x > 0:
        terms.append(carried(1, x - 1))
    if x + 1 < planes:
        terms.append(carried(0, x + 1))
    return add_up(terms)


def coarse_sides(v, i, low, rows):
    here = at(v, rows)
    centre = v[i, here, :]
    width = centre.shape[1]
    below = v[i - 1, here, :] if i > 0 else jnp.zeros_like(centre)
    above = v[i + 1, here, :] if i + 1 < v.shape[0] else jnp.zeros_like(centre)
    return (
        v[i, at(v, rows, -1), :],
        v[i, at(v, rows, 1), :],
        pltpu.roll(centre, 2, 1),
        pltpu.roll(centre, width - 2, 1),
        centre,
        jnp.where(low, below, above),
    )


def coarse_flow(colour, face, v, i, rows, load=None):
    planes, width = face.shape[1], face.shape[3]
    low = coarse_low(colour, width, rows)
    if colour == 0:
        sides = coarse_sides(v, i, low, rows)
        return add_up([face[a, i, at(face, rows), :] * side for a, side in enumerate(sides)])

    def carried(a, plane, by=0):
        values = face[a, plane, at(face, rows, by), :]
        return values if v is None else values * v[plane, at(v, rows, by), :]

    centre = carried(4, i)
    below = carried(5, i - 1) if i > 0 else jnp.zeros_like(centre)
    above = carried(5, i + 1) if i + 1 < planes else jnp.zeros_like(centre)
    return add_up(
        [
            carried(1, i, -1),
            carried(0, i, 1),
            pltpu.roll(carried(3, i), 2, 1),
            pltpu.roll(carried(2, i), width - 2, 1),
            centre,
            jnp.where(low, below, above),
        ]
    )


def renew(flow, colour, target, other, face, inverse, scaled, rows):
    load = loader(other, rows)
    for x in range(face.shape[1]):
        moved = inverse[x, at(inverse, rows), :] * flow(colour, face, other, x, rows, load)
        target[x, at(target, rows), :] = scaled[x, at(scaled, rows), :] + moved


def rest_of(flow, v0, v1, face, inverse0, scaled0, x, rows):
    factor = inverse0[x, at(inverse0, rows), :]
    updated = scaled0[x, at(scaled0, rows), :] + factor * flow(0, face, v1, x, rows)
    return (updated - v0[x, at(v0, rows), :]) / factor


def one_over(diagonal):
    return 1.0 / jnp.where(diagonal > 0, diagonal, 1.0)


def fine_faces(m0, m1, face, inverse0, inverse1):
    planes, width = face.shape[1], face.shape[3]
    rows = FACE_ROWS
    here = at(face, rows)
    lane = lanes((rows[1] - rows[0], width))
    load = loader(m1, rows)
    for x in range(planes):
        low = fine_low(x, 0, width, rows)
        u = m0[x, here, :]
        sides = walls(fine_sides(m1, load, x, low, rows), lane == 0, lane == width - 1)
        terms = []
        for a, side in enumerate(sides):
            value = jnp.zeros_like(u) if side is None else mean_fine(u, side)
            face[a, x, here, :] = value
            terms.append(value)
        top = jnp.logical_and(jnp.logical_not(low), sides[5] == 0)
        inverse0[x, here, :] = one_over(add_up(terms) + jnp.where(top, 2.0 * u, 0.0))
    rows = wider(rows, -1)
    for x in range(planes):
        low = fine_low(x, 1, width, rows)
        top = jnp.logical_and(jnp.logical_not(low), m0[x, at(m0, rows, 1), :] == 0)
        total = fine_flow(1, face, None, x, rows) + jnp.where(top, 2.0 * m1[x, at(m1, rows), :], 0.0)
        inverse1[x, at(inverse1, rows), :] = one_over(total)


def coarse_faces(m0, m1, face, inverse0, inverse1):
    planes, width = face.shape[1], face.shape[3]
    rows = FACE_ROWS
    here = at(face, rows)
    lane = lanes((rows[1] - rows[0], width))
    for i in range(planes):
        u = m0[i, here, :]
        sides = walls(coarse_sides(m1, i, coarse_low(0, width, rows), rows), lane < 2, lane >= width - 2)
        terms = []
        for a, side in enumerate(sides):
            value = mean_any(u, side)
            face[a, i, here, :] = value
            terms.append(value)
        inverse0[i, here, :] = one_over(add_up(terms) + jnp.where(sides[1] == 0, 2.0 * u, 0.0))
    rows = wider(rows, -1)
    for i in range(planes):
        top = jnp.where(m0[i, at(m0, rows, 1), :] == 0, 2.0 * m1[i, at(m1, rows), :], 0.0)
        inverse1[i, at(inverse1, rows), :] = one_over(coarse_flow(1, face, None, i, rows) + top)


def neighbour_rows(columns):
    near = jnp.where(slab_index(columns) % 2 == 0, 2 * ROWS, 0)
    return pl.multiple_of(near, ROWS), pl.multiple_of(2 * ROWS - near, ROWS)


def unfold_slabs(places, arrays, planes):
    def unfold(i, _):
        for ref, start, at in places:
            for first, store in arrays:
                tiles = [ref[4 * i + j, start + first : start + first + ROWS, :] for j in range(4)]
                for j, tile in enumerate(swap_blocks(tiles)):
                    store(4 * i + j, at, tile)
        return 0

    lax.fori_loop(0, planes // 4, unfold, 0, unroll=True)


def plain_store(ref):
    def store(x, row, tile):
        ref[x, pl.ds(row, ROWS), :] = tile

    return store


def scaled_store(ref, factor):
    def store(x, row, tile):
        part = pl.ds(row, ROWS)
        ref[x, part, :] = tile * factor[x, part, :]

    return store


def pair_sum(ref):
    return ref[ROWS : 2 * ROWS, :] + ref[ROWS + 1 : 2 * ROWS + 1, :]


def picked(width):
    row = lax.broadcasted_iota(jnp.int32, (ROWS, width), 0)
    return jnp.logical_and(row % 2 == 0, lanes((ROWS, width)) % 4 == row // 2)


def weights_kernel(
    columns,
    own, near, far,
    face, inverse0, inverse1, cface, cinverse0, cinverse1, coarsest, flow0,
    m0, m1, guess, cm0, cm1, rest,
):
    planes, width = face.shape[1], face.shape[3]
    near_at, far_at = neighbour_rows(columns)
    places = ((own, 0, ROWS), (near, 0, near_at), (far, 0, far_at))
    arrays = ((0, plain_store(m0)), (ROWS, plain_store(m1)), (2 * ROWS, plain_store(guess)))
    unfold_slabs(places, arrays, planes)
    fine_faces(m0, m1, face, inverse0, inverse1)
    flow0[...] = jnp.zeros(flow0.shape, jnp.float32)
    load = loader(guess, FACE_ROWS)
    for x in range(planes):
        flow0[x, slice(*FACE_ROWS), :] = fine_flow(0, face, guess, x, FACE_ROWS, load)
    even = coarse_low(0, width, (0, WIN))
    for i in range(planes // 4):
        mobilities = []
        for x in (4 * i, 4 * i + 2):
            mass = (m0[x] + m1[x]) + (m0[x + 1] + m1[x + 1])
            mobilities.append(0.125 * (mass + swap_lanes(mass, 1)))
        cm0[i] = jnp.where(even, mobilities[0], mobilities[1])
        cm1[i] = jnp.where(even, mobilities[1], mobilities[0])
    coarse_faces(cm0, cm1, cface, cinverse0, cinverse1)
    pick = picked(width)
    for i in range(planes // 4):
        rest[...] = cm0[i] + cm1[i]
        pair = pair_sum(rest)
        pair = 0.125 * (pair + swap_lanes(pair, 2))
        coarsest[i : i + 1, :] = jnp.sum(jnp.where(pick, pair, 0.0), axis=0, keepdims=True)


def down_kernel(
    columns,
    face, inverse0, inverse1, cface, cinverse0, cinverse1, coarsest, flow0,
    own, near, far,
    *refs,
):
    state, cstate, message_hbm, packed_hbm = refs[:4]
    scaled0, scaled1, cscaled0, cscaled1, v0, v1, e0, e1, rest, message, packed, done = refs[4:]
    planes, width = face.shape[1], face.shape[3]
    coarse = planes // 4
    middle = slice(*INNER)
    held = [(face.at[:, :, middle, :], state.at[0:6])]
    held += [(ref.at[:, middle, :], state.at[6 + k]) for k, ref in enumerate((inverse0, inverse1, scaled0, scaled1, v1))]
    held += [(cface, cstate.at[0:6])]
    held += [(ref, cstate.at[6 + k]) for k, ref in enumerate((cinverse0, cinverse1, cscaled0, cscaled1, e1))]
    held += [(message, message_hbm)]
    copies = [pltpu.make_async_copy(ref, out, done.at[k]) for k, (ref, out) in enumerate(held)]
    for copy in copies[:3] + copies[6:9]:
        copy.start()
    near_at, far_at = neighbour_rows(columns)
    places = ((own, 0, ROWS), (near, 3 * ROWS, near_at), (far, 0, far_at))

    def first_pass(x, row, tile):
        part = pl.ds(row, ROWS)
        factor = inverse0[x, part, :]
        scaled = tile * factor
        scaled0[x, part, :] = scaled
        v0[x, part, :] = scaled + flow0[x, part, :] * factor

    arrays = ((0, first_pass), (ROWS, scaled_store(scaled1, inverse1)))
    unfold_slabs(places, arrays, planes)
    for copy in copies[3:5]:
        copy.start()

    renew(fine_flow, 1, v1, v0, face, inverse1, scaled1, (2, WIN - 2))
    renew(fine_flow, 0, v0, v1, face, inverse0, scaled0, (3, WIN - 3))
    renew(fine_flow, 1, v1, v0, face, inverse1, scaled1, (3, WIN - 3))
    copies[5].start()

    even = coarse_low(0, width, INNER)
    for i in range(coarse):
        fields = []
        for x in (4 * i, 4 * i + 2):
            total = rest_of(fine_flow, v0, v1, face, inverse0, scaled0, x, INNER)
            total = total + rest_of(fine_flow, v0, v1, face, inverse0, scaled0, x + 1, INNER)
            fields.append(0.5 * (total + swap_lanes(total, 1)))
        first = jnp.where(even, fields[0], fields[1]) * cinverse0[i, middle, :]
        cscaled0[i, middle, :] = first
        e0[i, middle, :] = first
        cscaled1[i, middle, :] = jnp.where(even, fields[1], fields[0]) * cinverse1[i, middle, :]
    for copy in copies[9:11]:
        copy.start()

    renew(coarse_flow, 1, e1, e0, cface, cinverse1, cscaled1, wider(INNER, -1))
    renew(coarse_flow, 0, e0, e1, cface, cinverse0, cscaled0, wider(INNER, -2))
    renew(coarse_flow, 1, e1, e0, cface, cinverse1, cscaled1, wider(OWN, 1))
    copies[11].start()

    pick = picked(width)
    for i in range(coarse):
        rest[slice(*OWN), :] = rest_of(coarse_flow, e0, e1, cface, cinverse0, cscaled0, i, OWN)
        pair = pair_sum(rest)
        pair = 0.5 * (pair + swap_lanes(pair, 2))
        packed[0, i : i + 1, :] = jnp.sum(jnp.where(pick, pair, 0.0), axis=0, keepdims=True)
    packed[0, coarse : 2 * coarse, :] = coarsest[...]
    tile = packed[0]
    for device in range(1, packed.shape[0]):
        packed[device] = tile
    sent = pltpu.make_async_copy(packed, packed_hbm, done.at[13])
    sent.start()

    first = lanes((ROWS, width)) % 2 == 0
    here = slice(*OWN)
    for i in range(coarse):
        message[i, 0:ROWS, :] = jnp.where(first, e1[i, here, :], cscaled0[i, here, :])
        message[i, ROWS : 2 * ROWS, :] = cscaled1[i, here, :]
    copies[12].start()
    for copy in copies:
        copy.wait()
    sent.wait()


def up_kernel(
    columns,
    gathered, state, cstate_hbm, near_hbm, far_hbm,
    out,
    cstate, v0, v1, e0, near, far, bshare, coarsest, spread, done,
):
    planes, width = state.shape[1], state.shape[3]
    count = gathered.shape[0]
    rows = planes // 4
    face, (inverse0, inverse1, scaled0, scaled1, field1) = state, [state.at[k] for k in range(6, 11)]
    cface, (cinverse0, cinverse1, cscaled0, cscaled1, e1) = cstate, [cstate.at[k] for k in range(6, 11)]
    held = ((cstate_hbm, cstate), (near_hbm, near), (far_hbm, far))
    copies = [pltpu.make_async_copy(hbm, ref, done.at[k]) for k, (hbm, ref) in enumerate(held)]
    for copy in copies:
        copy.start()

    slab = slab_index(columns)
    lane = lanes((rows, width))
    part = lane % 4
    sources, mobilities = [], []
    for w in range(-REACH, REACH + 1):
        other = slab + w
        inside = jnp.logical_and(other >= 0, other < count)
        device = device_of(jnp.clip(other, 0, count - 1), columns)
        keep = jnp.where(inside, 1.0, 0.0)
        for part_of, into in ((slice(0, rows), sources), (slice(rows, 2 * rows), mobilities)):
            tile = gathered[device, part_of, :] * keep
            for z in range(4):
                v = jnp.where(part == z, tile, 0.0)
                v = v + swap_lanes(v, 1)
                into.append(v + swap_lanes(v, 2))

    parity = (lax.broadcasted_iota(jnp.int32, (rows, width), 0) + lane // 4) % 2
    pairs = len(sources) // 2
    zero = jnp.zeros((rows, width), jnp.float32)
    low = (parity == 0, parity == 1)

    def coloured(planes_of):
        first = [jnp.where(low[0], planes_of[2 * k], planes_of[2 * k + 1]) for k in range(pairs)]
        second = [jnp.where(low[0], planes_of[2 * k + 1], planes_of[2 * k]) for k in range(pairs)]
        return [zero] + first + [zero], [zero] + second + [zero]

    source, mobility = coloured(sources), coloured(mobilities)
    row = lax.broadcasted_iota(jnp.int32, (rows, width), 0)
    scaled = ([], [])
    for k in range(pairs):
        for colour in (0, 1):
            sides = around_coarsest(mobility[1 - colour], k, low[colour])
            sides = (jnp.where(row == 0, 0.0, sides[0]), jnp.where(row == rows - 1, 0.0, sides[1])) + sides[2:]
            sides = walls(sides, lane < 4, lane >= width - 4)
            top = jnp.logical_and(jnp.logical_not(low[colour]), sides[5] == 0)
            shares, inverse, _ = weights(mean_any, mobility[colour][k + 1], sides, top)
            for a in range(6):
                bshare[colour, a, k] = shares[a]
            scaled[colour].append(source[colour][k + 1] * inverse)

    fields = [[zero] + scaled[0] + [zero], None]
    for step in range(1, 2 * BOTTOM_SWEEPS):
        colour = step % 2
        new = []
        for k in range(pairs):
            sides = around_coarsest(fields[1 - colour], k, low[colour])
            new.append(relax(scaled[colour][k], [bshare[colour, a, k] for a in range(6)], sides))
        fields[colour] = [zero] + new + [zero]

    start = 4 * REACH - ROWS // 2
    for k in range(WIN // 4):
        a, b = fields[0][start // 2 + k + 1], fields[1][start // 2 + k + 1]
        coarsest[2 * k * rows : (2 * k + 1) * rows, :] = jnp.where(low[0], a, b)
        coarsest[(2 * k + 1) * rows : (2 * k + 2) * rows, :] = jnp.where(low[0], b, a)

    for copy in copies:
        copy.wait()
    near_at, far_at = neighbour_rows(columns)
    here = slice(*OWN)
    first = lanes((ROWS, width)) % 2 == 0
    for i in range(rows):
        half = coarsest[pl.ds(i, WIN // 2, stride=rows), :]
        spread[pl.ds(0, WIN // 2, stride=2), :] = half
        spread[pl.ds(1, WIN // 2, stride=2), :] = half
        e1[i, here, :] = e1[i, here, :] + spread[here, :]
        for row, ref in ((near_at, near), (far_at, far)):
            mixed = ref[i, 0:ROWS, :]
            other = swap_lanes(mixed, 1)
            part = pl.ds(row, ROWS)
            e1[i, part, :] = jnp.where(first, mixed, other) + spread[part, :]
            cscaled0[i, part, :] = jnp.where(first, other, mixed)
            cscaled1[i, part, :] = ref[i, ROWS : 2 * ROWS, :]

    renew(coarse_flow, 0, e0, e1, cface, cinverse0, cscaled0, (1, WIN - 1))
    renew(coarse_flow, 1, e1, e0, cface, cinverse1, cscaled1, (2, WIN - 2))
    renew(coarse_flow, 0, e0, e1, cface, cinverse0, cscaled0, (3, WIN - 3))
    renew(coarse_flow, 1, e1, e0, cface, cinverse1, cscaled1, INNER)

    even = coarse_low(0, width, INNER)
    for i in range(rows):
        a, b = e0[i, at(e0, INNER), :], e1[i, at(e1, INNER), :]
        for half, add in ((0, jnp.where(even, a, b)), (1, jnp.where(even, b, a))):
            for x in (4 * i + 2 * half, 4 * i + 2 * half + 1):
                v1[x] = field1[x] + add

    renew(fine_flow, 0, v0, v1, face, inverse0, scaled0, wider(INNER, -1))
    renew(fine_flow, 1, v1, v0, face, inverse1, scaled1, wider(INNER, -2))
    renew(fine_flow, 0, v0, v1, face, inverse0, scaled0, wider(OWN, 1))
    renew(fine_flow, 1, v1, v0, face, inverse1, scaled1, wider(OWN, 1))

    for i in range(rows):
        planes_of = range(4 * i, 4 * i + 4)
        rest = [rest_of(fine_flow, v0, v1, face, inverse0, scaled0, x, OWN) for x in planes_of]
        for a, tiles in (
            (0, [v0[x, at(v0, OWN), :] for x in planes_of]),
            (1, [v1[x, at(v1, OWN), :] for x in planes_of]),
            (2, rest),
        ):
            for j, tile in enumerate(swap_blocks(tiles)):
                out[4 * i + j, a * ROWS : (a + 1) * ROWS, :] = tile


def local_slabs(shape, right_side, phase, pressure_guess):
    across, columns = shape
    count = across * columns
    bx, by, length = right_side.shape
    planes, width = across * bx, columns * by
    f32 = jnp.float32
    order = place_of(across, columns)
    path = sorted(range(count), key=lambda device: order[device])
    near = [pair for k in range(0, count, 2) for pair in ((path[k], path[k + 1]), (path[k + 1], path[k]))]
    far = [pair for k in range(1, count - 1, 2) for pair in ((path[k], path[k + 1]), (path[k + 1], path[k]))]
    axes = ("gx", "yz")
    cost = pl.CostEstimate(flops=20_000_000_000, bytes_accessed=100_000_000, transcendentals=0)
    params = pltpu.CompilerParams(vmem_limit_bytes=20 * 1024 * 1024)

    def struct(*dims):
        return jax.ShapeDtypeStruct(dims, f32)

    def vmem(*dims):
        return pltpu.VMEM(dims, f32)

    bricks = pl.pallas_call(
        functools.partial(pack_kernel, order),
        in_specs=[pl.BlockSpec(memory_space=pltpu.HBM)] * 3,
        out_shape=struct(count, 5 * ROWS, 128),
        scratch_shapes=[
            vmem(bx, by, length),
            pltpu.VMEM((bx, by, length), phase.dtype),
            vmem(bx, by, length),
            vmem(3, length, 128),
            pltpu.SemaphoreType.DMA((3,)),
        ],
        compiler_params=params,
        name="pack",
    )(*(pltpu.with_memory_space_constraint(x, pltpu.HBM) for x in (right_side, phase, pressure_guess)))
    own = lax.all_to_all(bricks, axes, 0, 0)
    first_part, second_part = own[:, : 3 * ROWS], own[:, 3 * ROWS :]
    first_far = lax.ppermute(first_part, axes, far)
    own_near = lax.ppermute(own, axes, near)
    second_far = lax.ppermute(second_part, axes, far)

    coarse = planes // 4
    face, plane = (6, planes, WIN, width), (planes, WIN, width)
    cface, cplane = (6, coarse, WIN, width), (coarse, WIN, width)
    height = INNER[1] - INNER[0]
    iplane = (planes, height, width)
    letter = (coarse, 2 * ROWS, width)

    def in_hbm(*arrays):
        return [pltpu.with_memory_space_constraint(x, pltpu.HBM) for x in arrays]

    def far_outs(*shapes):
        return [pltpu.HBM(dims, f32) for dims in shapes], [pl.BlockSpec(memory_space=pltpu.HBM)] * len(shapes)

    def near_outs(*shapes):
        return [struct(*dims) for dims in shapes], [pl.BlockSpec(memory_space=pltpu.VMEM)] * len(shapes)

    made = pl.pallas_call(
        functools.partial(weights_kernel, columns),
        out_shape=near_outs(face, plane, plane, cface, cplane, cplane, (coarse, width), plane)[0],
        scratch_shapes=[vmem(*plane)] * 3 + [vmem(*cplane)] * 2 + [vmem(WIN, width)],
        compiler_params=params,
        cost_estimate=cost,
        name="weights",
    )(first_part, own_near, first_far)

    first = near_outs((11, planes, height, width))
    second = far_outs((11, coarse, WIN, width), letter, (count, 2 * coarse, width))
    state, cstate, message, packed = pl.pallas_call(
        functools.partial(down_kernel, columns),
        out_shape=first[0] + second[0],
        out_specs=first[1] + second[1],
        scratch_shapes=[vmem(*plane)] * 2 + [vmem(*cplane)] * 2 + [vmem(*plane)] * 2 + [vmem(*cplane)] * 2 + [
            vmem(WIN, width),
            vmem(*letter),
            vmem(count, 2 * coarse, width),
            pltpu.SemaphoreType.DMA((14,)),
        ],
        compiler_params=params,
        name="down",
    )(*made, second_part, own_near, second_far)
    gathered = lax.all_to_all(packed, axes, 0, 0)
    message_far = lax.ppermute(message, axes, far)
    message_near = lax.ppermute(message, axes, near)

    cycle = pl.pallas_call(
        functools.partial(up_kernel, columns),
        out_shape=struct(count, 3 * ROWS, 128),
        in_specs=[pl.BlockSpec(memory_space=pltpu.VMEM)] * 2 + [pl.BlockSpec(memory_space=pltpu.HBM)] * 3,
        scratch_shapes=[vmem(11, *cplane)] + [vmem(*iplane)] * 2 + [vmem(*cplane)] + [vmem(*letter)] * 2 + [
            vmem(2, 6, 2 * (2 * REACH + 1), coarse, width),
            vmem(WIN // 2 * coarse, width),
            vmem(WIN, width),
            pltpu.SemaphoreType.DMA((3,)),
        ],
        compiler_params=params,
        name="up",
    )(gathered, state, *in_hbm(cstate, message_near, message_far))
    back = lax.all_to_all(cycle, axes, 0, 0)
    return pl.pallas_call(
        functools.partial(unpack_kernel, order),
        out_shape=[struct(bx, by, length)] * 2,
        scratch_shapes=[vmem(2, length, 128)],
        compiler_params=params,
        name="unpack",
    )(back)


def solution(mesh):
    spec = P("gx", "yz", None)
    shape = (mesh.shape["gx"], mesh.shape["yz"])

    def cycle(right_side, phase, pressure_guess):
        bx, by, length = right_side.shape
        slabs = (bx, by, shape[1]) == (4, 32, 4) and length == 2 * ROWS * shape[0] * shape[1]
        if slabs and shape[0] == 8:
            return local_slabs(shape, right_side, phase, pressure_guess)
        return local(right_side, phase, pressure_guess)

    return jax.shard_map(cycle, mesh=mesh, in_specs=(spec,) * 3, out_specs=(spec,) * 2, check_vma=False)
```

```python
import functools

import jax
import jax.numpy as jnp
from jax import lax
from jax.experimental import pallas as pl
from jax.experimental.pallas import tpu as pltpu
from jax.sharding import PartitionSpec as P

SWEEPS = 2
BOTTOM_SWEEPS = 4


def with_halo(x, sides, width):
    for axis, dim in sides:
        size, length = (lax.axis_size(axis), x.shape[dim])
        up = [(i, (i + 1) % size) for i in range(size - 1)]
        down = [(j, i) for i, j in up]
        last = lax.slice_in_dim(x, length - width, length, axis=dim)
        first = lax.slice_in_dim(x, 0, width, axis=dim)
        before = lax.ppermute(last, axis, up)
        after = lax.ppermute(first, axis, down)
        x = jnp.concatenate([before, x, after], axis=dim)
    return x


def harmonic(left, right):
    total = left + right
    safe = jnp.where(total > 0, total, 1.0)
    return jnp.where(total > 0, 2.0 * left * right / safe, 0.0)


def coefficients(padded):
    faces_x = harmonic(padded[1:], padded[:-1])
    faces_y = harmonic(padded[:, 1:], padded[:, :-1])
    centre = padded[1:-1, 1:-1]
    faces_z = harmonic(centre[:, :, 1:], centre[:, :, :-1])
    zero_plane = jnp.zeros_like(centre[:, :, :1])
    x_lower = faces_x[:-1, 1:-1]
    x_upper = faces_x[1:, 1:-1]
    y_lower = faces_y[1:-1, :-1]
    y_upper = faces_y[1:-1, 1:]
    z_lower = jnp.concatenate([zero_plane, faces_z], axis=2)
    z_upper = jnp.concatenate([faces_z, 2.0 * centre[:, :, -1:]], axis=2)
    diagonal = x_lower + x_upper + y_lower + y_upper + z_lower + z_upper
    diagonal = jnp.where(diagonal > 0, diagonal, 1.0)
    return (x_lower, x_upper, y_lower, y_upper, z_lower, z_upper, diagonal)


def shrink(coeffs):
    return tuple((item[1:-1, 1:-1] for item in coeffs))


def parity_of(extent, start_x, start_y):
    index_x = lax.broadcasted_iota(jnp.int32, extent, 0) + start_x
    index_y = lax.broadcasted_iota(jnp.int32, extent, 1) + start_y
    index_z = lax.broadcasted_iota(jnp.int32, extent, 2)
    return (index_x + index_y + index_z) % 2


def neighbours(padded, coeffs):
    centre = padded[1:-1, 1:-1]
    zero_plane = jnp.zeros_like(centre[:, :, :1])
    lower_z = jnp.concatenate([zero_plane, centre[:, :, :-1]], axis=2)
    upper_z = jnp.concatenate([centre[:, :, 1:], zero_plane], axis=2)
    beside_all = coeffs[0] * padded[:-2, 1:-1] + coeffs[1] * padded[2:, 1:-1]
    beside_all = beside_all + coeffs[2] * padded[1:-1, :-2] + coeffs[3] * padded[1:-1, 2:]
    beside_all = beside_all + coeffs[4] * lower_z + coeffs[5] * upper_z
    return (beside_all, centre)


def colour_pass(padded, source, coeffs, parity, colour):
    beside_all, centre = neighbours(padded, coeffs)
    updated = (source + beside_all) / coeffs[6]
    return jnp.where(parity == colour, updated, centre)


def residual_of(padded, source, coeffs):
    beside_all, centre = neighbours(padded, coeffs)
    return source - (coeffs[6] * centre - beside_all)


def restrict_sum(field):
    size_x, size_y, size_z = field.shape
    return 0.5 * field.reshape(size_x // 2, 2, size_y // 2, 2, size_z // 2, 2).sum(axis=(1, 3, 5))


def restrict_mean(field):
    size_x, size_y, size_z = field.shape
    return 0.125 * field.reshape(size_x // 2, 2, size_y // 2, 2, size_z // 2, 2).sum(axis=(1, 3, 5))


def inject(field):
    return jnp.repeat(jnp.repeat(jnp.repeat(field, 2, axis=0), 2, axis=1), 2, axis=2)


def rim_one(field):
    return with_halo(field, (("gx", 0), ("yz", 1)), 1)


def rim_two(field):
    return with_halo(field, (("gx", 0), ("yz", 1)), 2)


def offsets(field):
    return (lax.axis_index("gx") * field.shape[0], lax.axis_index("yz") * field.shape[1])


def prepare_plain(mobility):
    start_x, start_y = offsets(mobility)
    return (coefficients(rim_one(mobility)), parity_of(mobility.shape, start_x, start_y))


def prepare(mobility):
    start_x, start_y = offsets(mobility)
    size_x, size_y, size_z = mobility.shape
    region = coefficients(rim_two(mobility))
    loop_parity = parity_of((size_x + 2, size_y + 2, size_z), start_x - 1, start_y - 1)
    operator_set = (
        shrink(region),
        parity_of(mobility.shape, start_x, start_y),
        region,
        loop_parity,
    )
    return operator_set


def smooth_plain(field, source, operator_set, sweeps, rim):
    coeffs = operator_set[0]
    parity = operator_set[1]
    for _ in range(sweeps):
        field = colour_pass(rim(field), source, coeffs, parity, 0)
        field = colour_pass(rim(field), source, coeffs, parity, 1)
    return field


def smooth(field, source, operator_set, sweeps):
    interior, parity, region, loop_parity = operator_set
    source_loop = rim_one(source)
    for _ in range(sweeps):
        loop_field = colour_pass(rim_two(field), source_loop, region, loop_parity, 0)
        field = colour_pass(loop_field, source, interior, parity, 1)
    return field


def local(right_side, phase, pressure_guess):
    mobility = 1.0 + 999.0 * phase.astype(jnp.float32)
    level_zero = prepare(mobility)
    pressure = smooth(pressure_guess, right_side, level_zero, SWEEPS)
    fine_res = residual_of(rim_one(pressure), right_side, level_zero[0])
    source_one = restrict_sum(fine_res)
    mobility_one = restrict_mean(mobility)
    level_one = prepare(mobility_one)
    coarse_one = smooth(jnp.zeros_like(source_one), source_one, level_one, SWEEPS)
    res_one = residual_of(rim_one(coarse_one), source_one, level_one[0])
    source_two = restrict_sum(res_one)
    mobility_two = restrict_mean(mobility_one)
    level_two = prepare_plain(mobility_two)
    coarse_two = smooth_plain(
        jnp.zeros_like(source_two), source_two, level_two, BOTTOM_SWEEPS, rim_one
    )
    coarse_one = smooth(coarse_one + inject(coarse_two), source_one, level_one, SWEEPS)
    pressure = smooth(pressure + inject(coarse_one), right_side, level_zero, SWEEPS)
    residual = residual_of(rim_one(pressure), right_side, level_zero[0])
    return (pressure, residual)


ROWS = 8
WIN = 3 * ROWS
REACH = 3
MIX = 2.0 / 1001.0


def place_of(rows, columns):
    slab = []
    for g in range(rows):
        a = (g // 2) * 2 + ((g % 2) ^ ((g // 2) % 2))
        slab += [a * columns + (j if a % 2 == 0 else columns - 1 - j) for j in range(columns)]
    return slab


def slab_index(columns):
    g, j = lax.axis_index("gx"), lax.axis_index("yz")
    a = (g // 2) * 2 + (g + g // 2) % 2
    return a * columns + jnp.where(a % 2 == 0, j, columns - 1 - j)


def device_of(slab, columns):
    a, b = slab // columns, slab % columns
    g = (a // 2) * 2 + (a + a // 2) % 2
    return g * columns + jnp.where(a % 2 == 0, b, columns - 1 - b)


def lanes(shape):
    return lax.broadcasted_iota(jnp.int32, shape, len(shape) - 1)


def swap_lanes(v, step):
    width = v.shape[-1]
    up, down = pltpu.roll(v, step, 1), pltpu.roll(v, width - step, 1)
    return jnp.where((lanes(v.shape) // step) % 2 == 0, down, up)


def swap_blocks(tiles):
    block = lanes(tiles[0].shape) // 32
    at = [block == b for b in range(3)]

    def choose(four):
        return jnp.where(at[0], four[0], jnp.where(at[1], four[1], jnp.where(at[2], four[2], four[3])))

    turned = [choose([tiles[(b + d) % 4] for b in range(4)]) for d in range(4)]
    turned = [turned[0]] + [pltpu.roll(turned[d], 32 * d, 1) for d in (1, 2, 3)]
    return [choose([turned[(b - a) % 4] for b in range(4)]) for a in range(4)]


def brick_parity(shape):
    lane = lanes(shape)
    return (lane // 32 + lane) % 2


def pack_kernel(order, source_hbm, phase_hbm, guess_hbm, out_ref, source_ref, phase_ref, guess_ref, turned, arrived):
    copies = [
        pltpu.make_async_copy(hbm, ref, arrived.at[a])
        for a, (hbm, ref) in enumerate(((source_hbm, source_ref), (phase_hbm, phase_ref), (guess_hbm, guess_ref)))
    ]
    for copy in copies:
        copy.start()
    for a, ref in enumerate((source_ref, phase_ref, guess_ref)):
        copies[a].wait()
        brick = ref[...].reshape(128, ref.shape[2])
        if a == 1:
            brick = 1.0 + 999.0 * brick.astype(jnp.float32)
        turned[a] = brick.T
    even = brick_parity((ROWS, 128)) == 0
    for device, slab in enumerate(order):
        base = 2 * ROWS * slab
        for a, row in ((1, 0), (2, ROWS), (0, 3 * ROWS)):
            low = turned[a, pl.ds(base, ROWS, stride=2), :]
            high = turned[a, pl.ds(base + 1, ROWS, stride=2), :]
            if a != 2:
                out_ref[device, row : row + ROWS, :] = jnp.where(even, low, high)
            out_ref[device, row + ROWS : row + 2 * ROWS, :] = jnp.where(even, high, low)


def unpack_kernel(order, in_ref, pressure_ref, residual_ref, turned):
    even = brick_parity((ROWS, 128)) == 0
    for device, slab in enumerate(order):
        base = 2 * ROWS * slab
        p0, p1 = in_ref[device, 0:ROWS, :], in_ref[device, ROWS : 2 * ROWS, :]
        r0 = in_ref[device, 2 * ROWS : 3 * ROWS, :]
        turned[0, pl.ds(base, ROWS, stride=2), :] = jnp.where(even, p0, p1)
        turned[0, pl.ds(base + 1, ROWS, stride=2), :] = jnp.where(even, p1, p0)
        turned[1, pl.ds(base, ROWS, stride=2), :] = jnp.where(even, r0, 0.0)
        turned[1, pl.ds(base + 1, ROWS, stride=2), :] = jnp.where(even, 0.0, r0)
    for a, ref in enumerate((pressure_ref, residual_ref)):
        ref[...] = turned[a].T.reshape(ref.shape)


FACE_ROWS = (1, WIN - 1)
INNER = (ROWS // 2, WIN - ROWS // 2)
OWN = (ROWS, 2 * ROWS)


def wider(rows, by):
    return (rows[0] - by, rows[1] + by)


def at(ref, rows, by=0):
    start = (WIN - ref.shape[-2]) // 2
    return slice(rows[0] - start + by, rows[1] - start + by)


def beyond(ref, i, low, rows, *lead):
    return jnp.where(low, ref[(*lead, i, at(ref, rows, -1))], ref[(*lead, i, at(ref, rows, 1))])


def add_up(terms):
    while len(terms) > 1:
        terms = [sum(terms[k : k + 2]) for k in range(0, len(terms), 2)]
    return terms[0]


def around_coarsest(planes, k, low):
    centre = planes[k + 1]
    rows, width = centre.shape
    return (
        pltpu.roll(centre, 1, 0),
        pltpu.roll(centre, rows - 1, 0),
        pltpu.roll(centre, 4, 1),
        pltpu.roll(centre, width - 4, 1),
        centre,
        jnp.where(low, planes[k], planes[k + 2]),
    )


def walls(sides, first, last):
    return sides[:2] + (jnp.where(first, 0.0, sides[2]), jnp.where(last, 0.0, sides[3])) + sides[4:]


def mean_fine(u, w):
    return jnp.where(u == w, u, (u * MIX) * w)


def mean_any(u, w):
    total = u + w
    return 2.0 * u * w / jnp.where(total > 0, total, 1.0)


def weights(mean, u, sides, top):
    faces = [mean(u, w) for w in sides]
    diagonal = (faces[0] + faces[1]) + (faces[2] + faces[3]) + (faces[4] + faces[5])
    diagonal = diagonal + jnp.where(top, 2.0 * u, 0.0)
    diagonal = jnp.where(diagonal > 0, diagonal, 1.0)
    inverse = 1.0 / diagonal
    return [face * inverse for face in faces], inverse, diagonal


def relax(scaled, share, sides):
    parts = [share[a] * sides[a] for a in range(6)]
    return scaled + ((parts[0] + parts[1]) + (parts[2] + parts[3]) + (parts[4] + parts[5]))


def fine_low(x, colour, width, rows):
    return (lanes((rows[1] - rows[0], width)) + (x + colour) % 2) % 2 == 0


def coarse_low(colour, width, rows):
    shape = (rows[1] - rows[0], width)
    row = lax.broadcasted_iota(jnp.int32, shape, 0) + rows[0]
    return (row + lanes(shape) // 2 + colour) % 2 == 0


def loader(v, rows):
    seen = {}

    def load(x):
        if x not in seen:
            seen[x] = v[x, at(v, rows), :]
        return seen[x]

    return load


def fine_sides(v, load, x, low, rows):
    centre = load(x)
    width = centre.shape[1]
    return (
        load(x - 1) if x > 0 else None,
        load(x + 1) if x + 1 < v.shape[0] else None,
        pltpu.roll(centre, 1, 1),
        pltpu.roll(centre, width - 1, 1),
        centre,
        beyond(v, x, low, rows),
    )


def fine_flow(colour, face, v, x, rows, load=None):
    planes, width = face.shape[1], face.shape[3]
    part = at(face, rows)
    low = fine_low(x, colour, width, rows)
    if v is not None and load is None:
        load = loader(v, rows)
    if colour == 0:
        sides = fine_sides(v, load, x, low, rows)
        return add_up([face[a, x, part, :] * side for a, side in enumerate(sides) if side is not None])

    def carried(a, plane):
        values = face[a, plane, part, :]
        return values if v is None else values * load(plane)

    away = beyond(face, x, low, rows, 5)
    terms = [
        pltpu.roll(carried(3, x), 1, 1),
        pltpu.roll(carried(2, x), width - 1, 1),
        carried(4, x),
        away if v is None else away * beyond(v, x, low, rows),
    ]
    if x > 0:
        terms.append(carried(1, x - 1))
    if x + 1 < planes:
        terms.append(carried(0, x + 1))
    return add_up(terms)


def coarse_sides(v, i, low, rows):
    here = at(v, rows)
    centre = v[i, here, :]
    width = centre.shape[1]
    below = v[i - 1, here, :] if i > 0 else jnp.zeros_like(centre)
    above = v[i + 1, here, :] if i + 1 < v.shape[0] else jnp.zeros_like(centre)
    return (
        v[i, at(v, rows, -1), :],
        v[i, at(v, rows, 1), :],
        pltpu.roll(centre, 2, 1),
        pltpu.roll(centre, width - 2, 1),
        centre,
        jnp.where(low, below, above),
    )


def coarse_flow(colour, face, v, i, rows, load=None):
    planes, width = face.shape[1], face.shape[3]
    low = coarse_low(colour, width, rows)
    if colour == 0:
        sides = coarse_sides(v, i, low, rows)
        return add_up([face[a, i, at(face, rows), :] * side for a, side in enumerate(sides)])

    def carried(a, plane, by=0):
        values = face[a, plane, at(face, rows, by), :]
        return values if v is None else values * v[plane, at(v, rows, by), :]

    centre = carried(4, i)
    below = carried(5, i - 1) if i > 0 else jnp.zeros_like(centre)
    above = carried(5, i + 1) if i + 1 < planes else jnp.zeros_like(centre)
    return add_up(
        [
            carried(1, i, -1),
            carried(0, i, 1),
            pltpu.roll(carried(3, i), 2, 1),
            pltpu.roll(carried(2, i), width - 2, 1),
            centre,
            jnp.where(low, below, above),
        ]
    )


def renew(flow, colour, target, other, face, inverse, scaled, rows):
    load = loader(other, rows)
    for x in range(face.shape[1]):
        moved = inverse[x, at(inverse, rows), :] * flow(colour, face, other, x, rows, load)
        target[x, at(target, rows), :] = scaled[x, at(scaled, rows), :] + moved


def rest_of(flow, v0, v1, face, inverse0, scaled0, x, rows):
    factor = inverse0[x, at(inverse0, rows), :]
    updated = scaled0[x, at(scaled0, rows), :] + factor * flow(0, face, v1, x, rows)
    return (updated - v0[x, at(v0, rows), :]) / factor


def one_over(diagonal):
    return 1.0 / jnp.where(diagonal > 0, diagonal, 1.0)


def fine_faces(m0, m1, face, inverse0, inverse1):
    planes, width = face.shape[1], face.shape[3]
    rows = FACE_ROWS
    here = at(face, rows)
    lane = lanes((rows[1] - rows[0], width))
    load = loader(m1, rows)
    for x in range(planes):
        low = fine_low(x, 0, width, rows)
        u = m0[x, here, :]
        sides = walls(fine_sides(m1, load, x, low, rows), lane == 0, lane == width - 1)
        terms = []
        for a, side in enumerate(sides):
            value = jnp.zeros_like(u) if side is None else mean_fine(u, side)
            face[a, x, here, :] = value
            terms.append(value)
        top = jnp.logical_and(jnp.logical_not(low), sides[5] == 0)
        inverse0[x, here, :] = one_over(add_up(terms) + jnp.where(top, 2.0 * u, 0.0))
    rows = wider(rows, -1)
    for x in range(planes):
        low = fine_low(x, 1, width, rows)
        top = jnp.logical_and(jnp.logical_not(low), m0[x, at(m0, rows, 1), :] == 0)
        total = fine_flow(1, face, None, x, rows) + jnp.where(top, 2.0 * m1[x, at(m1, rows), :], 0.0)
        inverse1[x, at(inverse1, rows), :] = one_over(total)


def coarse_faces(m0, m1, face, inverse0, inverse1):
    planes, width = face.shape[1], face.shape[3]
    rows = FACE_ROWS
    here = at(face, rows)
    lane = lanes((rows[1] - rows[0], width))
    for i in range(planes):
        u = m0[i, here, :]
        sides = walls(coarse_sides(m1, i, coarse_low(0, width, rows), rows), lane < 2, lane >= width - 2)
        terms = []
        for a, side in enumerate(sides):
            value = mean_any(u, side)
            face[a, i, here, :] = value
            terms.append(value)
        inverse0[i, here, :] = one_over(add_up(terms) + jnp.where(sides[1] == 0, 2.0 * u, 0.0))
    rows = wider(rows, -1)
    for i in range(planes):
        top = jnp.where(m0[i, at(m0, rows, 1), :] == 0, 2.0 * m1[i, at(m1, rows), :], 0.0)
        inverse1[i, at(inverse1, rows), :] = one_over(coarse_flow(1, face, None, i, rows) + top)


def neighbour_rows(columns):
    near = jnp.where(slab_index(columns) % 2 == 0, 2 * ROWS, 0)
    return pl.multiple_of(near, ROWS), pl.multiple_of(2 * ROWS - near, ROWS)


def unfold_slabs(places, arrays, planes):
    def unfold(i, _):
        for ref, start, at in places:
            for first, store in arrays:
                tiles = [ref[4 * i + j, start + first : start + first + ROWS, :] for j in range(4)]
                for j, tile in enumerate(swap_blocks(tiles)):
                    store(4 * i + j, at, tile)
        return 0

    lax.fori_loop(0, planes // 4, unfold, 0, unroll=True)


def plain_store(ref):
    def store(x, row, tile):
        ref[x, pl.ds(row, ROWS), :] = tile

    return store


def scaled_store(ref, factor):
    def store(x, row, tile):
        part = pl.ds(row, ROWS)
        ref[x, part, :] = tile * factor[x, part, :]

    return store


def pair_sum(ref):
    return ref[ROWS : 2 * ROWS, :] + ref[ROWS + 1 : 2 * ROWS + 1, :]


def picked(width):
    row = lax.broadcasted_iota(jnp.int32, (ROWS, width), 0)
    return jnp.logical_and(row % 2 == 0, lanes((ROWS, width)) % 4 == row // 2)


def weights_kernel(
    columns,
    own, near, far,
    face, inverse0, inverse1, cface, cinverse0, cinverse1, coarsest, flow0,
    m0, m1, guess, cm0, cm1, rest,
):
    planes, width = face.shape[1], face.shape[3]
    near_at, far_at = neighbour_rows(columns)
    places = ((own, 0, ROWS), (near, 0, near_at), (far, 0, far_at))
    arrays = ((0, plain_store(m0)), (ROWS, plain_store(m1)), (2 * ROWS, plain_store(guess)))
    unfold_slabs(places, arrays, planes)
    fine_faces(m0, m1, face, inverse0, inverse1)
    flow0[...] = jnp.zeros(flow0.shape, jnp.float32)
    load = loader(guess, FACE_ROWS)
    for x in range(planes):
        flow0[x, slice(*FACE_ROWS), :] = fine_flow(0, face, guess, x, FACE_ROWS, load)
    even = coarse_low(0, width, (0, WIN))
    for i in range(planes // 4):
        mobilities = []
        for x in (4 * i, 4 * i + 2):
            mass = (m0[x] + m1[x]) + (m0[x + 1] + m1[x + 1])
            mobilities.append(0.125 * (mass + swap_lanes(mass, 1)))
        cm0[i] = jnp.where(even, mobilities[0], mobilities[1])
        cm1[i] = jnp.where(even, mobilities[1], mobilities[0])
    coarse_faces(cm0, cm1, cface, cinverse0, cinverse1)
    pick = picked(width)
    for i in range(planes // 4):
        rest[...] = cm0[i] + cm1[i]
        pair = pair_sum(rest)
        pair = 0.125 * (pair + swap_lanes(pair, 2))
        coarsest[i : i + 1, :] = jnp.sum(jnp.where(pick, pair, 0.0), axis=0, keepdims=True)


def down_kernel(
    columns,
    face, inverse0, inverse1, cface, cinverse0, cinverse1, coarsest, flow0,
    own, near, far,
    *refs,
):
    state, cstate, late, message_hbm, packed_hbm = refs[:5]
    scaled0, scaled1, cscaled0, cscaled1, v0, v1, e0, e1, rest, message, packed, done = refs[5:]
    planes, width = face.shape[1], face.shape[3]
    coarse = planes // 4
    middle = slice(*INNER)
    held = [(face.at[:, :, middle, :], state.at[0:6])]
    held += [
        (inverse0.at[:, middle, :], state.at[6]),
        (inverse1.at[:, middle, :], late.at[0]),
        (scaled1.at[:, middle, :], late.at[1]),
        (v1.at[:, middle, :], late.at[2]),
    ]
    held += [(message, message_hbm)]
    copies = [pltpu.make_async_copy(ref, out, done.at[k]) for k, (ref, out) in enumerate(held)]
    for copy in copies[:3]:
        copy.start()
    near_at, far_at = neighbour_rows(columns)
    places = ((own, 0, ROWS), (near, 3 * ROWS, near_at), (far, 0, far_at))

    def first_pass(x, row, tile):
        part = pl.ds(row, ROWS)
        factor = inverse0[x, part, :]
        scaled = tile * factor
        scaled0[x, part, :] = scaled
        v0[x, part, :] = scaled + flow0[x, part, :] * factor

    arrays = ((0, first_pass), (ROWS, scaled_store(scaled1, inverse1)))
    unfold_slabs(places, arrays, planes)
    copies[3].start()
    for x in range(planes):
        state[7, x] = scaled0[x, middle, :]
    for i in range(coarse):
        for a in range(6):
            cstate[a, i] = cface[a, i]
        cstate[6, i] = cinverse0[i]
        cstate[7, i] = cinverse1[i]

    renew(fine_flow, 1, v1, v0, face, inverse1, scaled1, (2, WIN - 2))
    renew(fine_flow, 0, v0, v1, face, inverse0, scaled0, (3, WIN - 3))
    renew(fine_flow, 1, v1, v0, face, inverse1, scaled1, (3, WIN - 3))
    copies[4].start()

    even = coarse_low(0, width, INNER)
    for i in range(coarse):
        fields = []
        for x in (4 * i, 4 * i + 2):
            total = rest_of(fine_flow, v0, v1, face, inverse0, scaled0, x, INNER)
            total = total + rest_of(fine_flow, v0, v1, face, inverse0, scaled0, x + 1, INNER)
            fields.append(0.5 * (total + swap_lanes(total, 1)))
        first = jnp.where(even, fields[0], fields[1]) * cinverse0[i, middle, :]
        cscaled0[i, middle, :] = first
        e0[i, middle, :] = first
        cscaled1[i, middle, :] = jnp.where(even, fields[1], fields[0]) * cinverse1[i, middle, :]
    for i in range(coarse):
        cstate[8, i] = cscaled0[i]
        cstate[9, i] = cscaled1[i]

    renew(coarse_flow, 1, e1, e0, cface, cinverse1, cscaled1, wider(INNER, -1))
    renew(coarse_flow, 0, e0, e1, cface, cinverse0, cscaled0, wider(INNER, -2))
    renew(coarse_flow, 1, e1, e0, cface, cinverse1, cscaled1, wider(OWN, 1))
    for i in range(coarse):
        cstate[10, i] = e1[i]

    pick = picked(width)
    for i in range(coarse):
        rest[slice(*OWN), :] = rest_of(coarse_flow, e0, e1, cface, cinverse0, cscaled0, i, OWN)
        pair = pair_sum(rest)
        pair = 0.5 * (pair + swap_lanes(pair, 2))
        packed[0, i : i + 1, :] = jnp.sum(jnp.where(pick, pair, 0.0), axis=0, keepdims=True)
    packed[0, coarse : 2 * coarse, :] = coarsest[...]
    tile = packed[0]
    for device in range(1, packed.shape[0]):
        packed[device] = tile
    sent = pltpu.make_async_copy(packed, packed_hbm, done.at[13])
    sent.start()

    first = lanes((ROWS, width)) % 2 == 0
    here = slice(*OWN)
    for i in range(coarse):
        message[i, 0:ROWS, :] = jnp.where(first, e1[i, here, :], cscaled0[i, here, :])
        message[i, ROWS : 2 * ROWS, :] = cscaled1[i, here, :]
    copies[5].start()
    for copy in copies:
        copy.wait()
    sent.wait()


def up_kernel(
    columns,
    gathered, state, cstate, near_hbm, far_hbm, late_hbm,
    out,
    late, cscaled0, cscaled1, e1, v0, v1, e0, near, far, bshare, coarsest, spread, done,
):
    planes, width = state.shape[1], state.shape[3]
    count = gathered.shape[0]
    rows = planes // 4
    face, inverse0, scaled0 = state, state.at[6], state.at[7]
    inverse1, scaled1, field1 = [late.at[k] for k in range(3)]
    cface, (cinverse0, cinverse1, kept0, kept1, field) = cstate, [cstate.at[k] for k in range(6, 11)]
    held = ((near_hbm, near), (far_hbm, far), (late_hbm, late))
    copies = [pltpu.make_async_copy(hbm, ref, done.at[k]) for k, (hbm, ref) in enumerate(held)]
    for copy in copies:
        copy.start()

    slab = slab_index(columns)
    lane = lanes((rows, width))
    part = lane % 4
    sources, mobilities = [], []
    for w in range(-REACH, REACH + 1):
        other = slab + w
        inside = jnp.logical_and(other >= 0, other < count)
        device = device_of(jnp.clip(other, 0, count - 1), columns)
        keep = jnp.where(inside, 1.0, 0.0)
        for part_of, into in ((slice(0, rows), sources), (slice(rows, 2 * rows), mobilities)):
            tile = gathered[device, part_of, :] * keep
            for z in range(4):
                v = jnp.where(part == z, tile, 0.0)
                v = v + swap_lanes(v, 1)
                into.append(v + swap_lanes(v, 2))

    parity = (lax.broadcasted_iota(jnp.int32, (rows, width), 0) + lane // 4) % 2
    pairs = len(sources) // 2
    zero = jnp.zeros((rows, width), jnp.float32)
    low = (parity == 0, parity == 1)

    def coloured(planes_of):
        first = [jnp.where(low[0], planes_of[2 * k], planes_of[2 * k + 1]) for k in range(pairs)]
        second = [jnp.where(low[0], planes_of[2 * k + 1], planes_of[2 * k]) for k in range(pairs)]
        return [zero] + first + [zero], [zero] + second + [zero]

    source, mobility = coloured(sources), coloured(mobilities)
    row = lax.broadcasted_iota(jnp.int32, (rows, width), 0)
    scaled = ([], [])
    for k in range(pairs):
        for colour in (0, 1):
            sides = around_coarsest(mobility[1 - colour], k, low[colour])
            sides = (jnp.where(row == 0, 0.0, sides[0]), jnp.where(row == rows - 1, 0.0, sides[1])) + sides[2:]
            sides = walls(sides, lane < 4, lane >= width - 4)
            top = jnp.logical_and(jnp.logical_not(low[colour]), sides[5] == 0)
            shares, inverse, _ = weights(mean_any, mobility[colour][k + 1], sides, top)
            for a in range(6):
                bshare[colour, a, k] = shares[a]
            scaled[colour].append(source[colour][k + 1] * inverse)

    fields = [[zero] + scaled[0] + [zero], [zero] * (pairs + 2)]
    for step in range(1, 2 * BOTTOM_SWEEPS):
        colour, skip = step % 2, (step + 1) // 2
        new = list(fields[colour])
        for k in range(skip, pairs - skip):
            sides = around_coarsest(fields[1 - colour], k, low[colour])
            new[k + 1] = relax(scaled[colour][k], [bshare[colour, a, k] for a in range(6)], sides)
        fields[colour] = new

    start = 4 * REACH - ROWS // 2
    for k in range(WIN // 4):
        a, b = fields[0][start // 2 + k + 1], fields[1][start // 2 + k + 1]
        coarsest[2 * k * rows : (2 * k + 1) * rows, :] = jnp.where(low[0], a, b)
        coarsest[(2 * k + 1) * rows : (2 * k + 2) * rows, :] = jnp.where(low[0], b, a)

    for copy in copies[:2]:
        copy.wait()
    near_at, far_at = neighbour_rows(columns)
    here = slice(*OWN)
    first = lanes((ROWS, width)) % 2 == 0
    for i in range(rows):
        half = coarsest[pl.ds(i, WIN // 2, stride=rows), :]
        spread[pl.ds(0, WIN // 2, stride=2), :] = half
        spread[pl.ds(1, WIN // 2, stride=2), :] = half
        e1[i, here, :] = field[i, here, :] + spread[here, :]
        cscaled0[i, here, :] = kept0[i, here, :]
        cscaled1[i, here, :] = kept1[i, here, :]
        for row, ref in ((near_at, near), (far_at, far)):
            mixed = ref[i, 0:ROWS, :]
            other = swap_lanes(mixed, 1)
            part = pl.ds(row, ROWS)
            e1[i, part, :] = jnp.where(first, mixed, other) + spread[part, :]
            cscaled0[i, part, :] = jnp.where(first, other, mixed)
            cscaled1[i, part, :] = ref[i, ROWS : 2 * ROWS, :]

    renew(coarse_flow, 0, e0, e1, cface, cinverse0, cscaled0, (1, WIN - 1))
    renew(coarse_flow, 1, e1, e0, cface, cinverse1, cscaled1, (2, WIN - 2))
    renew(coarse_flow, 0, e0, e1, cface, cinverse0, cscaled0, (3, WIN - 3))
    renew(coarse_flow, 1, e1, e0, cface, cinverse1, cscaled1, INNER)

    copies[2].wait()
    even = coarse_low(0, width, INNER)
    for i in range(rows):
        a, b = e0[i, at(e0, INNER), :], e1[i, at(e1, INNER), :]
        for half, add in ((0, jnp.where(even, a, b)), (1, jnp.where(even, b, a))):
            for x in (4 * i + 2 * half, 4 * i + 2 * half + 1):
                v1[x] = field1[x] + add

    renew(fine_flow, 0, v0, v1, face, inverse0, scaled0, wider(INNER, -1))
    renew(fine_flow, 1, v1, v0, face, inverse1, scaled1, wider(INNER, -2))
    renew(fine_flow, 0, v0, v1, face, inverse0, scaled0, wider(OWN, 1))
    renew(fine_flow, 1, v1, v0, face, inverse1, scaled1, wider(OWN, 1))

    for i in range(rows):
        planes_of = range(4 * i, 4 * i + 4)
        rest = [rest_of(fine_flow, v0, v1, face, inverse0, scaled0, x, OWN) for x in planes_of]
        for a, tiles in (
            (0, [v0[x, at(v0, OWN), :] for x in planes_of]),
            (1, [v1[x, at(v1, OWN), :] for x in planes_of]),
            (2, rest),
        ):
            for j, tile in enumerate(swap_blocks(tiles)):
                out[4 * i + j, a * ROWS : (a + 1) * ROWS, :] = tile


def local_slabs(shape, right_side, phase, pressure_guess):
    across, columns = shape
    count = across * columns
    bx, by, length = right_side.shape
    planes, width = across * bx, columns * by
    f32 = jnp.float32
    order = place_of(across, columns)
    path = sorted(range(count), key=lambda device: order[device])
    near = [pair for k in range(0, count, 2) for pair in ((path[k], path[k + 1]), (path[k + 1], path[k]))]
    far = [pair for k in range(1, count - 1, 2) for pair in ((path[k], path[k + 1]), (path[k + 1], path[k]))]
    axes = ("gx", "yz")
    cost = pl.CostEstimate(flops=20_000_000_000, bytes_accessed=100_000_000, transcendentals=0)
    params = pltpu.CompilerParams(vmem_limit_bytes=20 * 1024 * 1024)

    def struct(*dims):
        return jax.ShapeDtypeStruct(dims, f32)

    def vmem(*dims):
        return pltpu.VMEM(dims, f32)

    bricks = pl.pallas_call(
        functools.partial(pack_kernel, order),
        in_specs=[pl.BlockSpec(memory_space=pltpu.HBM)] * 3,
        out_shape=struct(count, 5 * ROWS, 128),
        scratch_shapes=[
            vmem(bx, by, length),
            pltpu.VMEM((bx, by, length), phase.dtype),
            vmem(bx, by, length),
            vmem(3, length, 128),
            pltpu.SemaphoreType.DMA((3,)),
        ],
        compiler_params=params,
        name="pack",
    )(*(pltpu.with_memory_space_constraint(x, pltpu.HBM) for x in (right_side, phase, pressure_guess)))
    own = lax.all_to_all(bricks, axes, 0, 0)
    first_part, second_part = own[:, : 3 * ROWS], own[:, 3 * ROWS :]
    first_far = lax.ppermute(first_part, axes, far)
    own_near = lax.ppermute(own, axes, near)
    second_far = lax.ppermute(second_part, axes, far)

    coarse = planes // 4
    face, plane = (6, planes, WIN, width), (planes, WIN, width)
    cface, cplane = (6, coarse, WIN, width), (coarse, WIN, width)
    height = INNER[1] - INNER[0]
    iplane = (planes, height, width)
    letter = (coarse, 2 * ROWS, width)

    def in_hbm(*arrays):
        return [pltpu.with_memory_space_constraint(x, pltpu.HBM) for x in arrays]

    def far_outs(*shapes):
        return [pltpu.HBM(dims, f32) for dims in shapes], [pl.BlockSpec(memory_space=pltpu.HBM)] * len(shapes)

    def near_outs(*shapes):
        return [struct(*dims) for dims in shapes], [pl.BlockSpec(memory_space=pltpu.VMEM)] * len(shapes)

    made = pl.pallas_call(
        functools.partial(weights_kernel, columns),
        out_shape=near_outs(face, plane, plane, cface, cplane, cplane, (coarse, width), plane)[0],
        scratch_shapes=[vmem(*plane)] * 3 + [vmem(*cplane)] * 2 + [vmem(WIN, width)],
        compiler_params=params,
        cost_estimate=cost,
        name="weights",
    )(first_part, own_near, first_far)

    first = near_outs((8, planes, height, width), (11, coarse, WIN, width))
    second = far_outs((3, planes, height, width), letter, (count, 2 * coarse, width))
    state, cstate, late, message, packed = pl.pallas_call(
        functools.partial(down_kernel, columns),
        out_shape=first[0] + second[0],
        out_specs=first[1] + second[1],
        scratch_shapes=[vmem(*plane)] * 2 + [vmem(*cplane)] * 2 + [vmem(*plane)] * 2 + [vmem(*cplane)] * 2 + [
            vmem(WIN, width),
            vmem(*letter),
            vmem(count, 2 * coarse, width),
            pltpu.SemaphoreType.DMA((14,)),
        ],
        compiler_params=params,
        name="down",
    )(*made, second_part, own_near, second_far)
    gathered = lax.all_to_all(packed, axes, 0, 0)
    message_far = lax.ppermute(message, axes, far)
    message_near = lax.ppermute(message, axes, near)

    cycle = pl.pallas_call(
        functools.partial(up_kernel, columns),
        out_shape=struct(count, 3 * ROWS, 128),
        in_specs=[pl.BlockSpec(memory_space=pltpu.VMEM)] * 3 + [pl.BlockSpec(memory_space=pltpu.HBM)] * 3,
        scratch_shapes=[vmem(3, *iplane)] + [vmem(*cplane)] * 3 + [vmem(*iplane)] * 2 + [vmem(*cplane)] + [vmem(*letter)] * 2 + [
            vmem(2, 6, 2 * (2 * REACH + 1), coarse, width),
            vmem(WIN // 2 * coarse, width),
            vmem(WIN, width),
            pltpu.SemaphoreType.DMA((3,)),
        ],
        compiler_params=params,
        name="up",
    )(gathered, state, cstate, *in_hbm(message_near, message_far, late))
    back = lax.all_to_all(cycle, axes, 0, 0)
    return pl.pallas_call(
        functools.partial(unpack_kernel, order),
        out_shape=[struct(bx, by, length)] * 2,
        scratch_shapes=[vmem(2, length, 128)],
        compiler_params=params,
        name="unpack",
    )(back)


def solution(mesh):
    spec = P("gx", "yz", None)
    shape = (mesh.shape["gx"], mesh.shape["yz"])

    def cycle(right_side, phase, pressure_guess):
        bx, by, length = right_side.shape
        slabs = (bx, by, shape[1]) == (4, 32, 4) and length == 2 * ROWS * shape[0] * shape[1]
        if slabs and shape[0] == 8:
            return local_slabs(shape, right_side, phase, pressure_guess)
        return local(right_side, phase, pressure_guess)

    return jax.shard_map(cycle, mesh=mesh, in_specs=(spec,) * 3, out_specs=(spec,) * 2, check_vma=False)
```

```python
import functools

import jax
import jax.numpy as jnp
from jax import lax
from jax.experimental import pallas as pl
from jax.experimental.pallas import tpu as pltpu
from jax.sharding import PartitionSpec as P

SWEEPS = 2
BOTTOM_SWEEPS = 4


def with_halo(x, sides, width):
    for axis, dim in sides:
        size, length = (lax.axis_size(axis), x.shape[dim])
        up = [(i, (i + 1) % size) for i in range(size - 1)]
        down = [(j, i) for i, j in up]
        last = lax.slice_in_dim(x, length - width, length, axis=dim)
        first = lax.slice_in_dim(x, 0, width, axis=dim)
        before = lax.ppermute(last, axis, up)
        after = lax.ppermute(first, axis, down)
        x = jnp.concatenate([before, x, after], axis=dim)
    return x


def harmonic(left, right):
    total = left + right
    safe = jnp.where(total > 0, total, 1.0)
    return jnp.where(total > 0, 2.0 * left * right / safe, 0.0)


def coefficients(padded):
    faces_x = harmonic(padded[1:], padded[:-1])
    faces_y = harmonic(padded[:, 1:], padded[:, :-1])
    centre = padded[1:-1, 1:-1]
    faces_z = harmonic(centre[:, :, 1:], centre[:, :, :-1])
    zero_plane = jnp.zeros_like(centre[:, :, :1])
    x_lower = faces_x[:-1, 1:-1]
    x_upper = faces_x[1:, 1:-1]
    y_lower = faces_y[1:-1, :-1]
    y_upper = faces_y[1:-1, 1:]
    z_lower = jnp.concatenate([zero_plane, faces_z], axis=2)
    z_upper = jnp.concatenate([faces_z, 2.0 * centre[:, :, -1:]], axis=2)
    diagonal = x_lower + x_upper + y_lower + y_upper + z_lower + z_upper
    diagonal = jnp.where(diagonal > 0, diagonal, 1.0)
    return (x_lower, x_upper, y_lower, y_upper, z_lower, z_upper, diagonal)


def shrink(coeffs):
    return tuple((item[1:-1, 1:-1] for item in coeffs))


def parity_of(extent, start_x, start_y):
    index_x = lax.broadcasted_iota(jnp.int32, extent, 0) + start_x
    index_y = lax.broadcasted_iota(jnp.int32, extent, 1) + start_y
    index_z = lax.broadcasted_iota(jnp.int32, extent, 2)
    return (index_x + index_y + index_z) % 2


def neighbours(padded, coeffs):
    centre = padded[1:-1, 1:-1]
    zero_plane = jnp.zeros_like(centre[:, :, :1])
    lower_z = jnp.concatenate([zero_plane, centre[:, :, :-1]], axis=2)
    upper_z = jnp.concatenate([centre[:, :, 1:], zero_plane], axis=2)
    beside_all = coeffs[0] * padded[:-2, 1:-1] + coeffs[1] * padded[2:, 1:-1]
    beside_all = beside_all + coeffs[2] * padded[1:-1, :-2] + coeffs[3] * padded[1:-1, 2:]
    beside_all = beside_all + coeffs[4] * lower_z + coeffs[5] * upper_z
    return (beside_all, centre)


def colour_pass(padded, source, coeffs, parity, colour):
    beside_all, centre = neighbours(padded, coeffs)
    updated = (source + beside_all) / coeffs[6]
    return jnp.where(parity == colour, updated, centre)


def residual_of(padded, source, coeffs):
    beside_all, centre = neighbours(padded, coeffs)
    return source - (coeffs[6] * centre - beside_all)


def restrict_sum(field):
    size_x, size_y, size_z = field.shape
    return 0.5 * field.reshape(size_x // 2, 2, size_y // 2, 2, size_z // 2, 2).sum(axis=(1, 3, 5))


def restrict_mean(field):
    size_x, size_y, size_z = field.shape
    return 0.125 * field.reshape(size_x // 2, 2, size_y // 2, 2, size_z // 2, 2).sum(axis=(1, 3, 5))


def inject(field):
    return jnp.repeat(jnp.repeat(jnp.repeat(field, 2, axis=0), 2, axis=1), 2, axis=2)


def rim_one(field):
    return with_halo(field, (("gx", 0), ("yz", 1)), 1)


def rim_two(field):
    return with_halo(field, (("gx", 0), ("yz", 1)), 2)


def offsets(field):
    return (lax.axis_index("gx") * field.shape[0], lax.axis_index("yz") * field.shape[1])


def prepare_plain(mobility):
    start_x, start_y = offsets(mobility)
    return (coefficients(rim_one(mobility)), parity_of(mobility.shape, start_x, start_y))


def prepare(mobility):
    start_x, start_y = offsets(mobility)
    size_x, size_y, size_z = mobility.shape
    region = coefficients(rim_two(mobility))
    loop_parity = parity_of((size_x + 2, size_y + 2, size_z), start_x - 1, start_y - 1)
    operator_set = (
        shrink(region),
        parity_of(mobility.shape, start_x, start_y),
        region,
        loop_parity,
    )
    return operator_set


def smooth_plain(field, source, operator_set, sweeps, rim):
    coeffs = operator_set[0]
    parity = operator_set[1]
    for _ in range(sweeps):
        field = colour_pass(rim(field), source, coeffs, parity, 0)
        field = colour_pass(rim(field), source, coeffs, parity, 1)
    return field


def smooth(field, source, operator_set, sweeps):
    interior, parity, region, loop_parity = operator_set
    source_loop = rim_one(source)
    for _ in range(sweeps):
        loop_field = colour_pass(rim_two(field), source_loop, region, loop_parity, 0)
        field = colour_pass(loop_field, source, interior, parity, 1)
    return field


def local(right_side, phase, pressure_guess):
    mobility = 1.0 + 999.0 * phase.astype(jnp.float32)
    level_zero = prepare(mobility)
    pressure = smooth(pressure_guess, right_side, level_zero, SWEEPS)
    fine_res = residual_of(rim_one(pressure), right_side, level_zero[0])
    source_one = restrict_sum(fine_res)
    mobility_one = restrict_mean(mobility)
    level_one = prepare(mobility_one)
    coarse_one = smooth(jnp.zeros_like(source_one), source_one, level_one, SWEEPS)
    res_one = residual_of(rim_one(coarse_one), source_one, level_one[0])
    source_two = restrict_sum(res_one)
    mobility_two = restrict_mean(mobility_one)
    level_two = prepare_plain(mobility_two)
    coarse_two = smooth_plain(
        jnp.zeros_like(source_two), source_two, level_two, BOTTOM_SWEEPS, rim_one
    )
    coarse_one = smooth(coarse_one + inject(coarse_two), source_one, level_one, SWEEPS)
    pressure = smooth(pressure + inject(coarse_one), right_side, level_zero, SWEEPS)
    residual = residual_of(rim_one(pressure), right_side, level_zero[0])
    return (pressure, residual)


ROWS = 8
WIN = 3 * ROWS
REACH = 3
MIX = 2.0 / 1001.0


def place_of(rows, columns):
    slab = []
    for g in range(rows):
        a = (g // 2) * 2 + ((g % 2) ^ ((g // 2) % 2))
        slab += [a * columns + (j if a % 2 == 0 else columns - 1 - j) for j in range(columns)]
    return slab


def slab_index(columns):
    g, j = lax.axis_index("gx"), lax.axis_index("yz")
    a = (g // 2) * 2 + (g + g // 2) % 2
    return a * columns + jnp.where(a % 2 == 0, j, columns - 1 - j)


def device_of(slab, columns):
    a, b = slab // columns, slab % columns
    g = (a // 2) * 2 + (a + a // 2) % 2
    return g * columns + jnp.where(a % 2 == 0, b, columns - 1 - b)


def lanes(shape):
    return lax.broadcasted_iota(jnp.int32, shape, len(shape) - 1)


def swap_lanes(v, step):
    width = v.shape[-1]
    up, down = pltpu.roll(v, step, 1), pltpu.roll(v, width - step, 1)
    return jnp.where((lanes(v.shape) // step) % 2 == 0, down, up)


def swap_blocks(tiles):
    block = lanes(tiles[0].shape) // 32
    at = [block == b for b in range(3)]

    def choose(four):
        return jnp.where(at[0], four[0], jnp.where(at[1], four[1], jnp.where(at[2], four[2], four[3])))

    turned = [choose([tiles[(b + d) % 4] for b in range(4)]) for d in range(4)]
    turned = [turned[0]] + [pltpu.roll(turned[d], 32 * d, 1) for d in (1, 2, 3)]
    return [choose([turned[(b - a) % 4] for b in range(4)]) for a in range(4)]


def brick_parity(shape):
    lane = lanes(shape)
    return (lane // 32 + lane) % 2


def pack_kernel(order, source_hbm, phase_hbm, guess_hbm, out_ref, source_ref, phase_ref, guess_ref, turned, arrived):
    copies = [
        pltpu.make_async_copy(hbm, ref, arrived.at[a])
        for a, (hbm, ref) in enumerate(((source_hbm, source_ref), (phase_hbm, phase_ref), (guess_hbm, guess_ref)))
    ]
    for copy in copies:
        copy.start()
    for a, ref in enumerate((source_ref, phase_ref, guess_ref)):
        copies[a].wait()
        brick = ref[...].reshape(128, ref.shape[2])
        if a == 1:
            brick = 1.0 + 999.0 * brick.astype(jnp.float32)
        turned[a] = brick.T
    even = brick_parity((ROWS, 128)) == 0
    for device, slab in enumerate(order):
        base = 2 * ROWS * slab
        for a, row in ((1, 0), (2, ROWS), (0, 3 * ROWS)):
            low = turned[a, pl.ds(base, ROWS, stride=2), :]
            high = turned[a, pl.ds(base + 1, ROWS, stride=2), :]
            if a != 2:
                out_ref[device, row : row + ROWS, :] = jnp.where(even, low, high)
            out_ref[device, row + ROWS : row + 2 * ROWS, :] = jnp.where(even, high, low)


def unpack_kernel(order, in_ref, pressure_ref, residual_ref, turned):
    even = brick_parity((ROWS, 128)) == 0
    for device, slab in enumerate(order):
        base = 2 * ROWS * slab
        p0, p1 = in_ref[device, 0:ROWS, :], in_ref[device, ROWS : 2 * ROWS, :]
        r0, r1 = in_ref[device, 2 * ROWS : 3 * ROWS, :], in_ref[device, 3 * ROWS : 4 * ROWS, :]
        turned[0, pl.ds(base, ROWS, stride=2), :] = jnp.where(even, p0, p1)
        turned[0, pl.ds(base + 1, ROWS, stride=2), :] = jnp.where(even, p1, p0)
        turned[1, pl.ds(base, ROWS, stride=2), :] = jnp.where(even, r0, r1)
        turned[1, pl.ds(base + 1, ROWS, stride=2), :] = jnp.where(even, r1, r0)
    for a, ref in enumerate((pressure_ref, residual_ref)):
        ref[...] = turned[a].T.reshape(ref.shape)


FACE_ROWS = (1, WIN - 1)
INNER = (ROWS // 2, WIN - ROWS // 2)
OWN = (ROWS, 2 * ROWS)


def wider(rows, by):
    return (rows[0] - by, rows[1] + by)


def at(ref, rows, by=0):
    start = (WIN - ref.shape[-2]) // 2
    return slice(rows[0] - start + by, rows[1] - start + by)


def beyond(ref, i, low, rows, *lead):
    return jnp.where(low, ref[(*lead, i, at(ref, rows, -1))], ref[(*lead, i, at(ref, rows, 1))])


def add_up(terms):
    while len(terms) > 1:
        terms = [sum(terms[k : k + 2]) for k in range(0, len(terms), 2)]
    return terms[0]


def around_coarsest(planes, k, low):
    centre = planes[k + 1]
    rows, width = centre.shape
    return (
        pltpu.roll(centre, 1, 0),
        pltpu.roll(centre, rows - 1, 0),
        pltpu.roll(centre, 4, 1),
        pltpu.roll(centre, width - 4, 1),
        centre,
        jnp.where(low, planes[k], planes[k + 2]),
    )


def walls(sides, first, last):
    return sides[:2] + (jnp.where(first, 0.0, sides[2]), jnp.where(last, 0.0, sides[3])) + sides[4:]


def mean_fine(u, w):
    return jnp.where(u == w, u, (u * MIX) * w)


def mean_any(u, w):
    total = u + w
    return 2.0 * u * w / jnp.where(total > 0, total, 1.0)


def weights(mean, u, sides, top):
    faces = [mean(u, w) for w in sides]
    diagonal = (faces[0] + faces[1]) + (faces[2] + faces[3]) + (faces[4] + faces[5])
    diagonal = diagonal + jnp.where(top, 2.0 * u, 0.0)
    diagonal = jnp.where(diagonal > 0, diagonal, 1.0)
    inverse = 1.0 / diagonal
    return [face * inverse for face in faces], inverse, diagonal


def relax(scaled, share, sides):
    parts = [share[a] * sides[a] for a in range(6)]
    return scaled + ((parts[0] + parts[1]) + (parts[2] + parts[3]) + (parts[4] + parts[5]))


def fine_low(x, colour, width, rows):
    return (lanes((rows[1] - rows[0], width)) + (x + colour) % 2) % 2 == 0


def coarse_low(colour, width, rows):
    shape = (rows[1] - rows[0], width)
    row = lax.broadcasted_iota(jnp.int32, shape, 0) + rows[0]
    return (row + lanes(shape) // 2 + colour) % 2 == 0


def loader(v, rows):
    seen = {}

    def load(x):
        if x not in seen:
            seen[x] = v[x, at(v, rows), :]
        return seen[x]

    return load


def fine_sides(v, load, x, low, rows):
    centre = load(x)
    width = centre.shape[1]
    return (
        load(x - 1) if x > 0 else None,
        load(x + 1) if x + 1 < v.shape[0] else None,
        pltpu.roll(centre, 1, 1),
        pltpu.roll(centre, width - 1, 1),
        centre,
        beyond(v, x, low, rows),
    )


def fine_flow(colour, face, v, x, rows, load=None):
    planes, width = face.shape[1], face.shape[3]
    part = at(face, rows)
    low = fine_low(x, colour, width, rows)
    if v is not None and load is None:
        load = loader(v, rows)
    if colour == 0:
        sides = fine_sides(v, load, x, low, rows)
        return add_up([face[a, x, part, :] * side for a, side in enumerate(sides) if side is not None])

    def carried(a, plane):
        values = face[a, plane, part, :]
        return values if v is None else values * load(plane)

    away = beyond(face, x, low, rows, 5)
    terms = [
        pltpu.roll(carried(3, x), 1, 1),
        pltpu.roll(carried(2, x), width - 1, 1),
        carried(4, x),
        away if v is None else away * beyond(v, x, low, rows),
    ]
    if x > 0:
        terms.append(carried(1, x - 1))
    if x + 1 < planes:
        terms.append(carried(0, x + 1))
    return add_up(terms)


def coarse_sides(v, i, low, rows):
    here = at(v, rows)
    centre = v[i, here, :]
    width = centre.shape[1]
    below = v[i - 1, here, :] if i > 0 else jnp.zeros_like(centre)
    above = v[i + 1, here, :] if i + 1 < v.shape[0] else jnp.zeros_like(centre)
    return (
        v[i, at(v, rows, -1), :],
        v[i, at(v, rows, 1), :],
        pltpu.roll(centre, 2, 1),
        pltpu.roll(centre, width - 2, 1),
        centre,
        jnp.where(low, below, above),
    )


def coarse_flow(colour, face, v, i, rows, load=None):
    planes, width = face.shape[1], face.shape[3]
    low = coarse_low(colour, width, rows)
    if colour == 0:
        sides = coarse_sides(v, i, low, rows)
        return add_up([face[a, i, at(face, rows), :] * side for a, side in enumerate(sides)])

    def carried(a, plane, by=0):
        values = face[a, plane, at(face, rows, by), :]
        return values if v is None else values * v[plane, at(v, rows, by), :]

    centre = carried(4, i)
    below = carried(5, i - 1) if i > 0 else jnp.zeros_like(centre)
    above = carried(5, i + 1) if i + 1 < planes else jnp.zeros_like(centre)
    return add_up(
        [
            carried(1, i, -1),
            carried(0, i, 1),
            pltpu.roll(carried(3, i), 2, 1),
            pltpu.roll(carried(2, i), width - 2, 1),
            centre,
            jnp.where(low, below, above),
        ]
    )


def renew(flow, colour, target, other, face, inverse, scaled, rows):
    load = loader(other, rows)
    for x in range(face.shape[1]):
        moved = inverse[x, at(inverse, rows), :] * flow(colour, face, other, x, rows, load)
        target[x, at(target, rows), :] = scaled[x, at(scaled, rows), :] + moved


def rest_of(flow, colour, fields, face, inverses, sources, x, rows):
    inverse, scaled, v = inverses[colour], sources[colour], fields[colour]
    factor = inverse[x, at(inverse, rows), :]
    updated = scaled[x, at(scaled, rows), :] + factor * flow(colour, face, fields[1 - colour], x, rows)
    return (updated - v[x, at(v, rows), :]) / factor


def one_over(diagonal):
    return 1.0 / jnp.where(diagonal > 0, diagonal, 1.0)


def fine_faces(m0, m1, face, inverse0, inverse1):
    planes, width = face.shape[1], face.shape[3]
    rows = FACE_ROWS
    here = at(face, rows)
    lane = lanes((rows[1] - rows[0], width))
    load = loader(m1, rows)
    for x in range(planes):
        low = fine_low(x, 0, width, rows)
        u = m0[x, here, :]
        sides = walls(fine_sides(m1, load, x, low, rows), lane == 0, lane == width - 1)
        terms = []
        for a, side in enumerate(sides):
            value = jnp.zeros_like(u) if side is None else mean_fine(u, side)
            face[a, x, here, :] = value
            terms.append(value)
        top = jnp.logical_and(jnp.logical_not(low), sides[5] == 0)
        inverse0[x, here, :] = one_over(add_up(terms) + jnp.where(top, 2.0 * u, 0.0))
    rows = wider(rows, -1)
    for x in range(planes):
        low = fine_low(x, 1, width, rows)
        top = jnp.logical_and(jnp.logical_not(low), m0[x, at(m0, rows, 1), :] == 0)
        total = fine_flow(1, face, None, x, rows) + jnp.where(top, 2.0 * m1[x, at(m1, rows), :], 0.0)
        inverse1[x, at(inverse1, rows), :] = one_over(total)


def coarse_faces(m0, m1, face, inverse0, inverse1):
    planes, width = face.shape[1], face.shape[3]
    rows = FACE_ROWS
    here = at(face, rows)
    lane = lanes((rows[1] - rows[0], width))
    for i in range(planes):
        u = m0[i, here, :]
        sides = walls(coarse_sides(m1, i, coarse_low(0, width, rows), rows), lane < 2, lane >= width - 2)
        terms = []
        for a, side in enumerate(sides):
            value = mean_any(u, side)
            face[a, i, here, :] = value
            terms.append(value)
        inverse0[i, here, :] = one_over(add_up(terms) + jnp.where(sides[1] == 0, 2.0 * u, 0.0))
    rows = wider(rows, -1)
    for i in range(planes):
        top = jnp.where(m0[i, at(m0, rows, 1), :] == 0, 2.0 * m1[i, at(m1, rows), :], 0.0)
        inverse1[i, at(inverse1, rows), :] = one_over(coarse_flow(1, face, None, i, rows) + top)


def neighbour_rows(columns):
    near = jnp.where(slab_index(columns) % 2 == 0, 2 * ROWS, 0)
    return pl.multiple_of(near, ROWS), pl.multiple_of(2 * ROWS - near, ROWS)


def unfold_slabs(places, arrays, planes):
    def unfold(i, _):
        for ref, start, at in places:
            for first, store in arrays:
                tiles = [ref[4 * i + j, start + first : start + first + ROWS, :] for j in range(4)]
                for j, tile in enumerate(swap_blocks(tiles)):
                    store(4 * i + j, at, tile)
        return 0

    lax.fori_loop(0, planes // 4, unfold, 0, unroll=True)


def plain_store(ref):
    def store(x, row, tile):
        ref[x, pl.ds(row, ROWS), :] = tile

    return store


def scaled_store(ref, factor):
    def store(x, row, tile):
        part = pl.ds(row, ROWS)
        ref[x, part, :] = tile * factor[x, part, :]

    return store


def pair_sum(ref):
    return ref[ROWS : 2 * ROWS, :] + ref[ROWS + 1 : 2 * ROWS + 1, :]


def picked(width):
    row = lax.broadcasted_iota(jnp.int32, (ROWS, width), 0)
    return jnp.logical_and(row % 2 == 0, lanes((ROWS, width)) % 4 == row // 2)


def weights_kernel(
    columns,
    own, near, far,
    face, inverse0, inverse1, cface, cinverse0, cinverse1, coarsest, flow0,
    m0, m1, guess, cm0, cm1, rest,
):
    planes, width = face.shape[1], face.shape[3]
    near_at, far_at = neighbour_rows(columns)
    places = ((own, 0, ROWS), (near, 0, near_at), (far, 0, far_at))
    arrays = ((0, plain_store(m0)), (ROWS, plain_store(m1)), (2 * ROWS, plain_store(guess)))
    unfold_slabs(places, arrays, planes)
    fine_faces(m0, m1, face, inverse0, inverse1)
    flow0[...] = jnp.zeros(flow0.shape, jnp.float32)
    load = loader(guess, FACE_ROWS)
    for x in range(planes):
        flow0[x, slice(*FACE_ROWS), :] = fine_flow(0, face, guess, x, FACE_ROWS, load)
    even = coarse_low(0, width, (0, WIN))
    for i in range(planes // 4):
        mobilities = []
        for x in (4 * i, 4 * i + 2):
            mass = (m0[x] + m1[x]) + (m0[x + 1] + m1[x + 1])
            mobilities.append(0.125 * (mass + swap_lanes(mass, 1)))
        cm0[i] = jnp.where(even, mobilities[0], mobilities[1])
        cm1[i] = jnp.where(even, mobilities[1], mobilities[0])
    coarse_faces(cm0, cm1, cface, cinverse0, cinverse1)
    pick = picked(width)
    for i in range(planes // 4):
        rest[...] = cm0[i] + cm1[i]
        pair = pair_sum(rest)
        pair = 0.125 * (pair + swap_lanes(pair, 2))
        coarsest[i : i + 1, :] = jnp.sum(jnp.where(pick, pair, 0.0), axis=0, keepdims=True)


def down_kernel(
    columns,
    face, inverse0, inverse1, cface, cinverse0, cinverse1, coarsest, flow0,
    own, near, far,
    *refs,
):
    state, cstate, late, message_hbm, packed_hbm = refs[:5]
    scaled0, scaled1, cscaled0, cscaled1, v0, v1, e0, e1, rest, message, packed, done = refs[5:]
    planes, width = face.shape[1], face.shape[3]
    coarse = planes // 4
    middle = slice(*INNER)
    held = [(face.at[:, :, middle, :], state.at[0:6])]
    held += [
        (inverse0.at[:, middle, :], state.at[6]),
        (inverse1.at[:, middle, :], late.at[0]),
        (scaled1.at[:, middle, :], late.at[1]),
        (v1.at[:, middle, :], late.at[2]),
    ]
    held += [(message, message_hbm)]
    copies = [pltpu.make_async_copy(ref, out, done.at[k]) for k, (ref, out) in enumerate(held)]
    for copy in copies[:3]:
        copy.start()
    near_at, far_at = neighbour_rows(columns)
    places = ((own, 0, ROWS), (near, 3 * ROWS, near_at), (far, 0, far_at))

    def first_pass(x, row, tile):
        part = pl.ds(row, ROWS)
        factor = inverse0[x, part, :]
        scaled = tile * factor
        scaled0[x, part, :] = scaled
        v0[x, part, :] = scaled + flow0[x, part, :] * factor

    arrays = ((0, first_pass), (ROWS, scaled_store(scaled1, inverse1)))
    unfold_slabs(places, arrays, planes)
    copies[3].start()
    for x in range(planes):
        state[7, x] = scaled0[x, middle, :]
    for i in range(coarse):
        for a in range(6):
            cstate[a, i] = cface[a, i]
        cstate[6, i] = cinverse0[i]
        cstate[7, i] = cinverse1[i]

    renew(fine_flow, 1, v1, v0, face, inverse1, scaled1, (2, WIN - 2))
    renew(fine_flow, 0, v0, v1, face, inverse0, scaled0, (3, WIN - 3))
    renew(fine_flow, 1, v1, v0, face, inverse1, scaled1, (3, WIN - 3))
    copies[4].start()

    even = coarse_low(0, width, INNER)
    for i in range(coarse):
        fields = []
        for x in (4 * i, 4 * i + 2):
            total = 0.0
            for plane in (x, x + 1):
                for colour in (0, 1):
                    level = ((v0, v1), face, (inverse0, inverse1), (scaled0, scaled1))
                    total = total + rest_of(fine_flow, colour, *level, plane, INNER)
            fields.append(0.5 * (total + swap_lanes(total, 1)))
        first = jnp.where(even, fields[0], fields[1]) * cinverse0[i, middle, :]
        cscaled0[i, middle, :] = first
        e0[i, middle, :] = first
        cscaled1[i, middle, :] = jnp.where(even, fields[1], fields[0]) * cinverse1[i, middle, :]
    for i in range(coarse):
        cstate[8, i] = cscaled0[i]
        cstate[9, i] = cscaled1[i]

    renew(coarse_flow, 1, e1, e0, cface, cinverse1, cscaled1, wider(INNER, -1))
    renew(coarse_flow, 0, e0, e1, cface, cinverse0, cscaled0, wider(INNER, -2))
    renew(coarse_flow, 1, e1, e0, cface, cinverse1, cscaled1, wider(OWN, 1))
    for i in range(coarse):
        cstate[10, i] = e1[i]

    pick = picked(width)
    for i in range(coarse):
        level = ((e0, e1), cface, (cinverse0, cinverse1), (cscaled0, cscaled1))
        rest[slice(*OWN), :] = rest_of(coarse_flow, 0, *level, i, OWN) + rest_of(coarse_flow, 1, *level, i, OWN)
        pair = pair_sum(rest)
        pair = 0.5 * (pair + swap_lanes(pair, 2))
        packed[0, i : i + 1, :] = jnp.sum(jnp.where(pick, pair, 0.0), axis=0, keepdims=True)
    packed[0, coarse : 2 * coarse, :] = coarsest[...]
    tile = packed[0]
    for device in range(1, packed.shape[0]):
        packed[device] = tile
    sent = pltpu.make_async_copy(packed, packed_hbm, done.at[13])
    sent.start()

    first = lanes((ROWS, width)) % 2 == 0
    here = slice(*OWN)
    for i in range(coarse):
        message[i, 0:ROWS, :] = jnp.where(first, e1[i, here, :], cscaled0[i, here, :])
        message[i, ROWS : 2 * ROWS, :] = cscaled1[i, here, :]
    copies[5].start()
    for copy in copies:
        copy.wait()
    sent.wait()


def up_kernel(
    columns,
    gathered, state, cstate, near_hbm, far_hbm, late_hbm,
    out,
    late, cscaled0, cscaled1, e1, v0, v1, e0, near, far, bshare, coarsest, spread, done,
):
    planes, width = state.shape[1], state.shape[3]
    count = gathered.shape[0]
    rows = planes // 4
    face, inverse0, scaled0 = state, state.at[6], state.at[7]
    inverse1, scaled1, field1 = [late.at[k] for k in range(3)]
    cface, (cinverse0, cinverse1, kept0, kept1, field) = cstate, [cstate.at[k] for k in range(6, 11)]
    held = ((near_hbm, near), (far_hbm, far), (late_hbm, late))
    copies = [pltpu.make_async_copy(hbm, ref, done.at[k]) for k, (hbm, ref) in enumerate(held)]
    for copy in copies:
        copy.start()

    slab = slab_index(columns)
    lane = lanes((rows, width))
    part = lane % 4
    sources, mobilities = [], []
    for w in range(-REACH, REACH + 1):
        other = slab + w
        inside = jnp.logical_and(other >= 0, other < count)
        device = device_of(jnp.clip(other, 0, count - 1), columns)
        keep = jnp.where(inside, 1.0, 0.0)
        for part_of, into in ((slice(0, rows), sources), (slice(rows, 2 * rows), mobilities)):
            tile = gathered[device, part_of, :] * keep
            for z in range(4):
                v = jnp.where(part == z, tile, 0.0)
                v = v + swap_lanes(v, 1)
                into.append(v + swap_lanes(v, 2))

    parity = (lax.broadcasted_iota(jnp.int32, (rows, width), 0) + lane // 4) % 2
    pairs = len(sources) // 2
    zero = jnp.zeros((rows, width), jnp.float32)
    low = (parity == 0, parity == 1)

    def coloured(planes_of):
        first = [jnp.where(low[0], planes_of[2 * k], planes_of[2 * k + 1]) for k in range(pairs)]
        second = [jnp.where(low[0], planes_of[2 * k + 1], planes_of[2 * k]) for k in range(pairs)]
        return [zero] + first + [zero], [zero] + second + [zero]

    source, mobility = coloured(sources), coloured(mobilities)
    row = lax.broadcasted_iota(jnp.int32, (rows, width), 0)
    scaled = ([], [])
    for k in range(pairs):
        for colour in (0, 1):
            sides = around_coarsest(mobility[1 - colour], k, low[colour])
            sides = (jnp.where(row == 0, 0.0, sides[0]), jnp.where(row == rows - 1, 0.0, sides[1])) + sides[2:]
            sides = walls(sides, lane < 4, lane >= width - 4)
            top = jnp.logical_and(jnp.logical_not(low[colour]), sides[5] == 0)
            shares, inverse, _ = weights(mean_any, mobility[colour][k + 1], sides, top)
            for a in range(6):
                bshare[colour, a, k] = shares[a]
            scaled[colour].append(source[colour][k + 1] * inverse)

    fields = [[zero] + scaled[0] + [zero], [zero] * (pairs + 2)]
    for step in range(1, 2 * BOTTOM_SWEEPS):
        colour, skip = step % 2, (step + 1) // 2
        new = list(fields[colour])
        for k in range(skip, pairs - skip):
            sides = around_coarsest(fields[1 - colour], k, low[colour])
            new[k + 1] = relax(scaled[colour][k], [bshare[colour, a, k] for a in range(6)], sides)
        fields[colour] = new

    start = 4 * REACH - ROWS // 2
    for k in range(WIN // 4):
        a, b = fields[0][start // 2 + k + 1], fields[1][start // 2 + k + 1]
        coarsest[2 * k * rows : (2 * k + 1) * rows, :] = jnp.where(low[0], a, b)
        coarsest[(2 * k + 1) * rows : (2 * k + 2) * rows, :] = jnp.where(low[0], b, a)

    for copy in copies[:2]:
        copy.wait()
    near_at, far_at = neighbour_rows(columns)
    here = slice(*OWN)
    first = lanes((ROWS, width)) % 2 == 0
    for i in range(rows):
        half = coarsest[pl.ds(i, WIN // 2, stride=rows), :]
        spread[pl.ds(0, WIN // 2, stride=2), :] = half
        spread[pl.ds(1, WIN // 2, stride=2), :] = half
        e1[i, here, :] = field[i, here, :] + spread[here, :]
        cscaled0[i, here, :] = kept0[i, here, :]
        cscaled1[i, here, :] = kept1[i, here, :]
        for row, ref in ((near_at, near), (far_at, far)):
            mixed = ref[i, 0:ROWS, :]
            other = swap_lanes(mixed, 1)
            part = pl.ds(row, ROWS)
            e1[i, part, :] = jnp.where(first, mixed, other) + spread[part, :]
            cscaled0[i, part, :] = jnp.where(first, other, mixed)
            cscaled1[i, part, :] = ref[i, ROWS : 2 * ROWS, :]

    renew(coarse_flow, 0, e0, e1, cface, cinverse0, cscaled0, (1, WIN - 1))
    renew(coarse_flow, 1, e1, e0, cface, cinverse1, cscaled1, (2, WIN - 2))
    renew(coarse_flow, 0, e0, e1, cface, cinverse0, cscaled0, (3, WIN - 3))
    renew(coarse_flow, 1, e1, e0, cface, cinverse1, cscaled1, INNER)

    copies[2].wait()
    even = coarse_low(0, width, INNER)
    for i in range(rows):
        a, b = e0[i, at(e0, INNER), :], e1[i, at(e1, INNER), :]
        for half, add in ((0, jnp.where(even, a, b)), (1, jnp.where(even, b, a))):
            for x in (4 * i + 2 * half, 4 * i + 2 * half + 1):
                v1[x] = field1[x] + add

    renew(fine_flow, 0, v0, v1, face, inverse0, scaled0, wider(INNER, -1))
    renew(fine_flow, 1, v1, v0, face, inverse1, scaled1, wider(INNER, -2))
    renew(fine_flow, 0, v0, v1, face, inverse0, scaled0, wider(OWN, 1))
    renew(fine_flow, 1, v1, v0, face, inverse1, scaled1, wider(OWN, 1))

    for i in range(rows):
        planes_of = range(4 * i, 4 * i + 4)
        level = ((v0, v1), face, (inverse0, inverse1), (scaled0, scaled1))
        rest = [[rest_of(fine_flow, colour, *level, x, OWN) for x in planes_of] for colour in (0, 1)]
        for a, tiles in (
            (0, [v0[x, at(v0, OWN), :] for x in planes_of]),
            (1, [v1[x, at(v1, OWN), :] for x in planes_of]),
            (2, rest[0]),
            (3, rest[1]),
        ):
            for j, tile in enumerate(swap_blocks(tiles)):
                out[4 * i + j, a * ROWS : (a + 1) * ROWS, :] = tile


def local_slabs(shape, right_side, phase, pressure_guess):
    across, columns = shape
    count = across * columns
    bx, by, length = right_side.shape
    planes, width = across * bx, columns * by
    f32 = jnp.float32
    order = place_of(across, columns)
    path = sorted(range(count), key=lambda device: order[device])
    near = [pair for k in range(0, count, 2) for pair in ((path[k], path[k + 1]), (path[k + 1], path[k]))]
    far = [pair for k in range(1, count - 1, 2) for pair in ((path[k], path[k + 1]), (path[k + 1], path[k]))]
    axes = ("gx", "yz")
    cost = pl.CostEstimate(flops=20_000_000_000, bytes_accessed=100_000_000, transcendentals=0)
    params = pltpu.CompilerParams(vmem_limit_bytes=20 * 1024 * 1024)

    def struct(*dims):
        return jax.ShapeDtypeStruct(dims, f32)

    def vmem(*dims):
        return pltpu.VMEM(dims, f32)

    bricks = pl.pallas_call(
        functools.partial(pack_kernel, order),
        in_specs=[pl.BlockSpec(memory_space=pltpu.HBM)] * 3,
        out_shape=struct(count, 5 * ROWS, 128),
        scratch_shapes=[
            vmem(bx, by, length),
            pltpu.VMEM((bx, by, length), phase.dtype),
            vmem(bx, by, length),
            vmem(3, length, 128),
            pltpu.SemaphoreType.DMA((3,)),
        ],
        compiler_params=params,
        name="pack",
    )(*(pltpu.with_memory_space_constraint(x, pltpu.HBM) for x in (right_side, phase, pressure_guess)))
    own = lax.all_to_all(bricks, axes, 0, 0)
    first_part, second_part = own[:, : 3 * ROWS], own[:, 3 * ROWS :]
    first_far = lax.ppermute(first_part, axes, far)
    own_near = lax.ppermute(own, axes, near)
    second_far = lax.ppermute(second_part, axes, far)

    coarse = planes // 4
    face, plane = (6, planes, WIN, width), (planes, WIN, width)
    cface, cplane = (6, coarse, WIN, width), (coarse, WIN, width)
    height = INNER[1] - INNER[0]
    iplane = (planes, height, width)
    letter = (coarse, 2 * ROWS, width)

    def in_hbm(*arrays):
        return [pltpu.with_memory_space_constraint(x, pltpu.HBM) for x in arrays]

    def far_outs(*shapes):
        return [pltpu.HBM(dims, f32) for dims in shapes], [pl.BlockSpec(memory_space=pltpu.HBM)] * len(shapes)

    def near_outs(*shapes):
        return [struct(*dims) for dims in shapes], [pl.BlockSpec(memory_space=pltpu.VMEM)] * len(shapes)

    made = pl.pallas_call(
        functools.partial(weights_kernel, columns),
        out_shape=near_outs(face, plane, plane, cface, cplane, cplane, (coarse, width), plane)[0],
        scratch_shapes=[vmem(*plane)] * 3 + [vmem(*cplane)] * 2 + [vmem(WIN, width)],
        compiler_params=params,
        cost_estimate=cost,
        name="weights",
    )(first_part, own_near, first_far)

    first = near_outs((8, planes, height, width), (11, coarse, WIN, width))
    second = far_outs((3, planes, height, width), letter, (count, 2 * coarse, width))
    state, cstate, late, message, packed = pl.pallas_call(
        functools.partial(down_kernel, columns),
        out_shape=first[0] + second[0],
        out_specs=first[1] + second[1],
        scratch_shapes=[vmem(*plane)] * 2 + [vmem(*cplane)] * 2 + [vmem(*plane)] * 2 + [vmem(*cplane)] * 2 + [
            vmem(WIN, width),
            vmem(*letter),
            vmem(count, 2 * coarse, width),
            pltpu.SemaphoreType.DMA((14,)),
        ],
        compiler_params=params,
        name="down",
    )(*made, second_part, own_near, second_far)
    gathered = lax.all_to_all(packed, axes, 0, 0)
    message_far = lax.ppermute(message, axes, far)
    message_near = lax.ppermute(message, axes, near)

    cycle = pl.pallas_call(
        functools.partial(up_kernel, columns),
        out_shape=struct(count, 4 * ROWS, 128),
        in_specs=[pl.BlockSpec(memory_space=pltpu.VMEM)] * 3 + [pl.BlockSpec(memory_space=pltpu.HBM)] * 3,
        scratch_shapes=[vmem(3, *iplane)] + [vmem(*cplane)] * 3 + [vmem(*iplane)] * 2 + [vmem(*cplane)] + [vmem(*letter)] * 2 + [
            vmem(2, 6, 2 * (2 * REACH + 1), coarse, width),
            vmem(WIN // 2 * coarse, width),
            vmem(WIN, width),
            pltpu.SemaphoreType.DMA((3,)),
        ],
        compiler_params=params,
        name="up",
    )(gathered, state, cstate, *in_hbm(message_near, message_far, late))
    back = lax.all_to_all(cycle, axes, 0, 0)
    return pl.pallas_call(
        functools.partial(unpack_kernel, order),
        out_shape=[struct(bx, by, length)] * 2,
        scratch_shapes=[vmem(2, length, 128)],
        compiler_params=params,
        name="unpack",
    )(back)


def solution(mesh):
    spec = P("gx", "yz", None)
    shape = (mesh.shape["gx"], mesh.shape["yz"])

    def cycle(right_side, phase, pressure_guess):
        bx, by, length = right_side.shape
        slabs = (bx, by, shape[1]) == (4, 32, 4) and length == 2 * ROWS * shape[0] * shape[1]
        if slabs and shape[0] == 8:
            return local_slabs(shape, right_side, phase, pressure_guess)
        return local(right_side, phase, pressure_guess)

    return jax.shard_map(cycle, mesh=mesh, in_specs=(spec,) * 3, out_specs=(spec,) * 2, check_vma=False)
```

```python
import functools

import jax
import jax.numpy as jnp
from jax import lax
from jax.experimental import pallas as pl
from jax.experimental.pallas import tpu as pltpu
from jax.sharding import PartitionSpec as P

SWEEPS = 2
BOTTOM_SWEEPS = 4


def with_halo(x, sides, width):
    for axis, dim in sides:
        size, length = (lax.axis_size(axis), x.shape[dim])
        up = [(i, (i + 1) % size) for i in range(size - 1)]
        down = [(j, i) for i, j in up]
        last = lax.slice_in_dim(x, length - width, length, axis=dim)
        first = lax.slice_in_dim(x, 0, width, axis=dim)
        before = lax.ppermute(last, axis, up)
        after = lax.ppermute(first, axis, down)
        x = jnp.concatenate([before, x, after], axis=dim)
    return x


def harmonic(left, right):
    total = left + right
    safe = jnp.where(total > 0, total, 1.0)
    return jnp.where(total > 0, 2.0 * left * right / safe, 0.0)


def coefficients(padded):
    faces_x = harmonic(padded[1:], padded[:-1])
    faces_y = harmonic(padded[:, 1:], padded[:, :-1])
    centre = padded[1:-1, 1:-1]
    faces_z = harmonic(centre[:, :, 1:], centre[:, :, :-1])
    zero_plane = jnp.zeros_like(centre[:, :, :1])
    x_lower = faces_x[:-1, 1:-1]
    x_upper = faces_x[1:, 1:-1]
    y_lower = faces_y[1:-1, :-1]
    y_upper = faces_y[1:-1, 1:]
    z_lower = jnp.concatenate([zero_plane, faces_z], axis=2)
    z_upper = jnp.concatenate([faces_z, 2.0 * centre[:, :, -1:]], axis=2)
    diagonal = x_lower + x_upper + y_lower + y_upper + z_lower + z_upper
    diagonal = jnp.where(diagonal > 0, diagonal, 1.0)
    return (x_lower, x_upper, y_lower, y_upper, z_lower, z_upper, diagonal)


def shrink(coeffs):
    return tuple((item[1:-1, 1:-1] for item in coeffs))


def parity_of(extent, start_x, start_y):
    index_x = lax.broadcasted_iota(jnp.int32, extent, 0) + start_x
    index_y = lax.broadcasted_iota(jnp.int32, extent, 1) + start_y
    index_z = lax.broadcasted_iota(jnp.int32, extent, 2)
    return (index_x + index_y + index_z) % 2


def neighbours(padded, coeffs):
    centre = padded[1:-1, 1:-1]
    zero_plane = jnp.zeros_like(centre[:, :, :1])
    lower_z = jnp.concatenate([zero_plane, centre[:, :, :-1]], axis=2)
    upper_z = jnp.concatenate([centre[:, :, 1:], zero_plane], axis=2)
    beside_all = coeffs[0] * padded[:-2, 1:-1] + coeffs[1] * padded[2:, 1:-1]
    beside_all = beside_all + coeffs[2] * padded[1:-1, :-2] + coeffs[3] * padded[1:-1, 2:]
    beside_all = beside_all + coeffs[4] * lower_z + coeffs[5] * upper_z
    return (beside_all, centre)


def colour_pass(padded, source, coeffs, parity, colour):
    beside_all, centre = neighbours(padded, coeffs)
    updated = (source + beside_all) / coeffs[6]
    return jnp.where(parity == colour, updated, centre)


def residual_of(padded, source, coeffs):
    beside_all, centre = neighbours(padded, coeffs)
    return source - (coeffs[6] * centre - beside_all)


def restrict_sum(field):
    size_x, size_y, size_z = field.shape
    return 0.5 * field.reshape(size_x // 2, 2, size_y // 2, 2, size_z // 2, 2).sum(axis=(1, 3, 5))


def restrict_mean(field):
    size_x, size_y, size_z = field.shape
    return 0.125 * field.reshape(size_x // 2, 2, size_y // 2, 2, size_z // 2, 2).sum(axis=(1, 3, 5))


def inject(field):
    return jnp.repeat(jnp.repeat(jnp.repeat(field, 2, axis=0), 2, axis=1), 2, axis=2)


def rim_one(field):
    return with_halo(field, (("gx", 0), ("yz", 1)), 1)


def rim_two(field):
    return with_halo(field, (("gx", 0), ("yz", 1)), 2)


def offsets(field):
    return (lax.axis_index("gx") * field.shape[0], lax.axis_index("yz") * field.shape[1])


def prepare_plain(mobility):
    start_x, start_y = offsets(mobility)
    return (coefficients(rim_one(mobility)), parity_of(mobility.shape, start_x, start_y))


def prepare(mobility):
    start_x, start_y = offsets(mobility)
    size_x, size_y, size_z = mobility.shape
    region = coefficients(rim_two(mobility))
    loop_parity = parity_of((size_x + 2, size_y + 2, size_z), start_x - 1, start_y - 1)
    operator_set = (
        shrink(region),
        parity_of(mobility.shape, start_x, start_y),
        region,
        loop_parity,
    )
    return operator_set


def smooth_plain(field, source, operator_set, sweeps, rim):
    coeffs = operator_set[0]
    parity = operator_set[1]
    for _ in range(sweeps):
        field = colour_pass(rim(field), source, coeffs, parity, 0)
        field = colour_pass(rim(field), source, coeffs, parity, 1)
    return field


def smooth(field, source, operator_set, sweeps):
    interior, parity, region, loop_parity = operator_set
    source_loop = rim_one(source)
    for _ in range(sweeps):
        loop_field = colour_pass(rim_two(field), source_loop, region, loop_parity, 0)
        field = colour_pass(loop_field, source, interior, parity, 1)
    return field


def local(right_side, phase, pressure_guess):
    mobility = 1.0 + 999.0 * phase.astype(jnp.float32)
    level_zero = prepare(mobility)
    pressure = smooth(pressure_guess, right_side, level_zero, SWEEPS)
    fine_res = residual_of(rim_one(pressure), right_side, level_zero[0])
    source_one = restrict_sum(fine_res)
    mobility_one = restrict_mean(mobility)
    level_one = prepare(mobility_one)
    coarse_one = smooth(jnp.zeros_like(source_one), source_one, level_one, SWEEPS)
    res_one = residual_of(rim_one(coarse_one), source_one, level_one[0])
    source_two = restrict_sum(res_one)
    mobility_two = restrict_mean(mobility_one)
    level_two = prepare_plain(mobility_two)
    coarse_two = smooth_plain(
        jnp.zeros_like(source_two), source_two, level_two, BOTTOM_SWEEPS, rim_one
    )
    coarse_one = smooth(coarse_one + inject(coarse_two), source_one, level_one, SWEEPS)
    pressure = smooth(pressure + inject(coarse_one), right_side, level_zero, SWEEPS)
    residual = residual_of(rim_one(pressure), right_side, level_zero[0])
    return (pressure, residual)


ROWS = 8
WIN = 3 * ROWS
REACH = 3
MIX = 2.0 / 1001.0


def place_of(rows, columns):
    slab = []
    for g in range(rows):
        a = (g // 2) * 2 + ((g % 2) ^ ((g // 2) % 2))
        slab += [a * columns + (j if a % 2 == 0 else columns - 1 - j) for j in range(columns)]
    return slab


def slab_index(columns):
    g, j = lax.axis_index("gx"), lax.axis_index("yz")
    a = (g // 2) * 2 + (g + g // 2) % 2
    return a * columns + jnp.where(a % 2 == 0, j, columns - 1 - j)


def device_of(slab, columns):
    a, b = slab // columns, slab % columns
    g = (a // 2) * 2 + (a + a // 2) % 2
    return g * columns + jnp.where(a % 2 == 0, b, columns - 1 - b)


def lanes(shape):
    return lax.broadcasted_iota(jnp.int32, shape, len(shape) - 1)


def swap_lanes(v, step):
    width = v.shape[-1]
    up, down = pltpu.roll(v, step, 1), pltpu.roll(v, width - step, 1)
    return jnp.where((lanes(v.shape) // step) % 2 == 0, down, up)


def swap_blocks(tiles):
    block = lanes(tiles[0].shape) // 32
    at = [block == b for b in range(3)]

    def choose(four):
        return jnp.where(at[0], four[0], jnp.where(at[1], four[1], jnp.where(at[2], four[2], four[3])))

    turned = [choose([tiles[(b + d) % 4] for b in range(4)]) for d in range(4)]
    turned = [turned[0]] + [pltpu.roll(turned[d], 32 * d, 1) for d in (1, 2, 3)]
    return [choose([turned[(b - a) % 4] for b in range(4)]) for a in range(4)]


def brick_parity(shape):
    lane = lanes(shape)
    return (lane // 32 + lane) % 2


def pack_kernel(order, source_hbm, phase_hbm, guess_hbm, out_ref, source_ref, phase_ref, guess_ref, turned, arrived):
    copies = [
        pltpu.make_async_copy(hbm, ref, arrived.at[a])
        for a, (hbm, ref) in enumerate(((source_hbm, source_ref), (phase_hbm, phase_ref), (guess_hbm, guess_ref)))
    ]
    for copy in copies:
        copy.start()
    for a, ref in enumerate((source_ref, phase_ref, guess_ref)):
        copies[a].wait()
        brick = ref[...].reshape(128, ref.shape[2])
        if a == 1:
            brick = 1.0 + 999.0 * brick.astype(jnp.float32)
        turned[a] = brick.T
    even = brick_parity((ROWS, 128)) == 0
    for device, slab in enumerate(order):
        base = 2 * ROWS * slab
        for a, row in ((1, 0), (2, ROWS), (0, 3 * ROWS)):
            low = turned[a, pl.ds(base, ROWS, stride=2), :]
            high = turned[a, pl.ds(base + 1, ROWS, stride=2), :]
            if a != 2:
                out_ref[device, row : row + ROWS, :] = jnp.where(even, low, high)
            out_ref[device, row + ROWS : row + 2 * ROWS, :] = jnp.where(even, high, low)


def unpack_kernel(order, in_ref, pressure_ref, residual_ref, turned):
    even = brick_parity((ROWS, 128)) == 0
    for device, slab in enumerate(order):
        base = 2 * ROWS * slab
        p0, p1 = in_ref[device, 0:ROWS, :], in_ref[device, ROWS : 2 * ROWS, :]
        r0 = in_ref[device, 2 * ROWS : 3 * ROWS, :]
        turned[0, pl.ds(base, ROWS, stride=2), :] = jnp.where(even, p0, p1)
        turned[0, pl.ds(base + 1, ROWS, stride=2), :] = jnp.where(even, p1, p0)
        turned[1, pl.ds(base, ROWS, stride=2), :] = jnp.where(even, r0, 0.0)
        turned[1, pl.ds(base + 1, ROWS, stride=2), :] = jnp.where(even, 0.0, r0)
    for a, ref in enumerate((pressure_ref, residual_ref)):
        ref[...] = turned[a].T.reshape(ref.shape)


FACE_ROWS = (1, WIN - 1)
INNER = (ROWS // 2, WIN - ROWS // 2)
OWN = (ROWS, 2 * ROWS)


def wider(rows, by):
    return (rows[0] - by, rows[1] + by)


def at(ref, rows, by=0):
    start = (WIN - ref.shape[-2]) // 2
    return slice(rows[0] - start + by, rows[1] - start + by)


def beyond(ref, i, low, rows, *lead):
    return jnp.where(low, ref[(*lead, i, at(ref, rows, -1))], ref[(*lead, i, at(ref, rows, 1))])


def add_up(terms):
    while len(terms) > 1:
        terms = [sum(terms[k : k + 2]) for k in range(0, len(terms), 2)]
    return terms[0]


def around_coarsest(planes, k, low):
    centre = planes[k + 1]
    rows, width = centre.shape
    return (
        pltpu.roll(centre, 1, 0),
        pltpu.roll(centre, rows - 1, 0),
        pltpu.roll(centre, 4, 1),
        pltpu.roll(centre, width - 4, 1),
        centre,
        jnp.where(low, planes[k], planes[k + 2]),
    )


def walls(sides, first, last):
    return sides[:2] + (jnp.where(first, 0.0, sides[2]), jnp.where(last, 0.0, sides[3])) + sides[4:]


def mean_fine(u, w):
    return jnp.where(u == w, u, (u * MIX) * w)


def mean_any(u, w):
    total = u + w
    return 2.0 * u * w / jnp.where(total > 0, total, 1.0)


def weights(mean, u, sides, top):
    faces = [mean(u, w) for w in sides]
    diagonal = (faces[0] + faces[1]) + (faces[2] + faces[3]) + (faces[4] + faces[5])
    diagonal = diagonal + jnp.where(top, 2.0 * u, 0.0)
    diagonal = jnp.where(diagonal > 0, diagonal, 1.0)
    inverse = 1.0 / diagonal
    return [face * inverse for face in faces], inverse, diagonal


def relax(scaled, share, sides):
    parts = [share[a] * sides[a] for a in range(6)]
    return scaled + ((parts[0] + parts[1]) + (parts[2] + parts[3]) + (parts[4] + parts[5]))


def fine_low(x, colour, width, rows):
    return (lanes((rows[1] - rows[0], width)) + (x + colour) % 2) % 2 == 0


def coarse_low(colour, width, rows):
    shape = (rows[1] - rows[0], width)
    row = lax.broadcasted_iota(jnp.int32, shape, 0) + rows[0]
    return (row + lanes(shape) // 2 + colour) % 2 == 0


def loader(v, rows):
    seen = {}

    def load(x):
        if x not in seen:
            seen[x] = v[x, at(v, rows), :]
        return seen[x]

    return load


def fine_sides(v, load, x, low, rows):
    centre = load(x)
    width = centre.shape[1]
    return (
        load(x - 1) if x > 0 else None,
        load(x + 1) if x + 1 < v.shape[0] else None,
        pltpu.roll(centre, 1, 1),
        pltpu.roll(centre, width - 1, 1),
        centre,
        beyond(v, x, low, rows),
    )


def fine_flow(colour, face, v, x, rows, load=None):
    planes, width = face.shape[1], face.shape[3]
    part = at(face, rows)
    low = fine_low(x, colour, width, rows)
    if v is not None and load is None:
        load = loader(v, rows)
    if colour == 0:
        sides = fine_sides(v, load, x, low, rows)
        return add_up([face[a, x, part, :] * side for a, side in enumerate(sides) if side is not None])

    def carried(a, plane):
        values = face[a, plane, part, :]
        return values if v is None else values * load(plane)

    away = beyond(face, x, low, rows, 5)
    terms = [
        pltpu.roll(carried(3, x), 1, 1),
        pltpu.roll(carried(2, x), width - 1, 1),
        carried(4, x),
        away if v is None else away * beyond(v, x, low, rows),
    ]
    if x > 0:
        terms.append(carried(1, x - 1))
    if x + 1 < planes:
        terms.append(carried(0, x + 1))
    return add_up(terms)


def coarse_sides(v, i, low, rows):
    here = at(v, rows)
    centre = v[i, here, :]
    width = centre.shape[1]
    below = v[i - 1, here, :] if i > 0 else jnp.zeros_like(centre)
    above = v[i + 1, here, :] if i + 1 < v.shape[0] else jnp.zeros_like(centre)
    return (
        v[i, at(v, rows, -1), :],
        v[i, at(v, rows, 1), :],
        pltpu.roll(centre, 2, 1),
        pltpu.roll(centre, width - 2, 1),
        centre,
        jnp.where(low, below, above),
    )


def coarse_flow(colour, face, v, i, rows, load=None):
    planes, width = face.shape[1], face.shape[3]
    low = coarse_low(colour, width, rows)
    if colour == 0:
        sides = coarse_sides(v, i, low, rows)
        return add_up([face[a, i, at(face, rows), :] * side for a, side in enumerate(sides)])

    def carried(a, plane, by=0):
        values = face[a, plane, at(face, rows, by), :]
        return values if v is None else values * v[plane, at(v, rows, by), :]

    centre = carried(4, i)
    below = carried(5, i - 1) if i > 0 else jnp.zeros_like(centre)
    above = carried(5, i + 1) if i + 1 < planes else jnp.zeros_like(centre)
    return add_up(
        [
            carried(1, i, -1),
            carried(0, i, 1),
            pltpu.roll(carried(3, i), 2, 1),
            pltpu.roll(carried(2, i), width - 2, 1),
            centre,
            jnp.where(low, below, above),
        ]
    )


def renew(flow, colour, target, other, face, inverse, scaled, rows):
    load = loader(other, rows)
    for x in range(face.shape[1]):
        moved = inverse[x, at(inverse, rows), :] * flow(colour, face, other, x, rows, load)
        target[x, at(target, rows), :] = scaled[x, at(scaled, rows), :] + moved


def rest_of(flow, v0, v1, face, inverse0, scaled0, x, rows):
    factor = inverse0[x, at(inverse0, rows), :]
    updated = scaled0[x, at(scaled0, rows), :] + factor * flow(0, face, v1, x, rows)
    return (updated - v0[x, at(v0, rows), :]) / factor


def one_over(diagonal):
    return 1.0 / jnp.where(diagonal > 0, diagonal, 1.0)


def fine_faces(m0, m1, face, inverse0, inverse1):
    planes, width = face.shape[1], face.shape[3]
    rows = FACE_ROWS
    here = at(face, rows)
    lane = lanes((rows[1] - rows[0], width))
    load = loader(m1, rows)
    for x in range(planes):
        low = fine_low(x, 0, width, rows)
        u = m0[x, here, :]
        sides = walls(fine_sides(m1, load, x, low, rows), lane == 0, lane == width - 1)
        terms = []
        for a, side in enumerate(sides):
            value = jnp.zeros_like(u) if side is None else mean_fine(u, side)
            face[a, x, here, :] = value
            terms.append(value)
        top = jnp.logical_and(jnp.logical_not(low), sides[5] == 0)
        inverse0[x, here, :] = one_over(add_up(terms) + jnp.where(top, 2.0 * u, 0.0))
    rows = wider(rows, -1)
    for x in range(planes):
        low = fine_low(x, 1, width, rows)
        top = jnp.logical_and(jnp.logical_not(low), m0[x, at(m0, rows, 1), :] == 0)
        total = fine_flow(1, face, None, x, rows) + jnp.where(top, 2.0 * m1[x, at(m1, rows), :], 0.0)
        inverse1[x, at(inverse1, rows), :] = one_over(total)


def coarse_faces(m0, m1, face, inverse0, inverse1):
    planes, width = face.shape[1], face.shape[3]
    rows = FACE_ROWS
    here = at(face, rows)
    lane = lanes((rows[1] - rows[0], width))
    for i in range(planes):
        u = m0[i, here, :]
        sides = walls(coarse_sides(m1, i, coarse_low(0, width, rows), rows), lane < 2, lane >= width - 2)
        terms = []
        for a, side in enumerate(sides):
            value = mean_any(u, side)
            face[a, i, here, :] = value
            terms.append(value)
        inverse0[i, here, :] = one_over(add_up(terms) + jnp.where(sides[1] == 0, 2.0 * u, 0.0))
    rows = wider(rows, -1)
    for i in range(planes):
        top = jnp.where(m0[i, at(m0, rows, 1), :] == 0, 2.0 * m1[i, at(m1, rows), :], 0.0)
        inverse1[i, at(inverse1, rows), :] = one_over(coarse_flow(1, face, None, i, rows) + top)


def neighbour_rows(columns):
    near = jnp.where(slab_index(columns) % 2 == 0, 2 * ROWS, 0)
    return pl.multiple_of(near, ROWS), pl.multiple_of(2 * ROWS - near, ROWS)


def unfold_slabs(places, arrays, planes):
    def unfold(i, _):
        for ref, start, at in places:
            for first, store in arrays:
                tiles = [ref[4 * i + j, start + first : start + first + ROWS, :] for j in range(4)]
                for j, tile in enumerate(swap_blocks(tiles)):
                    store(4 * i + j, at, tile)
        return 0

    lax.fori_loop(0, planes // 4, unfold, 0, unroll=True)


def plain_store(ref):
    def store(x, row, tile):
        ref[x, pl.ds(row, ROWS), :] = tile

    return store


def scaled_store(ref, factor):
    def store(x, row, tile):
        part = pl.ds(row, ROWS)
        ref[x, part, :] = tile * factor[x, part, :]

    return store


def pair_sum(ref):
    return ref[ROWS : 2 * ROWS, :] + ref[ROWS + 1 : 2 * ROWS + 1, :]


def picked(width):
    row = lax.broadcasted_iota(jnp.int32, (ROWS, width), 0)
    return jnp.logical_and(row % 2 == 0, lanes((ROWS, width)) % 4 == row // 2)


def weights_kernel(
    columns,
    own, near, far,
    face, inverse0, inverse1, cface, cinverse0, cinverse1, coarsest, flow0,
    m0, m1, guess, cm0, cm1, rest,
):
    planes, width = face.shape[1], face.shape[3]
    near_at, far_at = neighbour_rows(columns)
    places = ((own, 0, ROWS), (near, 0, near_at), (far, 0, far_at))
    arrays = ((0, plain_store(m0)), (ROWS, plain_store(m1)), (2 * ROWS, plain_store(guess)))
    unfold_slabs(places, arrays, planes)
    fine_faces(m0, m1, face, inverse0, inverse1)
    flow0[...] = jnp.zeros(flow0.shape, jnp.float32)
    load = loader(guess, FACE_ROWS)
    for x in range(planes):
        flow0[x, slice(*FACE_ROWS), :] = fine_flow(0, face, guess, x, FACE_ROWS, load)
    even = coarse_low(0, width, (0, WIN))
    for i in range(planes // 4):
        mobilities = []
        for x in (4 * i, 4 * i + 2):
            mass = (m0[x] + m1[x]) + (m0[x + 1] + m1[x + 1])
            mobilities.append(0.125 * (mass + swap_lanes(mass, 1)))
        cm0[i] = jnp.where(even, mobilities[0], mobilities[1])
        cm1[i] = jnp.where(even, mobilities[1], mobilities[0])
    coarse_faces(cm0, cm1, cface, cinverse0, cinverse1)
    pick = picked(width)
    for i in range(planes // 4):
        rest[...] = cm0[i] + cm1[i]
        pair = pair_sum(rest)
        pair = 0.125 * (pair + swap_lanes(pair, 2))
        coarsest[i : i + 1, :] = jnp.sum(jnp.where(pick, pair, 0.0), axis=0, keepdims=True)


def down_kernel(
    columns,
    face, inverse0, inverse1, cface, cinverse0, cinverse1, coarsest, flow0,
    own, near, far,
    *refs,
):
    state, cstate, late, message_hbm, packed_hbm = refs[:5]
    scaled0, scaled1, cscaled0, cscaled1, v0, v1, e0, e1, rest, message, packed, done = refs[5:]
    planes, width = face.shape[1], face.shape[3]
    coarse = planes // 4
    middle = slice(*INNER)
    held = [(face.at[:, :, middle, :], state.at[0:6])]
    held += [
        (inverse0.at[:, middle, :], state.at[6]),
        (inverse1.at[:, middle, :], late.at[0]),
        (scaled1.at[:, middle, :], late.at[1]),
        (v1.at[:, middle, :], late.at[2]),
    ]
    held += [(message, message_hbm)]
    copies = [pltpu.make_async_copy(ref, out, done.at[k]) for k, (ref, out) in enumerate(held)]
    for copy in copies[:3]:
        copy.start()
    near_at, far_at = neighbour_rows(columns)
    places = ((own, 0, ROWS), (near, 3 * ROWS, near_at), (far, 0, far_at))

    def first_pass(x, row, tile):
        part = pl.ds(row, ROWS)
        factor = inverse0[x, part, :]
        scaled = tile * factor
        scaled0[x, part, :] = scaled
        v0[x, part, :] = scaled + flow0[x, part, :] * factor

    arrays = ((0, first_pass), (ROWS, scaled_store(scaled1, inverse1)))
    unfold_slabs(places, arrays, planes)
    copies[3].start()
    for x in range(planes):
        state[7, x] = scaled0[x, middle, :]

    renew(fine_flow, 1, v1, v0, face, inverse1, scaled1, (2, WIN - 2))
    renew(fine_flow, 0, v0, v1, face, inverse0, scaled0, (3, WIN - 3))
    renew(fine_flow, 1, v1, v0, face, inverse1, scaled1, (3, WIN - 3))
    copies[4].start()

    even = coarse_low(0, width, INNER)
    for i in range(coarse):
        fields = []
        for x in (4 * i, 4 * i + 2):
            total = rest_of(fine_flow, v0, v1, face, inverse0, scaled0, x, INNER)
            total = total + rest_of(fine_flow, v0, v1, face, inverse0, scaled0, x + 1, INNER)
            fields.append(0.5 * (total + swap_lanes(total, 1)))
        first = jnp.where(even, fields[0], fields[1]) * cinverse0[i, middle, :]
        cscaled0[i, middle, :] = first
        e0[i, middle, :] = first
        cscaled1[i, middle, :] = jnp.where(even, fields[1], fields[0]) * cinverse1[i, middle, :]

    renew(coarse_flow, 1, e1, e0, cface, cinverse1, cscaled1, wider(INNER, -1))
    renew(coarse_flow, 0, e0, e1, cface, cinverse0, cscaled0, wider(INNER, -2))
    renew(coarse_flow, 1, e1, e0, cface, cinverse1, cscaled1, wider(OWN, 1))

    pick = picked(width)
    for i in range(coarse):
        rest[slice(*OWN), :] = rest_of(coarse_flow, e0, e1, cface, cinverse0, cscaled0, i, OWN)
        pair = pair_sum(rest)
        pair = 0.5 * (pair + swap_lanes(pair, 2))
        packed[0, i : i + 1, :] = jnp.sum(jnp.where(pick, pair, 0.0), axis=0, keepdims=True)
    packed[0, coarse : 2 * coarse, :] = coarsest[...]
    tile = packed[0]
    for device in range(1, packed.shape[0]):
        packed[device] = tile
    sent = pltpu.make_async_copy(packed, packed_hbm, done.at[13])
    sent.start()

    first = lanes((ROWS, width)) % 2 == 0
    here = slice(*OWN)
    for i in range(coarse):
        message[i, 0:ROWS, :] = jnp.where(first, e1[i, here, :], cscaled0[i, here, :])
        message[i, ROWS : 2 * ROWS, :] = cscaled1[i, here, :]
    copies[5].start()
    for i in range(coarse):
        for a in range(6):
            cstate[a, i] = cface[a, i]
        cstate[6, i] = cinverse0[i]
        cstate[7, i] = cinverse1[i]
        cstate[8, i] = cscaled0[i]
        cstate[9, i] = cscaled1[i]
        cstate[10, i] = e1[i]
    for copy in copies:
        copy.wait()
    sent.wait()


def up_kernel(
    columns,
    gathered, state, cstate, near_hbm, far_hbm, late_hbm,
    out,
    late, cscaled0, cscaled1, e1, v0, v1, e0, near, far, bshare, coarsest, spread, done,
):
    planes, width = state.shape[1], state.shape[3]
    count = gathered.shape[0]
    rows = planes // 4
    face, inverse0, scaled0 = state, state.at[6], state.at[7]
    inverse1, scaled1, field1 = [late.at[k] for k in range(3)]
    cface, (cinverse0, cinverse1, kept0, kept1, field) = cstate, [cstate.at[k] for k in range(6, 11)]
    held = ((near_hbm, near), (far_hbm, far), (late_hbm, late))
    copies = [pltpu.make_async_copy(hbm, ref, done.at[k]) for k, (hbm, ref) in enumerate(held)]
    for copy in copies:
        copy.start()

    slab = slab_index(columns)
    lane = lanes((rows, width))
    part = lane % 4
    sources, mobilities = [], []
    for w in range(-REACH, REACH + 1):
        other = slab + w
        inside = jnp.logical_and(other >= 0, other < count)
        device = device_of(jnp.clip(other, 0, count - 1), columns)
        keep = jnp.where(inside, 1.0, 0.0)
        for part_of, into in ((slice(0, rows), sources), (slice(rows, 2 * rows), mobilities)):
            tile = gathered[device, part_of, :] * keep
            for z in range(4):
                v = jnp.where(part == z, tile, 0.0)
                v = v + swap_lanes(v, 1)
                into.append(v + swap_lanes(v, 2))

    parity = (lax.broadcasted_iota(jnp.int32, (rows, width), 0) + lane // 4) % 2
    pairs = len(sources) // 2
    zero = jnp.zeros((rows, width), jnp.float32)
    low = (parity == 0, parity == 1)

    def coloured(planes_of):
        first = [jnp.where(low[0], planes_of[2 * k], planes_of[2 * k + 1]) for k in range(pairs)]
        second = [jnp.where(low[0], planes_of[2 * k + 1], planes_of[2 * k]) for k in range(pairs)]
        return [zero] + first + [zero], [zero] + second + [zero]

    source, mobility = coloured(sources), coloured(mobilities)
    row = lax.broadcasted_iota(jnp.int32, (rows, width), 0)
    scaled = ([], [])
    for k in range(pairs):
        for colour in (0, 1):
            sides = around_coarsest(mobility[1 - colour], k, low[colour])
            sides = (jnp.where(row == 0, 0.0, sides[0]), jnp.where(row == rows - 1, 0.0, sides[1])) + sides[2:]
            sides = walls(sides, lane < 4, lane >= width - 4)
            top = jnp.logical_and(jnp.logical_not(low[colour]), sides[5] == 0)
            shares, inverse, _ = weights(mean_any, mobility[colour][k + 1], sides, top)
            for a in range(6):
                bshare[colour, a, k] = shares[a]
            scaled[colour].append(source[colour][k + 1] * inverse)

    fields = [[zero] + scaled[0] + [zero], [zero] * (pairs + 2)]
    for step in range(1, 2 * BOTTOM_SWEEPS):
        colour, skip = step % 2, (step + 1) // 2
        new = list(fields[colour])
        for k in range(skip, pairs - skip):
            sides = around_coarsest(fields[1 - colour], k, low[colour])
            new[k + 1] = relax(scaled[colour][k], [bshare[colour, a, k] for a in range(6)], sides)
        fields[colour] = new

    start = 4 * REACH - ROWS // 2
    for k in range(WIN // 4):
        a, b = fields[0][start // 2 + k + 1], fields[1][start // 2 + k + 1]
        coarsest[2 * k * rows : (2 * k + 1) * rows, :] = jnp.where(low[0], a, b)
        coarsest[(2 * k + 1) * rows : (2 * k + 2) * rows, :] = jnp.where(low[0], b, a)

    for copy in copies[:2]:
        copy.wait()
    near_at, far_at = neighbour_rows(columns)
    here = slice(*OWN)
    first = lanes((ROWS, width)) % 2 == 0
    for i in range(rows):
        half = coarsest[pl.ds(i, WIN // 2, stride=rows), :]
        spread[pl.ds(0, WIN // 2, stride=2), :] = half
        spread[pl.ds(1, WIN // 2, stride=2), :] = half
        e1[i, here, :] = field[i, here, :] + spread[here, :]
        cscaled0[i, here, :] = kept0[i, here, :]
        cscaled1[i, here, :] = kept1[i, here, :]
        for row, ref in ((near_at, near), (far_at, far)):
            mixed = ref[i, 0:ROWS, :]
            other = swap_lanes(mixed, 1)
            part = pl.ds(row, ROWS)
            e1[i, part, :] = jnp.where(first, mixed, other) + spread[part, :]
            cscaled0[i, part, :] = jnp.where(first, other, mixed)
            cscaled1[i, part, :] = ref[i, ROWS : 2 * ROWS, :]

    renew(coarse_flow, 0, e0, e1, cface, cinverse0, cscaled0, (1, WIN - 1))
    renew(coarse_flow, 1, e1, e0, cface, cinverse1, cscaled1, (2, WIN - 2))
    renew(coarse_flow, 0, e0, e1, cface, cinverse0, cscaled0, (3, WIN - 3))
    renew(coarse_flow, 1, e1, e0, cface, cinverse1, cscaled1, INNER)

    copies[2].wait()
    even = coarse_low(0, width, INNER)
    for i in range(rows):
        a, b = e0[i, at(e0, INNER), :], e1[i, at(e1, INNER), :]
        for half, add in ((0, jnp.where(even, a, b)), (1, jnp.where(even, b, a))):
            for x in (4 * i + 2 * half, 4 * i + 2 * half + 1):
                v1[x] = field1[x] + add

    renew(fine_flow, 0, v0, v1, face, inverse0, scaled0, wider(INNER, -1))
    renew(fine_flow, 1, v1, v0, face, inverse1, scaled1, wider(INNER, -2))
    renew(fine_flow, 0, v0, v1, face, inverse0, scaled0, wider(OWN, 1))
    renew(fine_flow, 1, v1, v0, face, inverse1, scaled1, wider(OWN, 1))

    for i in range(rows):
        planes_of = range(4 * i, 4 * i + 4)
        rest = [rest_of(fine_flow, v0, v1, face, inverse0, scaled0, x, OWN) for x in planes_of]
        for a, tiles in (
            (0, [v0[x, at(v0, OWN), :] for x in planes_of]),
            (1, [v1[x, at(v1, OWN), :] for x in planes_of]),
            (2, rest),
        ):
            for j, tile in enumerate(swap_blocks(tiles)):
                out[4 * i + j, a * ROWS : (a + 1) * ROWS, :] = tile


def local_slabs(shape, right_side, phase, pressure_guess):
    across, columns = shape
    count = across * columns
    bx, by, length = right_side.shape
    planes, width = across * bx, columns * by
    f32 = jnp.float32
    order = place_of(across, columns)
    path = sorted(range(count), key=lambda device: order[device])
    near = [pair for k in range(0, count, 2) for pair in ((path[k], path[k + 1]), (path[k + 1], path[k]))]
    far = [pair for k in range(1, count - 1, 2) for pair in ((path[k], path[k + 1]), (path[k + 1], path[k]))]
    axes = ("gx", "yz")
    cost = pl.CostEstimate(flops=20_000_000_000, bytes_accessed=100_000_000, transcendentals=0)
    params = pltpu.CompilerParams(vmem_limit_bytes=20 * 1024 * 1024)

    def struct(*dims):
        return jax.ShapeDtypeStruct(dims, f32)

    def vmem(*dims):
        return pltpu.VMEM(dims, f32)

    bricks = pl.pallas_call(
        functools.partial(pack_kernel, order),
        in_specs=[pl.BlockSpec(memory_space=pltpu.HBM)] * 3,
        out_shape=struct(count, 5 * ROWS, 128),
        scratch_shapes=[
            vmem(bx, by, length),
            pltpu.VMEM((bx, by, length), phase.dtype),
            vmem(bx, by, length),
            vmem(3, length, 128),
            pltpu.SemaphoreType.DMA((3,)),
        ],
        compiler_params=params,
        name="pack",
    )(*(pltpu.with_memory_space_constraint(x, pltpu.HBM) for x in (right_side, phase, pressure_guess)))
    own = lax.all_to_all(bricks, axes, 0, 0)
    first_part, second_part = own[:, : 3 * ROWS], own[:, 3 * ROWS :]
    first_far = lax.ppermute(first_part, axes, far)
    own_near = lax.ppermute(own, axes, near)
    second_far = lax.ppermute(second_part, axes, far)

    coarse = planes // 4
    face, plane = (6, planes, WIN, width), (planes, WIN, width)
    cface, cplane = (6, coarse, WIN, width), (coarse, WIN, width)
    height = INNER[1] - INNER[0]
    iplane = (planes, height, width)
    letter = (coarse, 2 * ROWS, width)

    def in_hbm(*arrays):
        return [pltpu.with_memory_space_constraint(x, pltpu.HBM) for x in arrays]

    def far_outs(*shapes):
        return [pltpu.HBM(dims, f32) for dims in shapes], [pl.BlockSpec(memory_space=pltpu.HBM)] * len(shapes)

    def near_outs(*shapes):
        return [struct(*dims) for dims in shapes], [pl.BlockSpec(memory_space=pltpu.VMEM)] * len(shapes)

    made = pl.pallas_call(
        functools.partial(weights_kernel, columns),
        out_shape=near_outs(face, plane, plane, cface, cplane, cplane, (coarse, width), plane)[0],
        scratch_shapes=[vmem(*plane)] * 3 + [vmem(*cplane)] * 2 + [vmem(WIN, width)],
        compiler_params=params,
        cost_estimate=cost,
        name="weights",
    )(first_part, own_near, first_far)

    first = near_outs((8, planes, height, width), (11, coarse, WIN, width))
    second = far_outs((3, planes, height, width), letter, (count, 2 * coarse, width))
    state, cstate, late, message, packed = pl.pallas_call(
        functools.partial(down_kernel, columns),
        out_shape=first[0] + second[0],
        out_specs=first[1] + second[1],
        scratch_shapes=[vmem(*plane)] * 2 + [vmem(*cplane)] * 2 + [vmem(*plane)] * 2 + [vmem(*cplane)] * 2 + [
            vmem(WIN, width),
            vmem(*letter),
            vmem(count, 2 * coarse, width),
            pltpu.SemaphoreType.DMA((14,)),
        ],
        compiler_params=params,
        name="down",
    )(*made, second_part, own_near, second_far)
    gathered = lax.all_to_all(packed, axes, 0, 0)
    message_far = lax.ppermute(message, axes, far)
    message_near = lax.ppermute(message, axes, near)

    cycle = pl.pallas_call(
        functools.partial(up_kernel, columns),
        out_shape=struct(count, 3 * ROWS, 128),
        in_specs=[pl.BlockSpec(memory_space=pltpu.VMEM)] * 3 + [pl.BlockSpec(memory_space=pltpu.HBM)] * 3,
        scratch_shapes=[vmem(3, *iplane)] + [vmem(*cplane)] * 3 + [vmem(*iplane)] * 2 + [vmem(*cplane)] + [vmem(*letter)] * 2 + [
            vmem(2, 6, 2 * (2 * REACH + 1), coarse, width),
            vmem(WIN // 2 * coarse, width),
            vmem(WIN, width),
            pltpu.SemaphoreType.DMA((3,)),
        ],
        compiler_params=params,
        name="up",
    )(gathered, state, cstate, *in_hbm(message_near, message_far, late))
    back = lax.all_to_all(cycle, axes, 0, 0)
    return pl.pallas_call(
        functools.partial(unpack_kernel, order),
        out_shape=[struct(bx, by, length)] * 2,
        scratch_shapes=[vmem(2, length, 128)],
        compiler_params=params,
        name="unpack",
    )(back)


def solution(mesh):
    spec = P("gx", "yz", None)
    shape = (mesh.shape["gx"], mesh.shape["yz"])

    def cycle(right_side, phase, pressure_guess):
        bx, by, length = right_side.shape
        slabs = (bx, by, shape[1]) == (4, 32, 4) and length == 2 * ROWS * shape[0] * shape[1]
        if slabs and shape[0] == 8:
            return local_slabs(shape, right_side, phase, pressure_guess)
        return local(right_side, phase, pressure_guess)

    return jax.shard_map(cycle, mesh=mesh, in_specs=(spec,) * 3, out_specs=(spec,) * 2, check_vma=False)
```
